32 devices in a mesh: dp: 8 (over z, y), mp: 4 (over x, core).
Axes of the slice: x: 2, y: 2, z: 4, core: 2. Of those that a mesh axis runs over, the one named last changes fastest.
Arguments:
- latents: bfloat16 [16, 256, 1152], P('dp', None, 'mp'), may hold values from -6 to 6
- condition: bfloat16 [16, 1152], P('dp'), may hold values from -6 to 6
- noise_bins: int32 [16], P('dp'), may hold values from 0 to 7
- slot_valid: int32 [16], P('dp'), may hold values from 0 to 1, as said below
- ada_weight: bfloat16 [1152, 6, 1152], P('dp', None, 'mp'), may hold values from -0.1875 to 0.1875
- ada_bias: float32 [6, 1152], P(None, 'mp'), may hold values from -3 to 3
- qkv_weight: bfloat16 [1152, 3, 1152], P('dp', None, 'mp'), may hold values from -0.1875 to 0.1875
- query_gain: float32 [72], replicated, may hold values from 1 to 1.6
- key_gain: float32 [72], replicated, may hold values from 1 to 1.6
- out_weight: bfloat16 [1152, 1152], P('mp', 'dp'), may hold values from -0.75 to 0.75
- gate_up: bfloat16 [1152, 2, 3072], P('dp', None, 'mp'), may hold values from -0.1875 to 0.1875
- down_weight: bfloat16 [3072, 1152], P('mp', 'dp'), may hold values from -0.109375 to 0.109375
- cotangent: bfloat16 [16, 256, 1152], P('dp', None, 'mp'), may hold values from -6 to 6
Outputs:
- block_out: bfloat16 [16, 256, 1152], P('dp', None, 'mp')
- latent_grad: bfloat16 [16, 256, 1152], P('dp', None, 'mp')
- condition_grad: bfloat16 [16, 1152], P('dp')
- ada_grad: float32 [1152, 6, 1152], P('dp', None, 'mp')
- bias_grad: float32 [6, 1152], P(None, 'mp')
- qkv_grad: float32 [1152, 3, 1152], P('dp', None, 'mp')
- qnorm_grad: float32 [72], replicated
- knorm_grad: float32 [72], replicated
- out_grad: float32 [1152, 1152], P('mp', 'dp')
- gateup_grad: float32 [1152, 2, 3072], P('dp', None, 'mp')
- down_grad: float32 [3072, 1152], P('mp', 'dp')
The draws below stay inside these ranges and needn't reach their ends.
Inputs may be any that keep to these rules, and one draw needn't show every extreme that they name: `slot_valid`: exactly 8 slots in all hold images; at least one dp index has all its 2 slots valid.
All inputs are finite; a program needn't handle non-finite values.
Results may differ from the reference program's by a relative error of at most 0.015.
Values may be sent and summed in bfloat16 or wider, within the bound.
No kernel may reach another device: no remote copies, remote signals or barrier semaphores. Data moves between devices by JAX's collectives and lax.ppermute only.
A program may use at most 128 MiB of HBM per device.

```python
import math
import jax
import jax.numpy as jnp
import numpy as np
from jax import lax

D = 1152
HEADS = 16
HEAD = 72
FF = 3072
GRID = 16
BINS = 8
IMG_DEV = 2
P_SIZE = 256
IMAGES = 16


def draw_slot_valid(key, part):
    key = jax.random.fold_in(key, 11)
    tier_key, noise_key, favour_key = jax.random.split(key, 3)
    owners = IMAGES // IMG_DEV
    tiers = jax.random.randint(tier_key, (owners,), 0, 8)
    noise = jax.random.randint(noise_key, (IMAGES,), 0, 4096)
    favoured = jax.random.randint(favour_key, (), 0, owners)
    owner = jnp.arange(IMAGES, dtype=jnp.int32) // IMG_DEV
    boost = 1 + jnp.take(tiers * tiers, owner)
    score = noise * boost * IMAGES + jnp.arange(IMAGES, dtype=jnp.int32)
    score = score + jnp.where(owner == favoured, 2 ** 30, 0)
    chosen = lax.top_k(score, IMAGES // 2)[1]
    return jnp.zeros((IMAGES,), jnp.int32).at[chosen].set(1)


def set_ends(array, rng, smallest, top_value):
    extent = array.shape
    index_at = [jax.random.randint(jax.random.fold_in(rng, axis), (), 0, extent[axis]) for axis in range(len(extent))]
    array = array.at[tuple(index_at)].set(smallest)
    longest = extent.index(max(extent))
    index_at[longest] = (index_at[longest] + 1) % extent[longest]
    return array.at[tuple(index_at)].set(top_value)


def raised(array, rng, source, target, parts, factor):
    owner, partner = [(jnp.arange(array.shape[position]) // (array.shape[position] // parts)).reshape([-1 if axis == position else 1 for axis in range(array.ndim)]) for position in (source, target)]
    chosen = jax.random.permutation(rng, parts)[partner]
    strong = (owner == chosen) | (owner == (partner + parts // 2) % parts)
    return jnp.where(strong, factor * array, array)


def shard_levels(key, extent, pieces, smallest, high):
    def one(axis_at, shards_of):
        heights = jax.random.uniform(jax.random.fold_in(jax.random.fold_in(key, 6), axis_at), (shards_of,), jnp.float32, smallest / len(pieces), high / len(pieces))
        return jnp.repeat(jnp.exp(heights), extent[axis_at] // shards_of).reshape((-1,) + (1,) * (len(extent) - axis_at - 1))

    factor_of = one(*pieces[0])
    for cut in pieces[1:]:
        factor_of = factor_of * one(*cut)
    return factor_of


def rank_table(count, slope):
    portions = [(1 << 20) // math.isqrt(grade ** slope) + 1 for grade in range(1, count + 1)]
    spread = 1 + sum(portions) // (1 << 30)
    return np.cumsum(np.array([max(1, weight // spread) for weight in portions]))


def ranked(key, extent, number_of, skew):
    table = rank_table(number_of, skew)
    lot = jax.random.randint(jax.random.fold_in(key, 1), extent, 0, int(table[number_of - 1]))
    standing = jnp.searchsorted(jnp.asarray(table, jnp.int32), lot, side="right")
    return jax.random.permutation(jax.random.fold_in(key, 2), number_of)[standing].astype(jnp.int32)


def scatter_about(rng, shape, spread, reach, pieces=(), held_as=jnp.bfloat16):
    drawn = spread * jax.random.normal(rng, shape, jnp.float32)
    if pieces:
        drawn = drawn * shard_levels(rng, shape, pieces, -0.22, 0.18)
    return jnp.clip(drawn, -reach, reach).astype(held_as)


def heavy_noise(rng, dims, deviation, bound, pieces, heavy, held_as=jnp.bfloat16):
    drawn = deviation * jax.random.normal(rng, dims, jnp.float32)
    if pieces:
        drawn = drawn * shard_levels(rng, dims, pieces, -0.22, 0.18)
    return jnp.clip(raised(drawn, jax.random.fold_in(rng, 3), *heavy), -bound, bound).astype(held_as)


def setup_inputs(seed: int = 0) -> dict:
    arg_keys = jax.random.split(jax.random.key(seed), 14)
    latents = scatter_about(arg_keys[0], (IMAGES, P_SIZE, D), 1.0, 6.0, ((0, 8), (2, 4)))
    condition = scatter_about(arg_keys[1], (IMAGES, D), 1.0, 6.0, ((0, 8),))
    noise_bins = set_ends(ranked(arg_keys[2], (IMAGES,), BINS, 2), jax.random.fold_in(arg_keys[2], 3), 0, BINS - 1).astype(jnp.int32)
    slot_valid = draw_slot_valid(jax.random.fold_in(arg_keys[13], 71), 0)
    ada_weight = scatter_about(arg_keys[4], (D, 6, D), D ** -0.5, 0.1875, ((0, 8), (2, 4)))
    ada_bias = scatter_about(arg_keys[5], (6, D), 0.5, 3.0, ((1, 4),), jnp.float32)
    qkv_weight = scatter_about(arg_keys[6], (D, 3, D), D ** -0.5, 0.1875, ((0, 8), (2, 4)))
    query_gain = jnp.clip(jax.random.uniform(arg_keys[7], (HEAD,), jnp.float32, 1.0, 1.6), 1.0, 1.6)
    key_gain = jnp.clip(jax.random.uniform(arg_keys[8], (HEAD,), jnp.float32, 1.0, 1.6), 1.0, 1.6)
    out_weight = scatter_about(arg_keys[9], (D, D), (D * 16 // P_SIZE) ** -0.5, 0.75, ((0, 4), (1, 8)))
    gate_up = scatter_about(arg_keys[10], (D, 2, FF), D ** -0.5, 0.1875, ((0, 8), (2, 4)))
    down_weight = scatter_about(arg_keys[11], (FF, D), FF ** -0.5, 0.109375, ((0, 4), (1, 8)))
    cotangent = heavy_noise(arg_keys[12], (IMAGES, P_SIZE, D), 1.0, 6.0, ((0, 8), (2, 4)), (0, 2, 8, 2.0))
    return {"latents": latents, "condition": condition, "noise_bins": noise_bins, "slot_valid": slot_valid, "ada_weight": ada_weight, "ada_bias": ada_bias, "qkv_weight": qkv_weight, "query_gain": query_gain, "key_gain": key_gain, "out_weight": out_weight, "gate_up": gate_up, "down_weight": down_weight, "cotangent": cotangent}


@jax.custom_vjp
def low(v):
    return lax.optimization_barrier(v.astype(jnp.bfloat16)).astype(jnp.float32)

@jax.custom_vjp
def low_back(v):
    return v

def low_keep(v):
    return (low(v), None)

def low_pass(kept, grad):
    return (grad,)

def back_keep(v):
    return (v, None)

def back_low(kept, grad):
    return (low(grad),)
low.defvjp(low_keep, low_pass)
low_back.defvjp(back_keep, back_low)
eps = 1e-06
highest = lax.Precision.HIGHEST

def layer_norm(value):
    centred = value - lax.optimization_barrier(jnp.mean(value, axis=-1, keepdims=True))
    return centred * lax.rsqrt(lax.optimization_barrier(jnp.mean(centred * centred, axis=-1, keepdims=True)) + eps)

def rms_norm(value):
    return value * lax.rsqrt(lax.optimization_barrier(jnp.mean(value * value, axis=-1, keepdims=True)) + eps)

def rotary_tables():
    pairs = HEAD // 4
    freqs = 10000.0 ** (-jnp.arange(pairs, dtype=jnp.float32) / pairs)
    spots = jnp.arange(P_SIZE, dtype=jnp.int32)
    row_pos = (spots // GRID).astype(jnp.float32)
    col_pos = (spots % GRID).astype(jnp.float32)
    row_angle = row_pos[:, None] * freqs[None, :]
    col_angle = col_pos[:, None] * freqs[None, :]
    angles = jnp.concatenate([row_angle, row_angle, col_angle, col_angle], axis=1)
    return (jnp.cos(angles), jnp.sin(angles))

def mix_pairs(value):
    pairs = value.shape[-1] // 4
    first = value[..., :pairs]
    second = value[..., pairs:2 * pairs]
    third = value[..., 2 * pairs:3 * pairs]
    fourth = value[..., 3 * pairs:]
    return jnp.concatenate([-second, first, -fourth, third], axis=-1)

def rotate(value, cosine, sine):
    return value * cosine[:, None, :] + mix_pairs(value) * sine[:, None, :]

def forward(params, latent_in, cond_in):
    ada_weight, ada_bias, qkv_weight, query_gain, key_gain, out_weight, gate_up, down_weight = params
    images = latent_in.shape[0]
    cosine, sine = rotary_tables()
    inverse = 1.0 / math.sqrt(HEAD)
    cond_act = low(jax.nn.silu(cond_in))
    mods = low_back(jnp.einsum('nd,dce->nce', cond_act, ada_weight, precision=highest) + ada_bias[None])
    h_first = low(layer_norm(latent_in) * (1.0 + mods[:, 1, None]) + mods[:, 0, None])
    raw_qkv = low_back(jnp.einsum('npd,dce->npce', h_first, qkv_weight, precision=highest))
    raw_qkv = raw_qkv.reshape(images, P_SIZE, 3, HEADS, HEAD)
    queries = low(rotate(rms_norm(raw_qkv[:, :, 0]) * query_gain, cosine, sine))
    keys_rot = low(rotate(rms_norm(raw_qkv[:, :, 1]) * key_gain, cosine, sine))
    values = low(raw_qkv[:, :, 2])
    scores = low_back(jnp.einsum('nphe,nqhe->nhpq', queries, keys_rot, precision=highest) * inverse)
    expo = jnp.exp(scores - lax.optimization_barrier(jnp.max(scores, axis=-1, keepdims=True)))
    probs = expo / lax.optimization_barrier(jnp.sum(expo, axis=-1, keepdims=True))
    attended = jnp.einsum('nhpq,nqhe->nphe', low(probs), values, precision=highest)
    attended = low_back(low(attended)).reshape(images, P_SIZE, D)
    attn = low_back(jnp.einsum('npe,ed->npd', attended, out_weight, precision=highest))
    middle = latent_in + mods[:, 2, None] * attn
    h_second = low(layer_norm(middle) * (1.0 + mods[:, 4, None]) + mods[:, 3, None])
    gate_vals = low_back(jnp.einsum('npd,dcf->npcf', h_second, gate_up, precision=highest))
    hidden = low(jax.nn.silu(gate_vals[:, :, 0]) * gate_vals[:, :, 1])
    ffn = low_back(jnp.einsum('npf,fd->npd', hidden, down_weight, precision=highest))
    return middle + mods[:, 5, None] * ffn

def reference(latents, condition, noise_bins, slot_valid, ada_weight, ada_bias, qkv_weight, query_gain, key_gain, out_weight, gate_up, down_weight, cotangent):
    bin_ids = jnp.arange(BINS, dtype=jnp.int32)
    same_bin = (noise_bins[:, None] == bin_ids[None, :]).astype(jnp.int32)
    per_bin = lax.optimization_barrier(jnp.sum(same_bin * slot_valid[:, None], axis=0))
    total = jnp.sum(slot_valid)
    own_count = lax.optimization_barrier(jnp.sum(same_bin * per_bin[None, :], axis=1))
    img_weight = slot_valid.astype(jnp.float32) * total.astype(jnp.float32) / (BINS * jnp.maximum(own_count, 1).astype(jnp.float32))
    params = tuple((item.astype(jnp.float32) for item in (ada_weight, ada_bias, qkv_weight, query_gain, key_gain, out_weight, gate_up, down_weight)))
    group = math.gcd(IMAGES, 16)
    groups = IMAGES // group

    def step(carry, item):
        latent_g, cond_g, cot_g, weight_g = item
        out_g, pull = jax.vjp(forward, params, latent_g.astype(jnp.float32), cond_g.astype(jnp.float32))
        grad_params, grad_latent, grad_cond = pull(cot_g.astype(jnp.float32) * weight_g[:, None, None])
        carry = jax.tree.map(lambda left, right: left + right, carry, grad_params)
        return (carry, (out_g, grad_latent, grad_cond))
    init = jax.tree.map(jnp.zeros_like, params)
    sums, (outs, grad_latents, grad_conds) = lax.scan(step, init, (latents.reshape(groups, group, P_SIZE, D), condition.reshape(groups, group, D), cotangent.reshape(groups, group, P_SIZE, D), img_weight.reshape(groups, group)))
    block_out = (outs.reshape(IMAGES, P_SIZE, D) * slot_valid.astype(jnp.float32)[:, None, None]).astype(jnp.bfloat16)
    latent_grad = grad_latents.reshape(IMAGES, P_SIZE, D).astype(jnp.bfloat16)
    condition_grad = grad_conds.reshape(IMAGES, D).astype(jnp.bfloat16)
    return (block_out, latent_grad, condition_grad, sums[0], sums[1], sums[2], sums[3], sums[4], sums[5], sums[6], sums[7])
```

```python
import functools
import math

import jax
import jax.numpy as jnp
import numpy as np
from jax import lax
from jax.experimental import pallas as pl
from jax.experimental.pallas import tpu as pltpu
from jax.sharding import PartitionSpec as P

GRID = 16
BINS = 8
EPS = 1e-06
F32 = jnp.float32
BF16 = jnp.bfloat16
VMEM_BYTES = 56 * 1024 * 1024
LANES = 128
NT = (((1,), (1,)), ((), ()))
NN = (((1,), (0,)), ((), ()))
TN = (((0,), (0,)), ((), ()))


def dot(left, right, dims):
    return lax.dot_general(left, right, dims, preferred_element_type=F32)


def swap(value, axis, bit):
    size = lax.axis_size(axis)
    return lax.ppermute(value, axis, [(i, i ^ bit) for i in range(size)])


def round_up(value, unit):
    return -(-value // unit) * unit


def ordered(bit, mine, other, axis):
    first = jnp.where(bit == 0, mine, other)
    second = jnp.where(bit == 0, other, mine)
    return jnp.concatenate([first, second], axis=axis)


def gather_rows(value, axis):
    size, me = lax.axis_size(axis), lax.axis_index(axis)
    step = 1
    while step < size:
        other = swap(value, axis, step)
        value = ordered((me // step) % 2, value, other, 0)
        step *= 2
    return value


def scatter_rows(value, axis):
    size, me = lax.axis_size(axis), lax.axis_index(axis)
    step = size // 2
    while step >= 1:
        half = value.shape[0] // 2
        bit = (me // step) % 2
        keep = jnp.where(bit == 0, value[:half], value[half:])
        send = jnp.where(bit == 0, value[half:], value[:half])
        value = keep + swap(send, axis, step)
        step //= 2
    return value


def rows_to_columns(value, axis):
    size, me = lax.axis_size(axis), lax.axis_index(axis)
    step = 1
    while step < size:
        rows, cols = value.shape
        bit = (me // step) % 2
        per = rows // (size // step)
        split = value.reshape(size // step // 2, 2, per, cols)
        keep = jnp.where(bit == 0, split[:, 0], split[:, 1]).reshape(rows // 2, cols)
        send = jnp.where(bit == 0, split[:, 1], split[:, 0]).reshape(rows // 2, cols)
        value = ordered(bit, keep, swap(send, axis, step), 1)
        step *= 2
    return value


def mp_sum_small(value):
    step = lax.axis_size("mp") // 2
    while step >= 1:
        value = value + swap(value, "mp", step)
        step //= 2
    return value


def mp_pieces(value):
    far = swap(value, "mp", 2)
    near = swap(value, "mp", 1)
    both = swap(far, "mp", 1)
    return [value, far, near, both]


def mp_total(partial):
    other = swap(partial, "mp", 1)
    chip = (partial.astype(F32) + other.astype(F32)).astype(BF16)
    half = partial.shape[1] // 2
    core = lax.axis_index("mp") % 2
    mine = lax.dynamic_slice_in_dim(chip, core * half, half, 1)
    far = swap(mine, "mp", 2)
    far_other = swap(far, "mp", 1)
    return chip, far, far_other


def mp_quarter(partial):
    images, width, patches = partial.shape
    quarter = width // 4
    me = lax.axis_index("mp")
    core, side = me % 2, me // 2
    split = partial.reshape(images, 2, 2, quarter, patches)
    send = jnp.where(core == 0, split[:, :, 1], split[:, :, 0])
    keep = jnp.where(core == 0, split[:, :, 0], split[:, :, 1])
    chip = keep.astype(F32) + swap(send, "mp", 1).astype(F32)
    send = jnp.where(side == 0, chip[:, 1], chip[:, 0]).astype(BF16)
    keep = jnp.where(side == 0, chip[:, 0], chip[:, 1])
    return keep + swap(send, "mp", 2).astype(F32)


def dp_blocks(block):
    size, me = lax.axis_size("dp"), lax.axis_index("dp")
    outer = size // 2
    if size % 2 or outer > 4 or outer & (outer - 1):
        return [lax.all_gather(block, "dp", axis=0, tiled=True)], [jnp.int32(0)]
    blocks, owners = [block, swap(block, "dp", 1)], [me, me ^ 1]
    for step in range(1, outer):
        got = swap(block, "dp", 2 * step)
        blocks.append(got)
        owners.append(me ^ (2 * step))
        blocks.append(swap(got, "dp", 1))
        owners.append(me ^ (2 * step) ^ 1)
    return blocks, owners


def rotary_tables(patches, head_size):
    pairs = head_size // 4
    freqs = 10000.0 ** (-np.arange(pairs, dtype=np.float64) / pairs)
    spots = np.arange(patches)
    row = (spots // GRID)[None, :] * freqs[:, None]
    col = (spots % GRID)[None, :] * freqs[:, None]
    angles = np.concatenate([row, row, col, col], axis=0)
    cosine, sine = np.cos(angles), np.sin(angles)
    first = (np.arange(head_size) // pairs % 2 == 0)[:, None]
    up = np.where(first, -sine, 0.0)
    down = np.where(first, 0.0, sine)
    return np.stack([cosine, up, down]).astype(np.float32)


def turned(value, up, down):
    height = value.shape[0]
    pairs = height // 4
    return pltpu.roll(value, height - pairs, 0) * up + pltpu.roll(value, pairs, 0) * down


def normed(value):
    centred = value - jnp.mean(value, axis=0, keepdims=True)
    scale = lax.rsqrt(jnp.mean(centred * centred, axis=0, keepdims=True) + EPS)
    return centred * scale, scale


def norm_back(grad, unit, scale):
    return scale * (
        grad
        - jnp.mean(grad, axis=0, keepdims=True)
        - unit * jnp.mean(grad * unit, axis=0, keepdims=True)
    )


def row_sums(value):
    ones = jnp.ones((8, value.shape[1]), F32)
    return lax.dot_general(
        ones, value, NT, precision=lax.Precision.HIGHEST, preferred_element_type=F32
    )[0:1]


def rows_at(index, size):
    return pl.ds(pl.multiple_of(index * size, 16), size)


def heads_of(raw, gains, tables, head):
    size = gains.shape[0]
    width = raw.shape[0] // 3
    cosine, up, down = tables[0], tables[1], tables[2]
    found = []
    for part in range(2):
        rows = raw[part * width + head * size : part * width + (head + 1) * size]
        scale = lax.rsqrt(jnp.mean(rows * rows, axis=0, keepdims=True) + EPS)
        hat = rows * scale
        gained = hat * gains[:, part : part + 1]
        rotated = gained * cosine + turned(gained, up, down)
        found.append((hat, scale, rotated.astype(BF16)))
    value = raw[2 * width + head * size : 2 * width + (head + 1) * size].astype(BF16)
    return found[0], found[1], value


def attention_forward(
    dims, place, lat_refs, mods_ref, weight_refs, gains_ref, tables_ref, outs, scratch
):
    heads, block_rows = dims
    lat_ref, weight_ref, h_ref, raw_ref, lse_ref, ob_ref, attn_ref = outs
    (x_ref,) = scratch
    quarter = lat_refs[0].shape[1]
    width = quarter
    size = gains_ref.shape[0]
    inverse = 1.0 / math.sqrt(size)

    @pl.when(pl.program_id(0) == 0)
    def _():
        for k, ref in enumerate(weight_refs):
            if len(weight_refs) == 1:
                weight_ref[...] = ref[...]
            else:
                weight_ref[rows_at(place[4 + k], block_rows), :] = ref[...]

    for k, ref in enumerate(lat_refs):
        piece = ref[0]
        lat_ref[0, rows_at(place[k], quarter), :] = piece
        x_ref[rows_at(place[k], quarter), :] = piece.astype(F32)
    mods = mods_ref[0].T
    unit, _ = normed(x_ref[...])
    h = (unit * (1.0 + mods[:, 1:2]) + mods[:, 0:1]).astype(BF16)
    h_ref[0] = h
    span = round_up(3 * width, LANES)
    raw = dot(weight_ref[:, :span], h, TN)[: 3 * width]
    raw_ref[0] = raw
    gains, tables = gains_ref[...], tables_ref[...]
    pad = 4 * width - (3 * width) // LANES * LANES - width
    parts, tops = [], []
    for head in range(heads):
        (_, _, query), (_, _, key), value = heads_of(raw, gains, tables, head)
        scores = dot(key, query, TN) * inverse
        top = jnp.max(scores, axis=0, keepdims=True)
        expo = jnp.exp(scores - top)
        total = jnp.sum(expo, axis=0, keepdims=True)
        probs = (expo / total).astype(BF16)
        parts.append(dot(value, probs, NN))
        tops.append(top + jnp.log(total))
    lse_ref[0] = jnp.concatenate(tops, axis=0)
    patches = raw.shape[1]
    ob = jnp.concatenate([jnp.zeros((pad, patches), F32)] + parts, axis=0).astype(BF16)
    ob_ref[0] = ob
    attn_ref[0] = dot(weight_ref[:, 4 * width - width - pad :], ob, NN).astype(BF16)


def feed_forward(
    place, image_weight, lat_ref, sums, mods_ref, cot_refs, weight_ref, outs, scratch
):
    mid_ref, attn_ref, h_ref, hidden_ref, dffn_ref, dgu_ref, cot_ref, dh_ref = outs
    (x_ref,) = scratch
    chip_ref, far_ref, other_ref = sums
    half = far_ref.shape[1]
    quarter = cot_refs[0].shape[1]
    units = hidden_ref.shape[1]
    mods = mods_ref[0].T
    add_sums(place, x_ref, chip_ref, far_ref, other_ref, half)
    attn_ref[0] = x_ref[rows_at(place[0], quarter), :]
    mid = lat_ref[0].astype(F32) + mods[:, 2:3] * x_ref[...]
    mid_ref[0] = mid
    unit, _ = normed(mid)
    h = (unit * (1.0 + mods[:, 4:5]) + mods[:, 3:4]).astype(BF16)
    h_ref[0] = h
    for k, ref in enumerate(cot_refs):
        piece = ref[0]
        cot_ref[0, rows_at(place[k], quarter), :] = piece
    weight = image_weight[pl.program_id(0)]
    dffn = (mods[:, 5:6] * (cot_ref[0].astype(F32) * weight)).astype(BF16)
    dffn_ref[0] = dffn
    gate = dot(weight_ref[:, :units], h, TN)
    up = dot(weight_ref[:, units : 2 * units], h, TN)
    sig = jax.nn.sigmoid(gate)
    swish = gate * sig
    hidden_ref[0] = (swish * up).astype(BF16)
    dhidden = dot(weight_ref[:, 2 * units :], dffn, TN)
    dgu_ref[0, :units] = (dhidden * up * sig * (1.0 + gate * (1.0 - sig))).astype(BF16)
    dgu_ref[0, units:] = (dhidden * swish).astype(BF16)
    dh_ref[0] = dot(weight_ref[:, : 2 * units], dgu_ref[0], NN).astype(BF16)


def add_sums(place, x_ref, chip_ref, far_ref, other_ref, half):
    x_ref[...] = chip_ref[0].astype(F32)
    core = place[3 + 1]
    x_ref[rows_at(core, half), :] += far_ref[0].astype(F32)
    x_ref[rows_at(1 - core, half), :] += other_ref[0].astype(F32)


def feed_forward_grads(h_ref, hidden_ref, dffn_ref, dgu_ref, weight_ref, grad_ref, ffn_ref):
    images = h_ref.shape[0]
    units = hidden_ref.shape[1]
    total, down = None, None
    for n in range(images):
        term = dot(h_ref[n], dgu_ref[n], NT)
        term_down = dot(dffn_ref[n], hidden_ref[n], NT)
        total = term if total is None else total + term
        down = term_down if down is None else down + term_down
    grad_ref[:, : 2 * units] = total.astype(BF16)
    grad_ref[:, 2 * units :] = down.astype(BF16)
    for n in range(images):
        ffn_ref[n] = dot(weight_ref[...], hidden_ref[n], NN).astype(BF16)


def attention_backward(
    heads,
    place,
    image_weight,
    sums,
    mid_ref,
    attn_ref,
    cot_ref,
    mods_ref,
    raw_ref,
    lse_ref,
    gains_ref,
    tables_ref,
    weight_ref,
    outs,
    scratch,
):
    dmid_ref, dattn_ref, draw_ref, dh_ref, dmods_ref, qgain_ref, kgain_ref = outs
    x_ref, y_ref = scratch
    chip_ref, far_ref, other_ref = sums
    half = far_ref.shape[1]
    quarter = attn_ref.shape[1]
    width = quarter
    size = gains_ref.shape[0]
    inverse = 1.0 / math.sqrt(size)
    mods = mods_ref[0].T
    add_sums(place, x_ref, chip_ref, far_ref, other_ref, half)
    unit, scale = normed(mid_ref[0])
    y_ref[...] = unit
    own = rows_at(place[0], quarter)
    dh_own = x_ref[own, :]
    dmods_ref[0] = jnp.zeros(dmods_ref.shape[1:], F32)
    dmods_ref[0, 3:4, :] = row_sums(dh_own)
    dmods_ref[0, 4:5, :] = row_sums(dh_own * y_ref[own, :])
    weight = image_weight[pl.program_id(0)]
    dy = cot_ref[0].astype(F32) * weight
    dmid = dy + norm_back(x_ref[...] * (1.0 + mods[:, 4:5]), unit, scale)
    dmid_ref[0] = dmid
    x_ref[...] = dmid
    dmods_ref[0, 2:3, :] = row_sums(x_ref[own, :] * attn_ref[0])
    dattn = (mods[:, 2:3] * dmid).astype(BF16)
    dattn_ref[0] = dattn
    start = (3 * width) // LANES * LANES
    pad = 3 * width - start
    dob = dot(weight_ref[:, start:], dattn, TN)
    raw = raw_ref[0]
    gains, tables = gains_ref[...], tables_ref[...]
    cosine, up, down = tables[0], tables[1], tables[2]
    parts = [[], [], []]
    sums_of = [None, None]
    for head in range(heads):
        query, key, value = heads_of(raw, gains, tables, head)
        grad = dob[pad + head * size : pad + (head + 1) * size].astype(BF16)
        scores = dot(key[2], query[2], TN) * inverse
        probs = jnp.exp(scores - lse_ref[0, head : head + 1, :])
        dprobs = dot(value, grad, TN)
        parts[2].append(dot(grad, probs.astype(BF16), NT))
        dscores = probs * (dprobs - jnp.sum(probs * dprobs, axis=0, keepdims=True))
        dscores = dscores.astype(BF16)
        turned_grads = (
            dot(key[2], dscores, NN) * inverse,
            dot(query[2], dscores, NT) * inverse,
        )
        for part, (rot, (hat, rms, _)) in enumerate(zip(turned_grads, (query, key))):
            back = rot * cosine - turned(rot, up, down)
            term = back * hat
            sums_of[part] = term if sums_of[part] is None else sums_of[part] + term
            g = back * gains[:, part : part + 1]
            parts[part].append(rms * (g - hat * jnp.mean(g * hat, axis=0, keepdims=True)))
    qgain_ref[0] = jnp.broadcast_to(row_sums(sums_of[0]), qgain_ref.shape[1:])
    kgain_ref[0] = jnp.broadcast_to(row_sums(sums_of[1]), kgain_ref.shape[1:])
    span = round_up(3 * width, LANES)
    patches = raw.shape[1]
    tail = [jnp.zeros((span - 3 * width, patches), F32)] if span > 3 * width else []
    draw = jnp.concatenate(parts[0] + parts[1] + parts[2] + tail, axis=0).astype(BF16)
    draw_ref[0] = draw
    dh_ref[0] = dot(weight_ref[:, :span], draw, NN).astype(BF16)


def attention_grads(h_ref, draw_ref, dattn_ref, ob_ref, grad_ref):
    images = h_ref.shape[0]
    span = draw_ref.shape[1]
    full = grad_ref.shape[1]
    start = full - ob_ref.shape[1]
    total, out = None, None
    for n in range(images):
        term = dot(h_ref[n], draw_ref[n], NT)
        term_out = dot(dattn_ref[n], ob_ref[n], NT)
        total = term if total is None else total + term
        out = term_out if out is None else out + term_out
    grad_ref[:, :start] = total[:, :start].astype(BF16)
    grad_ref[:, start:span] = (total[:, start:] + out[:, : span - start]).astype(BF16)
    grad_ref[:, span:] = out[:, span - start :].astype(BF16)


def last_steps(
    place, image_weight, keep, sums, lat_ref, dmid_ref, mid_ref, cot_ref, mods_ref, ffn_ref,
    dmods_ref, outs, scratch
):
    out_ref, dlat_ref, dm_ref = outs
    x_ref, y_ref = scratch
    chip_ref, far_ref, other_ref = sums
    half = far_ref.shape[1]
    quarter = ffn_ref.shape[1]
    own = rows_at(place[0], quarter)
    mods = mods_ref[0].T
    add_sums(place, x_ref, chip_ref, far_ref, other_ref, half)
    unit, scale = normed(lat_ref[0].astype(F32))
    y_ref[...] = unit
    dh_own = x_ref[own, :]
    dm_ref[0] = dmods_ref[0]
    dm_ref[0, 0:1, :] = row_sums(dh_own)
    dm_ref[0, 1:2, :] = row_sums(dh_own * y_ref[own, :])
    back = norm_back(x_ref[...] * (1.0 + mods[:, 1:2]), unit, scale)
    x_ref[...] = back
    dlat_ref[0] = (dmid_ref[0, own, :] + x_ref[own, :]).astype(BF16)
    n = pl.program_id(0)
    ffn = ffn_ref[0]
    dy = cot_ref[0, own, :].astype(F32) * image_weight[n]
    dm_ref[0, 5:6, :] = row_sums(dy * ffn)
    y_ref[...] = jnp.broadcast_to(mods[:, 5:6], y_ref.shape)
    out_ref[0] = ((mid_ref[0, own, :] + y_ref[own, :] * ffn) * keep[n]).astype(BF16)


def whole(array):
    return pl.BlockSpec(array.shape, lambda n: (0,) * array.ndim)


def each(array):
    return pl.BlockSpec((1,) + array.shape[1:], lambda n: (n,) + (0,) * (array.ndim - 1))


SCALARS = pl.BlockSpec(memory_space=pltpu.SMEM)


def call(body, groups, outs, scratch, images, flops):
    flat, specs, counts = [], [], []
    for group in groups:
        counts.append(len(group))
        for array, kind in group:
            flat.append(array)
            specs.append(SCALARS if kind is None else kind(array))

    def kernel(*refs):
        at, lists = 0, []
        for count in counts:
            lists.append(list(refs[at : at + count]))
            at += count
        body(*lists, list(refs[at : at + len(outs)]), list(refs[at + len(outs) :]))

    moved = sum(a.size * a.dtype.itemsize for a in flat) + sum(
        math.prod(o.shape) * o.dtype.itemsize for o, _ in outs
    )
    return pl.pallas_call(
        kernel,
        grid=(images,),
        in_specs=specs,
        out_specs=[kind(o) for o, kind in outs],
        out_shape=[o for o, _ in outs],
        scratch_shapes=scratch,
        compiler_params=pltpu.CompilerParams(
            dimension_semantics=("arbitrary",), vmem_limit_bytes=VMEM_BYTES
        ),
        cost_estimate=pl.CostEstimate(flops=flops, bytes_accessed=moved, transcendentals=0),
    )(*flat)


def shaped(shape, dtype):
    return jax.ShapeDtypeStruct(shape, dtype)


def body(
    latents,
    condition,
    noise_bins,
    slot_valid,
    ada_weight,
    ada_bias,
    qkv_weight,
    query_gain,
    key_gain,
    out_weight,
    gate_up,
    down_weight,
    cotangent,
):
    images, patches, quarter = latents.shape
    width = condition.shape[1]
    rows = qkv_weight.shape[0]
    units = gate_up.shape[2]
    head_size = query_gain.shape[0]
    heads = quarter // head_size
    dp, mp = lax.axis_index("dp"), lax.axis_index("mp")
    dp_size = lax.axis_size("dp")
    all_images = dp_size * images
    tokens = images * patches

    extra = jnp.stack([noise_bins, slot_valid], axis=1).astype(BF16)
    told = jnp.concatenate([condition, extra, jnp.zeros((images, LANES - 2), BF16)], axis=1)
    told = gather_rows(told, "dp")
    all_bins, all_valid = told[:, width].astype(F32), told[:, width + 1].astype(F32)
    cond_all = told[:, :width].astype(F32)

    first_pack = jnp.concatenate(
        [
            jnp.transpose(qkv_weight, (1, 0, 2))[0],
            jnp.transpose(qkv_weight, (1, 0, 2))[1],
            jnp.transpose(qkv_weight, (1, 0, 2))[2],
            out_weight.T,
        ],
        axis=1,
    )
    second_pack = jnp.concatenate([gate_up[:, 0], gate_up[:, 1], down_weight.T], axis=1)
    lat_pieces = mp_pieces(jnp.transpose(latents, (0, 2, 1)))
    blocks, owners = dp_blocks(first_pack)
    second = lax.all_gather(second_pack, "dp", axis=0, tiled=True)
    cot_pieces = mp_pieces(jnp.transpose(cotangent, (0, 2, 1)))

    bin_ids = jnp.arange(BINS, dtype=F32)
    member = (all_bins[:, None] == bin_ids[None, :]).astype(F32) * all_valid[:, None]
    per_bin = jnp.sum(member, axis=0)
    own_count = jnp.sum(member * per_bin[None, :], axis=1)
    weight_all = all_valid * jnp.sum(all_valid) / (BINS * jnp.maximum(own_count, 1.0))
    image_weight = lax.dynamic_slice_in_dim(weight_all, dp * images, images)
    keep = slot_valid.astype(F32)

    cond_rows = lax.dynamic_slice_in_dim(cond_all, dp * rows, rows, 1)
    cond_act = jax.nn.silu(cond_rows).astype(BF16)
    ada = jnp.transpose(ada_weight, (1, 0, 2))
    mods_terms = jnp.einsum("nd,cde->nce", cond_act, ada, preferred_element_type=F32)
    mods_own = scatter_rows(mods_terms.reshape(all_images, -1), "dp")
    mods_own = mods_own.reshape(images, 6, quarter) + ada_bias[None]
    mods_own = jnp.pad(mods_own, ((0, 0), (0, 2), (0, 0)))
    side, core = mp // 2, mp % 2
    far = swap(mods_own, "mp", 2)
    pair = jnp.stack([jnp.where(side == 0, mods_own, far), jnp.where(side == 0, far, mods_own)])
    near = swap(pair, "mp", 1)
    quad = jnp.stack([jnp.where(core == 0, pair, near), jnp.where(core == 0, near, pair)], axis=1)
    mods = jnp.transpose(quad, (2, 3, 0, 1, 4)).reshape(images, 8, width)

    place = jnp.stack(
        [mp, mp ^ 2, mp ^ 1, mp ^ 3] + [jnp.asarray(o, jnp.int32) for o in owners]
    ).astype(jnp.int32)
    core_place = jnp.stack([mp, mp ^ 2, mp ^ 1, mp ^ 3, core]).astype(jnp.int32)
    gains = jnp.stack([query_gain, key_gain], axis=1)
    tables = jnp.asarray(rotary_tables(patches, head_size))
    full = 4 * quarter
    span = round_up(3 * quarter, LANES)
    start = 3 * quarter // LANES * LANES
    wide = lambda dtype: shaped((images, width, patches), dtype)
    tall = pltpu.VMEM((width, patches), F32)

    lat, first, h_one, raw, lse, ob, attn_part = call(
        lambda p, l, m, w, g, t, outs, s: attention_forward(
            (heads, rows), p[0], l, m[0], w, g[0], t[0], outs, s
        ),
        [
            [(place, None)],
            [(a, each) for a in lat_pieces],
            [(mods, each)],
            [(a, whole) for a in blocks],
            [(gains, whole)],
            [(tables, whole)],
        ],
        [
            (wide(BF16), each),
            (shaped((width, full), BF16), whole),
            (wide(BF16), each),
            (shaped((images, 3 * quarter, patches), F32), each),
            (shaped((images, heads, patches), F32), each),
            (shaped((images, full - start, patches), BF16), each),
            (wide(BF16), each),
        ],
        [tall],
        images,
        2 * tokens * width * full,
    )
    attn_sums = mp_total(attn_part)

    mid, attn_own, h_two, hidden, dffn, dgu, cot, dh_two_part = call(
        lambda p, w, l, s, m, c, k, outs, x: feed_forward(
            p[0], w[0], l[0], s, m[0], c, k[0], outs, x
        ),
        [
            [(core_place, None)],
            [(image_weight, None)],
            [(lat, each)],
            [(a, each) for a in attn_sums],
            [(mods, each)],
            [(a, each) for a in cot_pieces],
            [(second, whole)],
        ],
        [
            (wide(F32), each),
            (shaped((images, quarter, patches), F32), each),
            (wide(BF16), each),
            (shaped((images, units, patches), BF16), each),
            (wide(BF16), each),
            (shaped((images, 2 * units, patches), BF16), each),
            (wide(BF16), each),
            (wide(BF16), each),
        ],
        [tall],
        images,
        2 * tokens * width * units * 5,
    )
    dh_two_sums = mp_total(dh_two_part)
    second_grad, ffn_part = call(
        lambda a, outs, x: feed_forward_grads(*a, *outs),
        [[(h_two, whole), (hidden, whole), (dffn, whole), (dgu, whole), (second[:, 2 * units :], whole)]],
        [(shaped((width, 3 * units), BF16), whole), (wide(BF16), whole)],
        [],
        1,
        2 * tokens * width * units * 4,
    )
    second_sum = lax.psum_scatter(second_grad, "dp", scatter_dimension=0, tiled=True)
    ffn_own = mp_quarter(ffn_part)

    dmid, dattn, draw, dh_one_part, dmods_part, qgain, kgain = call(
        lambda p, w, s, a, outs, x: attention_backward(heads, p[0], w[0], s, *a, outs, x),
        [
            [(core_place, None)],
            [(image_weight, None)],
            [(a, each) for a in dh_two_sums],
            [
                (mid, each),
                (attn_own, each),
                (cot, each),
                (mods, each),
                (raw, each),
                (lse, each),
                (gains, whole),
                (tables, whole),
                (first, whole),
            ],
        ],
        [
            (wide(F32), each),
            (wide(BF16), each),
            (shaped((images, span, patches), BF16), each),
            (wide(BF16), each),
            (shaped((images, 8, quarter), F32), each),
            (shaped((images, 8, head_size), F32), each),
            (shaped((images, 8, head_size), F32), each),
        ],
        [tall, tall],
        images,
        2 * tokens * width * full,
    )
    dh_one_sums = mp_total(dh_one_part)
    (first_grad,) = call(
        lambda a, outs, x: attention_grads(*a, *outs),
        [[(h_one, whole), (draw, whole), (dattn, whole), (ob, whole)]],
        [(shaped((width, full), BF16), whole)],
        [],
        1,
        2 * tokens * width * full,
    )
    first_sum = lax.psum_scatter(first_grad, "dp", scatter_dimension=0, tiled=True)

    block_out, latent_grad, dmods = call(
        lambda p, w, k, s, a, outs, x: last_steps(p[0], w[0], k[0], s, *a, outs, x),
        [
            [(core_place, None)],
            [(image_weight, None)],
            [(keep, None)],
            [(a, each) for a in dh_one_sums],
            [
                (lat, each),
                (dmid, each),
                (mid, each),
                (cot, each),
                (mods, each),
                (ffn_own, each),
                (dmods_part, each),
            ],
        ],
        [
            (shaped((images, quarter, patches), BF16), each),
            (shaped((images, quarter, patches), BF16), each),
            (shaped((images, 8, quarter), F32), each),
        ],
        [tall, tall],
        images,
        tokens * width * 20,
    )

    gain_terms = jnp.concatenate([jnp.sum(qgain[:, 0], axis=0), jnp.sum(kgain[:, 0], axis=0)])
    high = gain_terms.astype(BF16)
    low = (gain_terms - high.astype(F32)).astype(BF16)
    beside = jnp.concatenate([high, low])[None]
    beside = jnp.concatenate([beside, jnp.zeros((images - 1, beside.shape[1]), BF16)], axis=0)
    told_back = jnp.concatenate(
        [dmods[:, :6].astype(BF16).reshape(images, 6 * quarter), beside], axis=1
    )
    told_back = gather_rows(told_back, "dp")
    dmods_all = told_back[:, : 6 * quarter].reshape(all_images, 6, quarter)
    gain_sum = jnp.sum(told_back[:, 6 * quarter :].astype(F32), axis=0)
    gain_sum = gain_sum[: 2 * head_size] + gain_sum[2 * head_size :]
    ada_grad = jnp.einsum("nd,nce->cde", cond_act, dmods_all, preferred_element_type=F32)
    ada_grad = jnp.transpose(ada_grad, (1, 0, 2))
    bias_grad = jnp.sum(dmods_all.astype(F32), axis=0)
    cond_terms = jnp.einsum("nce,cde->nd", dmods_all, ada, preferred_element_type=F32)
    both = jnp.concatenate([cond_terms.reshape(-1), gain_sum])
    both = mp_sum_small(both)
    gain_sum = both[cond_terms.size :]
    cond_sum = rows_to_columns(both[: cond_terms.size].reshape(cond_terms.shape), "dp")
    cond_own = condition.astype(F32)
    sig = jax.nn.sigmoid(cond_own)
    condition_grad = (cond_sum * sig * (1.0 + cond_own * (1.0 - sig))).astype(BF16)

    second_sum = second_sum.astype(F32)
    first_sum = first_sum.astype(F32)
    gateup_grad = jnp.stack([second_sum[:, :units], second_sum[:, units : 2 * units]], axis=1)
    down_grad = second_sum[:, 2 * units :].T
    qkv_grad = first_sum[:, : 3 * quarter].reshape(rows, 3, quarter)
    out_grad = first_sum[:, 3 * quarter :].T
    return (
        jnp.transpose(block_out, (0, 2, 1)),
        jnp.transpose(latent_grad, (0, 2, 1)),
        condition_grad,
        ada_grad,
        bias_grad,
        qkv_grad,
        gain_sum[:head_size],
        gain_sum[head_size:],
        out_grad,
        gateup_grad,
        down_grad,
    )


def solution(mesh):
    placed = (
        P("dp", None, "mp"),
        P("dp", None),
        P("dp"),
        P("dp"),
        P("dp", None, "mp"),
        P(None, "mp"),
        P("dp", None, "mp"),
        P(),
        P(),
        P("mp", "dp"),
        P("dp", None, "mp"),
        P("mp", "dp"),
        P("dp", None, "mp"),
    )
    return jax.shard_map(
        body,
        mesh=mesh,
        in_specs=placed,
        out_specs=(
            P("dp", None, "mp"),
            P("dp", None, "mp"),
            P("dp", None),
            P("dp", None, "mp"),
            P(None, "mp"),
            P("dp", None, "mp"),
            P(),
            P(),
            P("mp", "dp"),
            P("dp", None, "mp"),
            P("mp", "dp"),
        ),
        check_vma=False,
    )
```

```python
import functools
import math

import jax
import jax.numpy as jnp
import numpy as np
from jax import lax
from jax.experimental import pallas as pl
from jax.experimental.pallas import tpu as pltpu
from jax.sharding import PartitionSpec as P

GRID = 16
BINS = 8
EPS = 1e-06
F32 = jnp.float32
BF16 = jnp.bfloat16
VMEM_BYTES = 56 * 1024 * 1024
LANES = 128
NT = (((1,), (1,)), ((), ()))
NN = (((1,), (0,)), ((), ()))
TN = (((0,), (0,)), ((), ()))


def dot(left, right, dims):
    return lax.dot_general(left, right, dims, preferred_element_type=F32)


def swap(value, axis, bit):
    size = lax.axis_size(axis)
    return lax.ppermute(value, axis, [(i, i ^ bit) for i in range(size)])


def round_up(value, unit):
    return -(-value // unit) * unit


def region(given, work):
    shapes = jax.eval_shape(work)
    return lax.cond(given, work, lambda: jax.tree.map(lambda a: jnp.zeros(a.shape, a.dtype), shapes))


def ordered(bit, mine, other, axis):
    first = jnp.where(bit == 0, mine, other)
    second = jnp.where(bit == 0, other, mine)
    return jnp.concatenate([first, second], axis=axis)


def gather_rows(value, axis):
    size, me = lax.axis_size(axis), lax.axis_index(axis)
    steps = [1 << k for k in range(size.bit_length() - 1)]
    shape = value.shape
    steps = steps[1:] + steps[:1]
    for step in steps:
        value = ordered((me // step) % 2, value[None], swap(value, axis, step)[None], 0)
    count = len(steps)
    order = sorted(range(count), key=lambda k: -steps[count - 1 - k])
    value = jnp.transpose(value, order + [count, count + 1])
    return value.reshape((size * shape[0],) + shape[1:])


def scatter_rows(value, axis):
    size, me = lax.axis_size(axis), lax.axis_index(axis)
    step = size // 2
    while step >= 1:
        half = value.shape[0] // 2
        bit = (me // step) % 2
        keep = jnp.where(bit == 0, value[:half], value[half:])
        send = jnp.where(bit == 0, value[half:], value[:half])
        value = keep + swap(send, axis, step)
        step //= 2
    return value


def rows_to_columns(value, axis):
    size, me = lax.axis_size(axis), lax.axis_index(axis)
    step = 1
    while step < size:
        rows, cols = value.shape
        bit = (me // step) % 2
        per = rows // (size // step)
        split = value.reshape(size // step // 2, 2, per, cols)
        keep = jnp.where(bit == 0, split[:, 0], split[:, 1]).reshape(rows // 2, cols)
        send = jnp.where(bit == 0, split[:, 1], split[:, 0]).reshape(rows // 2, cols)
        value = ordered(bit, keep, swap(send, axis, step), 1)
        step *= 2
    return value


def mp_sum_small(value):
    step = lax.axis_size("mp") // 2
    while step >= 1:
        value = value + swap(value, "mp", step)
        step //= 2
    return value


def mp_pieces(value):
    far = swap(value, "mp", 2)
    near = swap(value, "mp", 1)
    both = swap(far, "mp", 1)
    return [value, far, near, both]


def mp_chip(mine, theirs, *tokens):
    return add_blocks(mine, swap(theirs, "mp", 1), *tokens)


def mp_join(chip, far, *tokens):
    half = add_blocks(chip, far, *tokens)
    return half, swap(half, "mp", 1)


def mp_total(mine, theirs, tokens=()):
    chip = mp_chip(mine, theirs)
    return mp_join(chip, swap(chip, "mp", 2), *tokens)


def mp_quarter(partial):
    images, width, patches = partial.shape
    quarter = width // 4
    me = lax.axis_index("mp")
    core, side = me % 2, me // 2
    split = partial.reshape(images, 2, 2, quarter, patches)
    send = jnp.where(core == 0, split[:, :, 1], split[:, :, 0])
    keep = jnp.where(core == 0, split[:, :, 0], split[:, :, 1])
    chip = keep.astype(F32) + swap(send, "mp", 1).astype(F32)
    send = jnp.where(side == 0, chip[:, 1], chip[:, 0]).astype(BF16)
    keep = jnp.where(side == 0, chip[:, 0], chip[:, 1])
    return keep + swap(send, "mp", 2).astype(F32)


def direct():
    return lax.axis_size("dp") in (2, 4, 8)


def dp_blocks(block):
    if not direct():
        return [lax.all_gather(block, "dp", axis=0, tiled=True)]
    size = lax.axis_size("dp")
    blocks = [block, swap(block, "dp", 1)]
    for k, near in [(k, swap(block, "dp", k)) for k in range(2, size, 2)]:
        blocks += [near, swap(near, "dp", 1)]
    return blocks


def dp_cross(parts):
    if len(parts) == 1:
        return [lax.psum_scatter(parts[0], "dp", scatter_dimension=0, tiled=True)]
    return [swap(parts[k + 1], "dp", 1) for k in range(0, len(parts), 2)]


def dp_pair_sums(parts, cross, *tokens):
    return [add_blocks(parts[2 * k], cross[k], *tokens) for k in range(1, len(cross))]


def dp_lines(halves):
    return [swap(half, "dp", 2 * k + 2) for k, half in enumerate(halves)]


def add_blocks(left, right, *tokens):
    def kernel(*refs):
        refs[-1][...] = (refs[0][...].astype(F32) + refs[1][...].astype(F32)).astype(BF16)

    return pl.pallas_call(
        kernel,
        in_specs=[pl.BlockSpec(memory_space=pltpu.VMEM)] * 2
        + [pl.BlockSpec(memory_space=pl.ANY)] * len(tokens),
        out_specs=pl.BlockSpec(memory_space=pltpu.VMEM),
        out_shape=shaped(left.shape, BF16),
        compiler_params=pltpu.CompilerParams(vmem_limit_bytes=VMEM_BYTES),
        cost_estimate=pl.CostEstimate(flops=1, bytes_accessed=1, transcendentals=0),
    )(left, right, *tokens)


def after(value, *others):
    if not others:
        return value

    def kernel(*refs):
        refs[-1][...] = refs[0][...]

    return pl.pallas_call(
        kernel,
        in_specs=[pl.BlockSpec(memory_space=pltpu.VMEM)]
        + [pl.BlockSpec(memory_space=pl.ANY)] * len(others),
        out_specs=pl.BlockSpec(memory_space=pltpu.VMEM),
        out_shape=shaped(value.shape, value.dtype),
        cost_estimate=pl.CostEstimate(flops=1, bytes_accessed=1, transcendentals=0),
    )(value, *others)


def copy_blocks(place, first, blocks, whole_ref):
    for k, ref in enumerate(blocks):
        if len(blocks) == 1:
            whole_ref[...] = ref[...]
        else:
            whole_ref[rows_at(place[first + k], ref.shape[0]), :] = ref[...]


def split_blocks(place, first, sum_ref, outs):
    for k, ref in enumerate(outs):
        if len(outs) == 1:
            ref[...] = sum_ref[...].astype(BF16)
        else:
            ref[...] = sum_ref[rows_at(place[first + k], ref.shape[0]), :].astype(BF16)


def rotary_tables(patches, head_size):
    pairs = head_size // 4
    freqs = 10000.0 ** (-np.arange(pairs, dtype=np.float64) / pairs)
    spots = np.arange(patches)
    row = (spots // GRID)[None, :] * freqs[:, None]
    col = (spots % GRID)[None, :] * freqs[:, None]
    angles = np.concatenate([row, row, col, col], axis=0)
    cosine, sine = np.cos(angles), np.sin(angles)
    first = (np.arange(head_size) // pairs % 2 == 0)[:, None]
    up = np.where(first, -sine, 0.0)
    down = np.where(first, 0.0, sine)
    return np.stack([cosine, up, down]).astype(np.float32)


def turned(value, up, down):
    height = value.shape[0]
    pairs = height // 4
    return pltpu.roll(value, height - pairs, 0) * up + pltpu.roll(value, pairs, 0) * down


def normed(value):
    centred = value - jnp.mean(value, axis=0, keepdims=True)
    scale = lax.rsqrt(jnp.mean(centred * centred, axis=0, keepdims=True) + EPS)
    return centred * scale, scale


def norm_back(grad, unit, scale):
    return scale * (
        grad
        - jnp.mean(grad, axis=0, keepdims=True)
        - unit * jnp.mean(grad * unit, axis=0, keepdims=True)
    )


def row_sums(value):
    ones = jnp.ones((8, value.shape[1]), F32)
    return lax.dot_general(
        ones, value, NT, precision=lax.Precision.HIGHEST, preferred_element_type=F32
    )[0:1]


def rows_at(index, size):
    return pl.ds(pl.multiple_of(index * size, 16), size)


def heads_of(raw, gains, tables, head):
    size = gains.shape[0]
    width = raw.shape[0] // 3
    cosine, up, down = tables[0], tables[1], tables[2]
    found = []
    for part in range(2):
        rows = raw[part * width + head * size : part * width + (head + 1) * size]
        scale = lax.rsqrt(jnp.mean(rows * rows, axis=0, keepdims=True) + EPS)
        hat = rows * scale
        gained = hat * gains[:, part : part + 1]
        rotated = gained * cosine + turned(gained, up, down)
        found.append((hat, scale, rotated.astype(BF16)))
    value = raw[2 * width + head * size : 2 * width + (head + 1) * size].astype(BF16)
    return found[0], found[1], value


def attention_forward(
    heads, place, lat_refs, mods_ref, weight_refs, gains_ref, tables_ref, outs, scratch
):
    lat_ref, weight_ref, h_ref, raw_ref, lse_ref, ob_ref, mine_ref, theirs_ref = outs
    (x_ref,) = scratch
    quarter = lat_refs[0].shape[1]
    width = quarter
    size = gains_ref.shape[0]
    inverse = 1.0 / math.sqrt(size)

    @pl.when(pl.program_id(0) == 0)
    def _():
        copy_blocks(place, 5, weight_refs, weight_ref)

    for k, ref in enumerate(lat_refs):
        piece = ref[0]
        lat_ref[0, rows_at(place[k], quarter), :] = piece
        x_ref[rows_at(place[k], quarter), :] = piece.astype(F32)
    mods = mods_ref[0].T
    unit, _ = normed(x_ref[...])
    h = (unit * (1.0 + mods[:, 1:2]) + mods[:, 0:1]).astype(BF16)
    h_ref[0] = h
    span = round_up(3 * width, LANES)
    raw = dot(weight_ref[:, :span], h, TN)[: 3 * width]
    raw_ref[0] = raw
    gains, tables = gains_ref[...], tables_ref[...]
    pad = 4 * width - (3 * width) // LANES * LANES - width
    parts, tops = [], []
    for head in range(heads):
        (_, _, query), (_, _, key), value = heads_of(raw, gains, tables, head)
        scores = dot(key, query, TN) * inverse
        top = jnp.max(scores, axis=0, keepdims=True)
        expo = jnp.exp(scores - top)
        total = jnp.sum(expo, axis=0, keepdims=True)
        probs = (expo / total).astype(BF16)
        parts.append(dot(value, probs, NN))
        tops.append(top + jnp.log(total))
    lse_ref[0] = jnp.concatenate(tops, axis=0)
    patches = raw.shape[1]
    ob = jnp.concatenate([jnp.zeros((pad, patches), F32)] + parts, axis=0).astype(BF16)
    ob_ref[0] = ob
    x_ref[...] = dot(weight_ref[:, 4 * width - width - pad :], ob, NN)
    put_halves(place, x_ref, mine_ref, theirs_ref)


def feed_forward(
    place, image_weight, lat_ref, sums, mods_ref, cot_refs, weight_ref, outs, scratch
):
    mid_ref, attn_ref, h_ref, hidden_ref, dffn_ref, dgu_ref, cot_ref, mine_ref, theirs_ref = outs
    (x_ref,) = scratch
    quarter = cot_refs[0].shape[1]
    units = hidden_ref.shape[1]
    mods = mods_ref[0].T
    take_halves(place, x_ref, sums)
    attn_ref[0] = x_ref[rows_at(place[0], quarter), :]
    mid = lat_ref[0].astype(F32) + mods[:, 2:3] * x_ref[...]
    mid_ref[0] = mid
    unit, _ = normed(mid)
    h = (unit * (1.0 + mods[:, 4:5]) + mods[:, 3:4]).astype(BF16)
    h_ref[0] = h
    for k, ref in enumerate(cot_refs):
        piece = ref[0]
        cot_ref[0, rows_at(place[k], quarter), :] = piece
    weight = image_weight[pl.program_id(0)]
    dffn = (mods[:, 5:6] * (cot_ref[0].astype(F32) * weight)).astype(BF16)
    dffn_ref[0] = dffn
    gate = dot(weight_ref[:, :units], h, TN)
    up = dot(weight_ref[:, units : 2 * units], h, TN)
    sig = jax.nn.sigmoid(gate)
    swish = gate * sig
    hidden_ref[0] = (swish * up).astype(BF16)
    dhidden = dot(weight_ref[:, 2 * units :], dffn, TN)
    dgu_ref[0, :units] = (dhidden * up * sig * (1.0 + gate * (1.0 - sig))).astype(BF16)
    dgu_ref[0, units:] = (dhidden * swish).astype(BF16)
    x_ref[...] = dot(weight_ref[:, : 2 * units], dgu_ref[0], NN)
    put_halves(place, x_ref, mine_ref, theirs_ref)


def put_halves(place, x_ref, mine_ref, theirs_ref):
    core, half = place[4], mine_ref.shape[1]
    mine_ref[0] = x_ref[rows_at(core, half), :].astype(BF16)
    theirs_ref[0] = x_ref[rows_at(1 - core, half), :].astype(BF16)


def take_halves(place, x_ref, halves):
    core, half = place[4], halves[0].shape[1]
    x_ref[rows_at(core, half), :] = halves[0][0].astype(F32)
    x_ref[rows_at(1 - core, half), :] = halves[1][0].astype(F32)


def over_images(left_ref, right_ref, rows=slice(None)):
    total = None
    for n in range(left_ref.shape[0]):
        term = dot(left_ref[n], right_ref[n, rows], NT)
        total = term if total is None else total + term
    return total


def feed_forward_grads(h_ref, hidden_ref, dffn_ref, dgu_ref, weight_ref, outs):
    units = hidden_ref.shape[1]
    grad_ref, ffn_ref = outs
    grad_ref[:, :units] = over_images(h_ref, dgu_ref, slice(0, units)).astype(BF16)
    grad_ref[:, units : 2 * units] = over_images(h_ref, dgu_ref, slice(units, 2 * units)).astype(BF16)
    grad_ref[:, 2 * units :] = over_images(dffn_ref, hidden_ref).astype(BF16)
    for n in range(h_ref.shape[0]):
        ffn_ref[n] = dot(weight_ref[...], hidden_ref[n], NN).astype(BF16)


def attention_backward(
    heads,
    place,
    image_weight,
    sums,
    mid_ref,
    attn_ref,
    cot_ref,
    mods_ref,
    raw_ref,
    lse_ref,
    gains_ref,
    tables_ref,
    weight_ref,
    outs,
    scratch,
):
    dmid_ref, dattn_ref, draw_ref, mine_ref, theirs_ref, dmods_ref, qgain_ref, kgain_ref = outs
    x_ref, y_ref = scratch
    quarter = attn_ref.shape[1]
    width = quarter
    size = gains_ref.shape[0]
    inverse = 1.0 / math.sqrt(size)
    mods = mods_ref[0].T
    take_halves(place, x_ref, sums)
    unit, scale = normed(mid_ref[0])
    y_ref[...] = unit
    own = rows_at(place[0], quarter)
    dh_own = x_ref[own, :]
    dmods_ref[0] = jnp.zeros(dmods_ref.shape[1:], F32)
    dmods_ref[0, 3:4, :] = row_sums(dh_own)
    dmods_ref[0, 4:5, :] = row_sums(dh_own * y_ref[own, :])
    weight = image_weight[pl.program_id(0)]
    dy = cot_ref[0].astype(F32) * weight
    dmid = dy + norm_back(x_ref[...] * (1.0 + mods[:, 4:5]), unit, scale)
    dmid_ref[0] = dmid
    x_ref[...] = dmid
    dmods_ref[0, 2:3, :] = row_sums(x_ref[own, :] * attn_ref[0])
    dattn = (mods[:, 2:3] * dmid).astype(BF16)
    dattn_ref[0] = dattn
    start = (3 * width) // LANES * LANES
    pad = 3 * width - start
    dob = dot(weight_ref[:, start:], dattn, TN)
    raw = raw_ref[0]
    gains, tables = gains_ref[...], tables_ref[...]
    cosine, up, down = tables[0], tables[1], tables[2]
    parts = [[], [], []]
    sums_of = [None, None]
    for head in range(heads):
        query, key, value = heads_of(raw, gains, tables, head)
        grad = dob[pad + head * size : pad + (head + 1) * size].astype(BF16)
        scores = dot(key[2], query[2], TN) * inverse
        probs = jnp.exp(scores - lse_ref[0, head : head + 1, :])
        dprobs = dot(value, grad, TN)
        parts[2].append(dot(grad, probs.astype(BF16), NT))
        dscores = probs * (dprobs - jnp.sum(probs * dprobs, axis=0, keepdims=True))
        dscores = dscores.astype(BF16)
        turned_grads = (
            dot(key[2], dscores, NN) * inverse,
            dot(query[2], dscores, NT) * inverse,
        )
        for part, (rot, (hat, rms, _)) in enumerate(zip(turned_grads, (query, key))):
            back = rot * cosine - turned(rot, up, down)
            term = back * hat
            sums_of[part] = term if sums_of[part] is None else sums_of[part] + term
            g = back * gains[:, part : part + 1]
            parts[part].append(rms * (g - hat * jnp.mean(g * hat, axis=0, keepdims=True)))
    qgain_ref[0] = jnp.broadcast_to(row_sums(sums_of[0]), qgain_ref.shape[1:])
    kgain_ref[0] = jnp.broadcast_to(row_sums(sums_of[1]), kgain_ref.shape[1:])
    span = round_up(3 * width, LANES)
    patches = raw.shape[1]
    tail = [jnp.zeros((span - 3 * width, patches), F32)] if span > 3 * width else []
    draw = jnp.concatenate(parts[0] + parts[1] + parts[2] + tail, axis=0).astype(BF16)
    draw_ref[0] = draw
    x_ref[...] = dot(weight_ref[:, :span], draw, NN)
    put_halves(place, x_ref, mine_ref, theirs_ref)


def attention_grads(place, h_ref, draw_ref, dattn_ref, ob_ref, outs, scratch):
    span = draw_ref.shape[1]
    (sum_ref,) = scratch
    start = sum_ref.shape[1] - ob_ref.shape[1]
    total = over_images(h_ref, draw_ref)
    out = over_images(dattn_ref, ob_ref)
    sum_ref[:, :start] = total[:, :start]
    sum_ref[:, start:span] = total[:, start:] + out[:, : span - start]
    sum_ref[:, span:] = out[:, span - start :]
    split_blocks(place, 5, sum_ref, outs)


def last_steps(
    place, image_weight, keep, sums, lat_ref, dmid_ref, mid_ref, cot_ref, mods_ref, ffn_ref,
    dmods_ref, outs, scratch
):
    out_ref, dlat_ref, dm_ref = outs
    x_ref, y_ref = scratch
    quarter = ffn_ref.shape[1]
    own = rows_at(place[0], quarter)
    mods = mods_ref[0].T
    take_halves(place, x_ref, sums)
    unit, scale = normed(lat_ref[0].astype(F32))
    y_ref[...] = unit
    dh_own = x_ref[own, :]
    dm_ref[0] = dmods_ref[0]
    dm_ref[0, 0:1, :] = row_sums(dh_own)
    dm_ref[0, 1:2, :] = row_sums(dh_own * y_ref[own, :])
    back = norm_back(x_ref[...] * (1.0 + mods[:, 1:2]), unit, scale)
    x_ref[...] = back
    dlat_ref[0] = (dmid_ref[0, own, :] + x_ref[own, :]).astype(BF16)
    n = pl.program_id(0)
    ffn = ffn_ref[0]
    dy = cot_ref[0, own, :].astype(F32) * image_weight[n]
    dm_ref[0, 5:6, :] = row_sums(dy * ffn)
    y_ref[...] = jnp.broadcast_to(mods[:, 5:6], y_ref.shape)
    out_ref[0] = ((mid_ref[0, own, :] + y_ref[own, :] * ffn) * keep[n]).astype(BF16)


def whole(array):
    return pl.BlockSpec(array.shape, lambda n: (0,) * array.ndim)


def last(array):
    width = array.shape[1] // 3
    return pl.BlockSpec((array.shape[0], width), lambda n: (0, 2))


def each(array):
    return pl.BlockSpec((1,) + array.shape[1:], lambda n: (n,) + (0,) * (array.ndim - 1))


def token(_):
    return pl.BlockSpec(memory_space=pl.ANY)


def scalars(_):
    return pl.BlockSpec(memory_space=pltpu.SMEM)


def call(body, groups, outs, scratch, images, flops=1):
    flat, specs, counts = [], [], []
    for group in groups:
        counts.append(len(group))
        for array, kind in group:
            flat.append(array)
            specs.append(kind(array))

    def kernel(*refs):
        at, lists = 0, []
        for count in counts:
            lists.append(list(refs[at : at + count]))
            at += count
        body(*lists, list(refs[at : at + len(outs)]), list(refs[at + len(outs) :]))

    moved = sum(a.size * a.dtype.itemsize for a in flat) if flops > 1 else 1
    return pl.pallas_call(
        kernel,
        grid=(images,),
        in_specs=specs,
        out_specs=[kind(o) for o, kind in outs],
        out_shape=[o for o, _ in outs],
        scratch_shapes=scratch,
        compiler_params=pltpu.CompilerParams(
            dimension_semantics=("arbitrary",), vmem_limit_bytes=VMEM_BYTES
        ),
        cost_estimate=pl.CostEstimate(flops=flops, bytes_accessed=moved, transcendentals=0),
    )(*flat)


def shaped(shape, dtype):
    return jax.ShapeDtypeStruct(shape, dtype)


def body(
    latents,
    condition,
    noise_bins,
    slot_valid,
    ada_weight,
    ada_bias,
    qkv_weight,
    query_gain,
    key_gain,
    out_weight,
    gate_up,
    down_weight,
    cotangent,
):
    images, patches, quarter = latents.shape
    width = condition.shape[1]
    rows = qkv_weight.shape[0]
    units = gate_up.shape[2]
    head_size = query_gain.shape[0]
    heads = quarter // head_size
    dp, mp = lax.axis_index("dp"), lax.axis_index("mp")
    core = mp % 2
    dp_size = lax.axis_size("dp")
    all_images = dp_size * images
    tokens = images * patches

    extra = jnp.stack([noise_bins, slot_valid], axis=1).astype(BF16)
    told = jnp.concatenate([condition, extra, jnp.zeros((images, LANES - 2), BF16)], axis=1)
    told = gather_rows(told, "dp")
    all_bins, all_valid = told[:, width].astype(F32), told[:, width + 1].astype(F32)
    cond_rows = lax.dynamic_slice_in_dim(told[:, :width], dp * rows, rows, 1).astype(F32)

    by_part = jnp.transpose(qkv_weight, (1, 0, 2))
    first_pack = jnp.concatenate([by_part[0], by_part[1], by_part[2], out_weight.T], axis=1)
    second_pack = jnp.concatenate([gate_up[:, 0], gate_up[:, 1], down_weight.T], axis=1)
    lat_pieces = mp_pieces(jnp.transpose(latents, (0, 2, 1)))
    first_blocks = dp_blocks(first_pack)
    second = lax.all_gather(second_pack, "dp", axis=0, tiled=True)
    cot_pieces = mp_pieces(jnp.transpose(cotangent, (0, 2, 1)))
    ada = jnp.transpose(ada_weight, (1, 0, 2))
    keep = slot_valid.astype(F32)
    given = noise_bins[0] >= 0

    bin_ids = jnp.arange(BINS, dtype=F32)
    member = (all_bins[:, None] == bin_ids[None, :]).astype(F32) * all_valid[:, None]
    per_bin = jnp.sum(member, axis=0)
    own_bins = noise_bins.astype(F32)
    own_count = jnp.sum((own_bins[:, None] == bin_ids[None, :]) * per_bin[None, :], axis=1)
    image_weight = keep * jnp.sum(all_valid) / (BINS * jnp.maximum(own_count, 1.0))

    cond_act = jax.nn.silu(cond_rows).astype(BF16)
    mods_terms = jnp.einsum("nd,cde->nce", cond_act, ada, preferred_element_type=F32)
    mods_own = scatter_rows(mods_terms.reshape(all_images, -1), "dp")
    mods_own = mods_own.reshape(images, 6, quarter) + ada_bias[None]
    mods_own = jnp.pad(mods_own, ((0, 0), (0, 2), (0, 0)))
    side = mp // 2
    far = swap(mods_own, "mp", 2)
    pair = jnp.stack([jnp.where(side == 0, mods_own, far), jnp.where(side == 0, far, mods_own)])
    beside = swap(pair, "mp", 1)
    quad = jnp.stack(
        [jnp.where(core == 0, pair, beside), jnp.where(core == 0, beside, pair)], axis=1
    )
    mods = jnp.transpose(quad, (2, 3, 0, 1, 4)).reshape(images, 8, width)

    count = dp_size if direct() else 1
    place = jnp.stack([mp, mp ^ 2, mp ^ 1, mp ^ 3, core] + [dp ^ k for k in range(count)])
    place = place.astype(jnp.int32)
    block_shape = (width // count,)
    gains = jnp.stack([query_gain, key_gain], axis=1)
    tables = jnp.asarray(rotary_tables(patches, head_size))
    full = 4 * quarter
    span = round_up(3 * quarter, LANES)
    start = 3 * quarter // LANES * LANES
    wide = lambda dtype: shaped((images, width, patches), dtype)
    half = shaped((images, width // 2, patches), BF16)
    tall = pltpu.VMEM((width, patches), F32)

    lat, first, h_one, raw, lse, ob, *attn_terms = call(
        lambda p, l, m, w, g, t, outs, s: attention_forward(
            heads, p[0], l, m[0], w, g[0], t[0], outs, s
        ),
        [
            [(place, scalars)],
            [(a, each) for a in lat_pieces],
            [(mods, each)],
            [(a, whole) for a in first_blocks],
            [(gains, whole)],
            [(tables, whole)],
        ],
        [
            (wide(BF16), each),
            (shaped((width, full), BF16), whole),
            (wide(BF16), each),
            (shaped((images, 3 * quarter, patches), F32), each),
            (shaped((images, heads, patches), F32), each),
            (shaped((images, full - start, patches), BF16), each),
            (half, each),
            (half, each),
        ],
        [tall],
        images,
        2 * images * patches * width * full,
    )
    attn_sums = mp_total(*attn_terms)

    def middle():
        mid, attn_own, h_two, hidden, dffn, dgu, cot, mine, theirs = call(
            lambda p, w, l, s, m, c, k, outs, x: feed_forward(
                p[0], w[0], l[0], s, m[0], c, k[0], outs, x
            ),
            [
                [(place, scalars)],
                [(image_weight, scalars)],
                [(lat, each)],
                [(a, each) for a in attn_sums],
                [(mods, each)],
                [(a, each) for a in cot_pieces],
                [(second, whole)],
            ],
            [
                (wide(F32), each),
                (shaped((images, quarter, patches), F32), each),
                (wide(BF16), each),
                (shaped((images, units, patches), BF16), each),
                (wide(BF16), each),
                (shaped((images, 2 * units, patches), BF16), each),
                (wide(BF16), each),
                (half, each),
                (half, each),
            ],
            [tall],
            images,
        )
        chip = mp_chip(mine, theirs)
        grads = call(
            lambda a, outs, x: feed_forward_grads(*a, outs),
            [[(h_two, whole), (hidden, whole), (dffn, whole), (dgu, whole), (second, last)]],
            [(shaped((width, 3 * units), BF16), whole), (wide(BF16), whole)],
            [],
            1,
        )
        return mid, attn_own, cot, chip, swap(chip, "mp", 2), grads

    mid, attn_own, cot, dh_two_chip, dh_two_far, grads = region(given, middle)
    second_terms, ffn_part = grads
    second_sum = lax.psum_scatter(second_terms, "dp", scatter_dimension=0, tiled=True)

    def backward():
        dh_two_sums = mp_join(dh_two_chip, dh_two_far)
        dmid, dattn, draw, mine, theirs, dmods_part, qgain, kgain = call(
            lambda p, w, s, a, outs, x: attention_backward(heads, p[0], w[0], s, *a, outs, x),
            [
                [(place, scalars)],
                [(image_weight, scalars)],
                [(a, each) for a in dh_two_sums],
                [
                    (mid, each),
                    (attn_own, each),
                    (cot, each),
                    (mods, each),
                    (raw, each),
                    (lse, each),
                    (gains, whole),
                    (tables, whole),
                    (first, whole),
                ],
            ],
            [
                (wide(F32), each),
                (wide(BF16), each),
                (shaped((images, span, patches), BF16), each),
                (half, each),
                (half, each),
                (shaped((images, 8, quarter), F32), each),
                (shaped((images, 8, head_size), F32), each),
                (shaped((images, 8, head_size), F32), each),
            ],
            [tall, tall],
            images,
        )
        first_terms = call(
            lambda p, a, outs, x: attention_grads(p[0], *a, outs, x),
            [
                [(place, scalars)],
                [(h_one, whole), (draw, whole), (dattn, whole), (ob, whole)],
            ],
            [(shaped(block_shape + (full,), BF16), whole)] * count,
            [pltpu.VMEM((width, full), F32)],
            1,
        )
        ffn_own = mp_quarter(ffn_part)
        first_beside = dp_cross(first_terms)
        dh_one_sums = mp_total(mine, theirs, tuple(first_terms))
        block_out, latent_grad, dmods = call(
            lambda p, w, k, s, a, outs, x: last_steps(p[0], w[0], k[0], s, *a, outs, x),
            [
                [(place, scalars)],
                [(image_weight, scalars)],
                [(keep, scalars)],
                [(a, each) for a in dh_one_sums],
                [
                    (lat, each),
                    (dmid, each),
                    (mid, each),
                    (cot, each),
                    (mods, each),
                    (ffn_own, each),
                    (dmods_part, each),
                ],
            ],
            [
                (shaped((images, quarter, patches), BF16), each),
                (shaped((images, quarter, patches), BF16), each),
                (shaped((images, 8, quarter), F32), each),
            ],
            [tall, tall],
            images,
        )

        gain_terms = jnp.concatenate([jnp.sum(qgain[:, 0], axis=0), jnp.sum(kgain[:, 0], axis=0)])
        high = gain_terms.astype(BF16)
        low = (gain_terms - high.astype(F32)).astype(BF16)
        beside = jnp.concatenate([high, low])[None]
        beside = jnp.concatenate([beside, jnp.zeros((images - 1, beside.shape[1]), BF16)], axis=0)
        rounded = dmods[:, :6].astype(BF16).reshape(images, 6 * quarter)
        told_back = gather_rows(jnp.concatenate([rounded, beside], axis=1), "dp")
        halves = dp_pair_sums(first_terms, first_beside) if count > 1 else []
        return block_out, latent_grad, told_back, first_terms[0], first_beside[0], halves

    block_out, latent_grad, told_back, first_own, first_beside, halves = region(given, backward)
    first_far = dp_lines(halves)

    def modulation_grads():
        dmods_all = told_back[:, : 6 * quarter].reshape(all_images, 6, quarter)
        gain_sum = jnp.sum(told_back[:, 6 * quarter :].astype(F32), axis=0)
        gain_sum = gain_sum[: 2 * head_size] + gain_sum[2 * head_size :]
        ada_grad = jnp.einsum("nd,nce->cde", cond_act, dmods_all, preferred_element_type=F32)
        bias_grad = jnp.sum(dmods_all.astype(F32), axis=0)
        cond_terms = jnp.einsum("nce,cde->nd", dmods_all, ada, preferred_element_type=F32)
        both = mp_sum_small(jnp.concatenate([cond_terms.reshape(-1), gain_sum]))
        gain_sum = both[cond_terms.size :]
        cond_sum = rows_to_columns(both[: cond_terms.size].reshape(cond_terms.shape), "dp")
        return ada_grad, bias_grad, gain_sum, cond_sum

    ada_grad, bias_grad, gain_sum, cond_sum = region(given, modulation_grads)
    first_sum = first_beside.astype(F32)
    if count > 1:
        first_sum = first_sum + first_own.astype(F32)
    for line in first_far:
        first_sum = first_sum + line.astype(F32)
    cond_own = condition.astype(F32)
    sig = jax.nn.sigmoid(cond_own)
    condition_grad = (cond_sum * sig * (1.0 + cond_own * (1.0 - sig))).astype(BF16)
    second_sum = second_sum.astype(F32)
    gateup_grad = jnp.stack([second_sum[:, :units], second_sum[:, units : 2 * units]], axis=1)
    down_grad = second_sum[:, 2 * units :].T
    qkv_grad = first_sum[:, : 3 * quarter].reshape(rows, 3, quarter)
    out_grad = first_sum[:, 3 * quarter :].T
    return (
        jnp.transpose(block_out, (0, 2, 1)),
        jnp.transpose(latent_grad, (0, 2, 1)),
        condition_grad,
        jnp.transpose(ada_grad, (1, 0, 2)),
        bias_grad,
        qkv_grad,
        gain_sum[:head_size],
        gain_sum[head_size:],
        out_grad,
        gateup_grad,
        down_grad,
    )


def solution(mesh):
    placed = (
        P("dp", None, "mp"),
        P("dp", None),
        P("dp"),
        P("dp"),
        P("dp", None, "mp"),
        P(None, "mp"),
        P("dp", None, "mp"),
        P(),
        P(),
        P("mp", "dp"),
        P("dp", None, "mp"),
        P("mp", "dp"),
        P("dp", None, "mp"),
    )
    return jax.shard_map(
        body,
        mesh=mesh,
        in_specs=placed,
        out_specs=(
            P("dp", None, "mp"),
            P("dp", None, "mp"),
            P("dp", None),
            P("dp", None, "mp"),
            P(None, "mp"),
            P("dp", None, "mp"),
            P(),
            P(),
            P("mp", "dp"),
            P("dp", None, "mp"),
            P("mp", "dp"),
        ),
        check_vma=False,
    )
```

```python
import functools
import math

import jax
import jax.numpy as jnp
import numpy as np
from jax import lax
from jax.experimental import pallas as pl
from jax.experimental.pallas import tpu as pltpu
from jax.sharding import PartitionSpec as P

GRID = 16
BINS = 8
EPS = 1e-06
F32 = jnp.float32
BF16 = jnp.bfloat16
VMEM_BYTES = 56 * 1024 * 1024
LANES = 128
NT = (((1,), (1,)), ((), ()))
NN = (((1,), (0,)), ((), ()))
TN = (((0,), (0,)), ((), ()))


def dot(left, right, dims):
    return lax.dot_general(left, right, dims, preferred_element_type=F32)


def swap(value, axis, bit):
    size = lax.axis_size(axis)
    return lax.ppermute(value, axis, [(i, i ^ bit) for i in range(size)])


def round_up(value, unit):
    return -(-value // unit) * unit


def region(given, work):
    shapes = jax.eval_shape(work)
    return lax.cond(given, work, lambda: jax.tree.map(lambda a: jnp.zeros(a.shape, a.dtype), shapes))


def ordered(bit, mine, other, axis):
    first = jnp.where(bit == 0, mine, other)
    second = jnp.where(bit == 0, other, mine)
    return jnp.concatenate([first, second], axis=axis)


def gather_rows(value, axis):
    size, me = lax.axis_size(axis), lax.axis_index(axis)
    steps = [1 << k for k in range(size.bit_length() - 1)]
    shape = value.shape
    steps = steps[1:] + steps[:1]
    for step in steps:
        value = ordered((me // step) % 2, value[None], swap(value, axis, step)[None], 0)
    count = len(steps)
    order = sorted(range(count), key=lambda k: -steps[count - 1 - k])
    value = jnp.transpose(value, order + [count, count + 1])
    return value.reshape((size * shape[0],) + shape[1:])


def scatter_rows(value, axis):
    size, me = lax.axis_size(axis), lax.axis_index(axis)
    step = size // 2
    while step >= 1:
        half = value.shape[0] // 2
        bit = (me // step) % 2
        keep = jnp.where(bit == 0, value[:half], value[half:])
        send = jnp.where(bit == 0, value[half:], value[:half])
        value = keep + swap(send, axis, step)
        step //= 2
    return value


def rows_to_columns(value, axis):
    size, me = lax.axis_size(axis), lax.axis_index(axis)
    step = 1
    while step < size:
        rows, cols = value.shape
        bit = (me // step) % 2
        per = rows // (size // step)
        split = value.reshape(size // step // 2, 2, per, cols)
        keep = jnp.where(bit == 0, split[:, 0], split[:, 1]).reshape(rows // 2, cols)
        send = jnp.where(bit == 0, split[:, 1], split[:, 0]).reshape(rows // 2, cols)
        value = ordered(bit, keep, swap(send, axis, step), 1)
        step *= 2
    return value


def mp_sum_small(value):
    step = lax.axis_size("mp") // 2
    while step >= 1:
        value = value + swap(value, "mp", step)
        step //= 2
    return value


def mp_pieces(value):
    far = swap(value, "mp", 2)
    near = swap(value, "mp", 1)
    both = swap(far, "mp", 1)
    return [value, far, near, both]


def mp_chip(mine, theirs, *tokens):
    return add_blocks(mine, swap(theirs, "mp", 1), *tokens)


def mp_join(chip, far, *tokens):
    half = add_blocks(chip, far, *tokens)
    return half, swap(half, "mp", 1)


def mp_total(mine, theirs, tokens=()):
    chip = mp_chip(mine, theirs)
    return mp_join(chip, swap(chip, "mp", 2), *tokens)


def mp_quarter(partial):
    images, width, patches = partial.shape
    quarter = width // 4
    me = lax.axis_index("mp")
    core, side = me % 2, me // 2
    split = partial.reshape(images, 2, 2, quarter, patches)
    send = jnp.where(core == 0, split[:, :, 1], split[:, :, 0])
    keep = jnp.where(core == 0, split[:, :, 0], split[:, :, 1])
    chip = keep.astype(F32) + swap(send, "mp", 1).astype(F32)
    send = jnp.where(side == 0, chip[:, 1], chip[:, 0]).astype(BF16)
    keep = jnp.where(side == 0, chip[:, 0], chip[:, 1])
    return keep + swap(send, "mp", 2).astype(F32)


def direct():
    return lax.axis_size("dp") in (2, 4, 8)


def along(value, pairs):
    return lax.ppermute(value, "dp", [(2 * a + y, 2 * b + y) for a, b in pairs for y in (0, 1)])


def line_first(block):
    up = along(block, [(0, 1), (1, 2), (2, 3)])
    return up, along(block, [(1, 0), (2, 1), (3, 2)])


def line_near(first, token):
    return pick(lax.axis_index("dp") // 2 % 2 == 1, first[0], first[1], token)


def line_second(first):
    return along(first[0], [(1, 2), (2, 3)]), along(first[1], [(1, 0), (2, 1)])


def line_two(first, token):
    second = line_second(first)
    return pick(lax.axis_index("dp") // 2 >= 2, second[0], second[1], token)


def line_rest(block, beside, first, one, two):
    me = lax.axis_index("dp")
    at = me // 2
    end = along(two, [(1, 0), (2, 3)])
    three = jnp.where(at == 0, end, jnp.where(at == 1, first[1], jnp.where(at == 2, first[0], end)))
    found = [block, one, two, three]
    places = [at, at ^ 1, jnp.where(at >= 2, at - 2, at + 2), 3 - at]
    blocks = found + beside + [swap(b, "dp", 1) for b in found[2:]]
    return blocks, [2 * p + me % 2 for p in places] + [2 * p + 1 - me % 2 for p in places]


def pick(flag, left, right, token):
    def kernel(flag_ref, left_ref, right_ref, _, out_ref):
        @pl.when(flag_ref[0] == 1)
        def _():
            out_ref[...] = left_ref[...]

        @pl.when(flag_ref[0] == 0)
        def _():
            out_ref[...] = right_ref[...]

    return pl.pallas_call(
        kernel,
        in_specs=[pl.BlockSpec(memory_space=pltpu.SMEM)]
        + [pl.BlockSpec(memory_space=pltpu.VMEM)] * 2
        + [pl.BlockSpec(memory_space=pl.ANY)],
        out_specs=pl.BlockSpec(memory_space=pltpu.VMEM),
        out_shape=shaped(left.shape, left.dtype),
        cost_estimate=pl.CostEstimate(flops=1, bytes_accessed=1, transcendentals=0),
    )(jnp.reshape(flag.astype(jnp.int32), (1,)), left, right, token)


def packed(gate_up, down, token):
    rows, units = down.shape

    def kernel(gate_up_ref, down_ref, _, out_ref):
        out_ref[:, :units] = gate_up_ref[0]
        out_ref[:, units : 2 * units] = gate_up_ref[1]
        out_ref[:, 2 * units :] = down_ref[...]

    return pl.pallas_call(
        kernel,
        in_specs=[pl.BlockSpec(memory_space=pltpu.VMEM)] * 2 + [pl.BlockSpec(memory_space=pl.ANY)],
        out_specs=pl.BlockSpec(memory_space=pltpu.VMEM),
        out_shape=shaped((rows, 3 * units), down.dtype),
        cost_estimate=pl.CostEstimate(flops=1, bytes_accessed=1, transcendentals=0),
    )(gate_up, down, token)


def dp_cross(parts):
    if len(parts) == 1:
        return [lax.psum_scatter(parts[0], "dp", scatter_dimension=0, tiled=True)]
    return [swap(parts[k + 1], "dp", 1) for k in range(0, len(parts), 2)]


def dp_pair_sums(parts, cross, *tokens):
    return [add_blocks(parts[2 * k], cross[k], *tokens) for k in range(1, len(cross))]


def dp_lines(halves):
    return [swap(half, "dp", 2 * k + 2) for k, half in enumerate(halves)]


def add_blocks(left, right, *tokens):
    def kernel(*refs):
        refs[-1][...] = (refs[0][...].astype(F32) + refs[1][...].astype(F32)).astype(BF16)

    return pl.pallas_call(
        kernel,
        in_specs=[pl.BlockSpec(memory_space=pltpu.VMEM)] * 2
        + [pl.BlockSpec(memory_space=pl.ANY)] * len(tokens),
        out_specs=pl.BlockSpec(memory_space=pltpu.VMEM),
        out_shape=shaped(left.shape, BF16),
        compiler_params=pltpu.CompilerParams(vmem_limit_bytes=VMEM_BYTES),
        cost_estimate=pl.CostEstimate(flops=1, bytes_accessed=1, transcendentals=0),
    )(left, right, *tokens)


def after(value, *others):
    if not others:
        return value

    def kernel(*refs):
        refs[-1][...] = refs[0][...]

    return pl.pallas_call(
        kernel,
        in_specs=[pl.BlockSpec(memory_space=pltpu.VMEM)]
        + [pl.BlockSpec(memory_space=pl.ANY)] * len(others),
        out_specs=pl.BlockSpec(memory_space=pltpu.VMEM),
        out_shape=shaped(value.shape, value.dtype),
        cost_estimate=pl.CostEstimate(flops=1, bytes_accessed=1, transcendentals=0),
    )(value, *others)


def copy_blocks(place, first, blocks, whole_ref):
    for k, ref in enumerate(blocks):
        if len(blocks) == 1:
            whole_ref[...] = ref[...]
        else:
            whole_ref[rows_at(place[first + k], ref.shape[0]), :] = ref[...]


def split_blocks(place, first, sum_ref, outs):
    for k, ref in enumerate(outs):
        if len(outs) == 1:
            ref[...] = sum_ref[...].astype(BF16)
        else:
            ref[...] = sum_ref[rows_at(place[first + k], ref.shape[0]), :].astype(BF16)


def rotary_tables(patches, head_size):
    pairs = head_size // 4
    freqs = 10000.0 ** (-np.arange(pairs, dtype=np.float64) / pairs)
    spots = np.arange(patches)
    row = (spots // GRID)[None, :] * freqs[:, None]
    col = (spots % GRID)[None, :] * freqs[:, None]
    angles = np.concatenate([row, row, col, col], axis=0)
    cosine, sine = np.cos(angles), np.sin(angles)
    first = (np.arange(head_size) // pairs % 2 == 0)[:, None]
    up = np.where(first, -sine, 0.0)
    down = np.where(first, 0.0, sine)
    return np.stack([cosine, up, down]).astype(np.float32)


def turned(value, up, down):
    height = value.shape[0]
    pairs = height // 4
    return pltpu.roll(value, height - pairs, 0) * up + pltpu.roll(value, pairs, 0) * down


def normed(value):
    centred = value - jnp.mean(value, axis=0, keepdims=True)
    scale = lax.rsqrt(jnp.mean(centred * centred, axis=0, keepdims=True) + EPS)
    return centred * scale, scale


def norm_back(grad, unit, scale):
    return scale * (
        grad
        - jnp.mean(grad, axis=0, keepdims=True)
        - unit * jnp.mean(grad * unit, axis=0, keepdims=True)
    )


def row_sums(value):
    ones = jnp.ones((8, value.shape[1]), F32)
    return lax.dot_general(
        ones, value, NT, precision=lax.Precision.HIGHEST, preferred_element_type=F32
    )[0:1]


def rows_at(index, size):
    return pl.ds(pl.multiple_of(index * size, 16), size)


def heads_of(raw, gains, tables, head):
    size = gains.shape[0]
    width = raw.shape[0] // 3
    cosine, up, down = tables[0], tables[1], tables[2]
    found = []
    for part in range(2):
        rows = raw[part * width + head * size : part * width + (head + 1) * size]
        scale = lax.rsqrt(jnp.mean(rows * rows, axis=0, keepdims=True) + EPS)
        hat = rows * scale
        gained = hat * gains[:, part : part + 1]
        rotated = gained * cosine + turned(gained, up, down)
        found.append((hat, scale, rotated.astype(BF16)))
    value = raw[2 * width + head * size : 2 * width + (head + 1) * size].astype(BF16)
    return found[0], found[1], value


def attention_forward(
    heads, place, lat_refs, mods_ref, weight_ref, gains_ref, tables_ref, outs, scratch
):
    lat_ref, h_ref, raw_ref, lse_ref, ob_ref, mine_ref, theirs_ref = outs
    (x_ref,) = scratch
    quarter = lat_refs[0].shape[1]
    width = quarter
    size = gains_ref.shape[0]
    inverse = 1.0 / math.sqrt(size)

    for k, ref in enumerate(lat_refs):
        piece = ref[0]
        lat_ref[0, rows_at(place[k], quarter), :] = piece
        x_ref[rows_at(place[k], quarter), :] = piece.astype(F32)
    mods = mods_ref[0].T
    unit, _ = normed(x_ref[...])
    h = (unit * (1.0 + mods[:, 1:2]) + mods[:, 0:1]).astype(BF16)
    h_ref[0] = h
    span = round_up(3 * width, LANES)
    raw = dot(weight_ref[:, :span], h, TN)[: 3 * width]
    raw_ref[0] = raw
    gains, tables = gains_ref[...], tables_ref[...]
    pad = 4 * width - (3 * width) // LANES * LANES - width
    parts, tops = [], []
    for head in range(heads):
        (_, _, query), (_, _, key), value = heads_of(raw, gains, tables, head)
        scores = dot(key, query, TN) * inverse
        top = jnp.max(scores, axis=0, keepdims=True)
        expo = jnp.exp(scores - top)
        total = jnp.sum(expo, axis=0, keepdims=True)
        probs = (expo / total).astype(BF16)
        parts.append(dot(value, probs, NN))
        tops.append(top + jnp.log(total))
    lse_ref[0] = jnp.concatenate(tops, axis=0)
    patches = raw.shape[1]
    ob = jnp.concatenate([jnp.zeros((pad, patches), F32)] + parts, axis=0).astype(BF16)
    ob_ref[0] = ob
    x_ref[...] = dot(weight_ref[:, 4 * width - width - pad :], ob, NN)
    put_halves(place, x_ref, mine_ref, theirs_ref)


def feed_forward(
    place, image_weight, lat_ref, sums, mods_ref, cot_refs, weight_ref, outs, scratch
):
    mid_ref, attn_ref, h_ref, hidden_ref, dffn_ref, dgu_ref, cot_ref, mine_ref, theirs_ref = outs
    (x_ref,) = scratch
    quarter = cot_refs[0].shape[1]
    units = hidden_ref.shape[1]
    mods = mods_ref[0].T
    take_halves(place, x_ref, sums)
    attn_ref[0] = x_ref[rows_at(place[0], quarter), :]
    mid = lat_ref[0].astype(F32) + mods[:, 2:3] * x_ref[...]
    mid_ref[0] = mid
    unit, _ = normed(mid)
    h = (unit * (1.0 + mods[:, 4:5]) + mods[:, 3:4]).astype(BF16)
    h_ref[0] = h
    for k, ref in enumerate(cot_refs):
        piece = ref[0]
        cot_ref[0, rows_at(place[k], quarter), :] = piece
    weight = image_weight[pl.program_id(0)]
    dffn = (mods[:, 5:6] * (cot_ref[0].astype(F32) * weight)).astype(BF16)
    dffn_ref[0] = dffn
    gate = dot(weight_ref[:, :units], h, TN)
    up = dot(weight_ref[:, units : 2 * units], h, TN)
    sig = jax.nn.sigmoid(gate)
    swish = gate * sig
    hidden_ref[0] = (swish * up).astype(BF16)
    dhidden = dot(weight_ref[:, 2 * units :], dffn, TN)
    dgu_ref[0, :units] = (dhidden * up * sig * (1.0 + gate * (1.0 - sig))).astype(BF16)
    dgu_ref[0, units:] = (dhidden * swish).astype(BF16)
    x_ref[...] = dot(weight_ref[:, : 2 * units], dgu_ref[0], NN)
    put_halves(place, x_ref, mine_ref, theirs_ref)


def put_halves(place, x_ref, mine_ref, theirs_ref):
    core, half = place[4], mine_ref.shape[1]
    mine_ref[0] = x_ref[rows_at(core, half), :].astype(BF16)
    theirs_ref[0] = x_ref[rows_at(1 - core, half), :].astype(BF16)


def take_halves(place, x_ref, halves):
    core, half = place[4], halves[0].shape[1]
    x_ref[rows_at(core, half), :] = halves[0][0].astype(F32)
    x_ref[rows_at(1 - core, half), :] = halves[1][0].astype(F32)


def over_images(left_ref, right_ref, rows=slice(None)):
    total = None
    for n in range(left_ref.shape[0]):
        term = dot(left_ref[n], right_ref[n, rows], NT)
        total = term if total is None else total + term
    return total


def feed_forward_grads(h_ref, hidden_ref, dffn_ref, dgu_ref, weight_ref, outs):
    units = hidden_ref.shape[1]
    grad_ref, ffn_ref = outs
    grad_ref[:, :units] = over_images(h_ref, dgu_ref, slice(0, units)).astype(BF16)
    grad_ref[:, units : 2 * units] = over_images(h_ref, dgu_ref, slice(units, 2 * units)).astype(BF16)
    grad_ref[:, 2 * units :] = over_images(dffn_ref, hidden_ref).astype(BF16)
    for n in range(h_ref.shape[0]):
        ffn_ref[n] = dot(weight_ref[...], hidden_ref[n], NN).astype(BF16)


def attention_backward(
    heads,
    place,
    image_weight,
    sums,
    mid_ref,
    attn_ref,
    cot_ref,
    mods_ref,
    raw_ref,
    lse_ref,
    gains_ref,
    tables_ref,
    weight_ref,
    outs,
    scratch,
):
    dmid_ref, dattn_ref, draw_ref, mine_ref, theirs_ref, dmods_ref, qgain_ref, kgain_ref = outs
    x_ref, y_ref = scratch
    quarter = attn_ref.shape[1]
    width = quarter
    size = gains_ref.shape[0]
    inverse = 1.0 / math.sqrt(size)
    mods = mods_ref[0].T
    take_halves(place, x_ref, sums)
    unit, scale = normed(mid_ref[0])
    y_ref[...] = unit
    own = rows_at(place[0], quarter)
    dh_own = x_ref[own, :]
    dmods_ref[0] = jnp.zeros(dmods_ref.shape[1:], F32)
    dmods_ref[0, 3:4, :] = row_sums(dh_own)
    dmods_ref[0, 4:5, :] = row_sums(dh_own * y_ref[own, :])
    weight = image_weight[pl.program_id(0)]
    dy = cot_ref[0].astype(F32) * weight
    dmid = dy + norm_back(x_ref[...] * (1.0 + mods[:, 4:5]), unit, scale)
    dmid_ref[0] = dmid
    x_ref[...] = dmid
    dmods_ref[0, 2:3, :] = row_sums(x_ref[own, :] * attn_ref[0])
    dattn = (mods[:, 2:3] * dmid).astype(BF16)
    dattn_ref[0] = dattn
    start = (3 * width) // LANES * LANES
    pad = 3 * width - start
    dob = dot(weight_ref[:, start:], dattn, TN)
    raw = raw_ref[0]
    gains, tables = gains_ref[...], tables_ref[...]
    cosine, up, down = tables[0], tables[1], tables[2]
    parts = [[], [], []]
    sums_of = [None, None]
    for head in range(heads):
        query, key, value = heads_of(raw, gains, tables, head)
        grad = dob[pad + head * size : pad + (head + 1) * size].astype(BF16)
        scores = dot(key[2], query[2], TN) * inverse
        probs = jnp.exp(scores - lse_ref[0, head : head + 1, :])
        dprobs = dot(value, grad, TN)
        parts[2].append(dot(grad, probs.astype(BF16), NT))
        dscores = probs * (dprobs - jnp.sum(probs * dprobs, axis=0, keepdims=True))
        dscores = dscores.astype(BF16)
        turned_grads = (
            dot(key[2], dscores, NN) * inverse,
            dot(query[2], dscores, NT) * inverse,
        )
        for part, (rot, (hat, rms, _)) in enumerate(zip(turned_grads, (query, key))):
            back = rot * cosine - turned(rot, up, down)
            term = back * hat
            sums_of[part] = term if sums_of[part] is None else sums_of[part] + term
            g = back * gains[:, part : part + 1]
            parts[part].append(rms * (g - hat * jnp.mean(g * hat, axis=0, keepdims=True)))
    qgain_ref[0] = jnp.broadcast_to(row_sums(sums_of[0]), qgain_ref.shape[1:])
    kgain_ref[0] = jnp.broadcast_to(row_sums(sums_of[1]), kgain_ref.shape[1:])
    span = round_up(3 * width, LANES)
    patches = raw.shape[1]
    tail = [jnp.zeros((span - 3 * width, patches), F32)] if span > 3 * width else []
    draw = jnp.concatenate(parts[0] + parts[1] + parts[2] + tail, axis=0).astype(BF16)
    draw_ref[0] = draw
    x_ref[...] = dot(weight_ref[:, :span], draw, NN)
    put_halves(place, x_ref, mine_ref, theirs_ref)


def attention_grads(place, h_ref, draw_ref, dattn_ref, ob_ref, outs, scratch):
    span = draw_ref.shape[1]
    (sum_ref,) = scratch
    start = sum_ref.shape[1] - ob_ref.shape[1]
    total = over_images(h_ref, draw_ref)
    out = over_images(dattn_ref, ob_ref)
    sum_ref[:, :start] = total[:, :start]
    sum_ref[:, start:span] = total[:, start:] + out[:, : span - start]
    sum_ref[:, span:] = out[:, span - start :]
    split_blocks(place, 5, sum_ref, outs)


def last_steps(
    place, image_weight, keep, sums, lat_ref, dmid_ref, mid_ref, cot_ref, mods_ref, ffn_ref,
    dmods_ref, outs, scratch
):
    out_ref, dlat_ref, dm_ref = outs
    x_ref, y_ref = scratch
    quarter = ffn_ref.shape[1]
    own = rows_at(place[0], quarter)
    mods = mods_ref[0].T
    take_halves(place, x_ref, sums)
    unit, scale = normed(lat_ref[0].astype(F32))
    y_ref[...] = unit
    dh_own = x_ref[own, :]
    dm_ref[0] = dmods_ref[0]
    dm_ref[0, 0:1, :] = row_sums(dh_own)
    dm_ref[0, 1:2, :] = row_sums(dh_own * y_ref[own, :])
    back = norm_back(x_ref[...] * (1.0 + mods[:, 1:2]), unit, scale)
    x_ref[...] = back
    dlat_ref[0] = (dmid_ref[0, own, :] + x_ref[own, :]).astype(BF16)
    n = pl.program_id(0)
    ffn = ffn_ref[0]
    dy = cot_ref[0, own, :].astype(F32) * image_weight[n]
    dm_ref[0, 5:6, :] = row_sums(dy * ffn)
    y_ref[...] = jnp.broadcast_to(mods[:, 5:6], y_ref.shape)
    out_ref[0] = ((mid_ref[0, own, :] + y_ref[own, :] * ffn) * keep[n]).astype(BF16)


def whole(array):
    return pl.BlockSpec(array.shape, lambda n: (0,) * array.ndim)


def last(array):
    width = array.shape[1] // 3
    return pl.BlockSpec((array.shape[0], width), lambda n: (0, 2))


def each(array):
    return pl.BlockSpec((1,) + array.shape[1:], lambda n: (n,) + (0,) * (array.ndim - 1))


def token(_):
    return pl.BlockSpec(memory_space=pl.ANY)


def scalars(_):
    return pl.BlockSpec(memory_space=pltpu.SMEM)


def call(body, groups, outs, scratch, images, flops=1):
    flat, specs, counts = [], [], []
    for group in groups:
        counts.append(len(group))
        for array, kind in group:
            flat.append(array)
            specs.append(kind(array))

    def kernel(*refs):
        at, lists = 0, []
        for count in counts:
            lists.append(list(refs[at : at + count]))
            at += count
        body(*lists, list(refs[at : at + len(outs)]), list(refs[at + len(outs) :]))

    moved = sum(a.size * a.dtype.itemsize for a in flat) if flops > 1 else 1
    return pl.pallas_call(
        kernel,
        grid=(images,),
        in_specs=specs,
        out_specs=[kind(o) for o, kind in outs],
        out_shape=[o for o, _ in outs],
        scratch_shapes=scratch,
        compiler_params=pltpu.CompilerParams(
            dimension_semantics=("arbitrary",), vmem_limit_bytes=VMEM_BYTES
        ),
        cost_estimate=pl.CostEstimate(flops=flops, bytes_accessed=moved, transcendentals=0),
    )(*flat)


def shaped(shape, dtype):
    return jax.ShapeDtypeStruct(shape, dtype)


def body(
    latents,
    condition,
    noise_bins,
    slot_valid,
    ada_weight,
    ada_bias,
    qkv_weight,
    query_gain,
    key_gain,
    out_weight,
    gate_up,
    down_weight,
    cotangent,
):
    images, patches, quarter = latents.shape
    width = condition.shape[1]
    rows = qkv_weight.shape[0]
    units = gate_up.shape[2]
    head_size = query_gain.shape[0]
    heads = quarter // head_size
    dp, mp = lax.axis_index("dp"), lax.axis_index("mp")
    core = mp % 2
    dp_size = lax.axis_size("dp")
    all_images = dp_size * images
    tokens = images * patches

    by_part = jnp.transpose(qkv_weight, (1, 0, 2))
    first_pack = jnp.concatenate([by_part[0], by_part[1], by_part[2], out_weight.T], axis=1)
    first = lax.all_gather(first_pack, "dp", axis=0, tiled=True)
    lat_pieces = mp_pieces(jnp.transpose(latents, (0, 2, 1)))
    cot_pieces = mp_pieces(jnp.transpose(cotangent, (0, 2, 1)))
    ada = jnp.transpose(ada_weight, (1, 0, 2))
    keep = slot_valid.astype(F32)
    given = noise_bins[0] >= 0
    on_line = dp_size == 8

    def over_dp():
        extra = jnp.stack([noise_bins, slot_valid], axis=1).astype(BF16)
        told = jnp.concatenate([condition, extra, jnp.zeros((images, LANES - 2), BF16)], axis=1)
        told = gather_rows(told, "dp")
        all_bins, all_valid = told[:, width].astype(F32), told[:, width + 1].astype(F32)
        cond_rows = lax.dynamic_slice_in_dim(told[:, :width], dp * rows, rows, 1).astype(F32)

        bin_ids = jnp.arange(BINS, dtype=F32)
        member = (all_bins[:, None] == bin_ids[None, :]).astype(F32) * all_valid[:, None]
        per_bin = jnp.sum(member, axis=0)
        own_bins = noise_bins.astype(F32)
        own_count = jnp.sum((own_bins[:, None] == bin_ids[None, :]) * per_bin[None, :], axis=1)
        image_weight = keep * jnp.sum(all_valid) / (BINS * jnp.maximum(own_count, 1.0))

        cond_act = jax.nn.silu(cond_rows).astype(BF16)
        mods_terms = jnp.einsum("nd,cde->nce", cond_act, ada, preferred_element_type=F32)
        mods_own = scatter_rows(mods_terms.reshape(all_images, -1), "dp")
        pack = packed(jnp.transpose(gate_up, (1, 0, 2)), down_weight.T, mods_own)
        mods_own = mods_own.reshape(images, 6, quarter) + ada_bias[None]
        mods_own = jnp.pad(mods_own, ((0, 0), (0, 2), (0, 0)))
        return cond_act, image_weight, mods_own, pack

    cond_act, image_weight, mods_own, second_pack = region(given, over_dp)
    hop_one = line_first(second_pack) if on_line else ()
    beside = [swap(second_pack, "dp", 1)] if on_line else []
    near = line_near(hop_one, beside[0]) if on_line else None
    beside += [swap(near, "dp", 1)] if on_line else []
    two = line_two(hop_one, beside[1]) if on_line else None
    held = [*beside, two] if on_line else []
    side = mp // 2
    far = swap(mods_own, "mp", 2)
    pair = jnp.stack([jnp.where(side == 0, mods_own, far), jnp.where(side == 0, far, mods_own)])
    other = swap(pair, "mp", 1)
    quad = jnp.stack([jnp.where(core == 0, pair, other), jnp.where(core == 0, other, pair)], axis=1)
    mods = jnp.transpose(quad, (2, 3, 0, 1, 4)).reshape(images, 8, width)

    count = dp_size if direct() else 1
    place = jnp.stack([mp, mp ^ 2, mp ^ 1, mp ^ 3, core] + [dp ^ k for k in range(count)])
    place = place.astype(jnp.int32)
    block_shape = (width // count,)
    gains = jnp.stack([query_gain, key_gain], axis=1)
    tables = jnp.asarray(rotary_tables(patches, head_size))
    full = 4 * quarter
    span = round_up(3 * quarter, LANES)
    start = 3 * quarter // LANES * LANES
    wide = lambda dtype: shaped((images, width, patches), dtype)
    half = shaped((images, width // 2, patches), BF16)
    tall = pltpu.VMEM((width, patches), F32)

    lat, h_one, raw, lse, ob, *attn_terms = call(
        lambda p, l, m, w, g, t, _, outs, s: attention_forward(
            heads, p[0], l, m[0], w[0], g[0], t[0], outs, s
        ),
        [
            [(place, scalars)],
            [(a, each) for a in lat_pieces],
            [(mods, each)],
            [(first, whole)],
            [(gains, whole)],
            [(tables, whole)],
            [(a, token) for a in held],
        ],
        [
            (wide(BF16), each),
            (wide(BF16), each),
            (shaped((images, 3 * quarter, patches), F32), each),
            (shaped((images, heads, patches), F32), each),
            (shaped((images, full - start, patches), BF16), each),
            (half, each),
            (half, each),
        ],
        [tall],
        images,
    )
    if on_line:
        blocks, block_owners = line_rest(second_pack, beside, hop_one, near, two)
        attn_chip = mp_chip(*attn_terms, blocks[6])

        def assemble(p, blocks, outs, _):
            copy_blocks(p[0], 0, blocks, outs[0])

        (second,) = call(
            assemble,
            [
                [(jnp.stack(block_owners).astype(jnp.int32), scalars)],
                [(a, whole) for a in blocks],
            ],
            [(shaped((width, 3 * units), BF16), whole)],
            [],
            1,
        )
        attn_sums = mp_join(attn_chip, swap(attn_chip, "mp", 2), blocks[7])
    else:
        second = lax.all_gather(second_pack, "dp", axis=0, tiled=True)
        attn_sums = mp_total(*attn_terms)

    def middle():
        mid, attn_own, h_two, hidden, dffn, dgu, cot, mine, theirs = call(
            lambda p, w, l, s, m, c, k, outs, x: feed_forward(
                p[0], w[0], l[0], s, m[0], c, k[0], outs, x
            ),
            [
                [(place, scalars)],
                [(image_weight, scalars)],
                [(lat, each)],
                [(a, each) for a in attn_sums],
                [(mods, each)],
                [(a, each) for a in cot_pieces],
                [(second, whole)],
            ],
            [
                (wide(F32), each),
                (shaped((images, quarter, patches), F32), each),
                (wide(BF16), each),
                (shaped((images, units, patches), BF16), each),
                (wide(BF16), each),
                (shaped((images, 2 * units, patches), BF16), each),
                (wide(BF16), each),
                (half, each),
                (half, each),
            ],
            [tall],
            images,
        )
        chip = mp_chip(mine, theirs)
        grads = call(
            lambda a, outs, x: feed_forward_grads(*a, outs),
            [[(h_two, whole), (hidden, whole), (dffn, whole), (dgu, whole), (second, last)]],
            [(shaped((width, 3 * units), BF16), whole), (wide(BF16), whole)],
            [],
            1,
        )
        return mid, attn_own, cot, chip, swap(chip, "mp", 2), grads

    mid, attn_own, cot, dh_two_chip, dh_two_far, grads = region(given, middle)
    second_terms, ffn_part = grads
    second_sum = lax.psum_scatter(second_terms, "dp", scatter_dimension=0, tiled=True)

    def backward():
        dh_two_sums = mp_join(dh_two_chip, dh_two_far)
        dmid, dattn, draw, mine, theirs, dmods_part, qgain, kgain = call(
            lambda p, w, s, a, outs, x: attention_backward(heads, p[0], w[0], s, *a, outs, x),
            [
                [(place, scalars)],
                [(image_weight, scalars)],
                [(a, each) for a in dh_two_sums],
                [
                    (mid, each),
                    (attn_own, each),
                    (cot, each),
                    (mods, each),
                    (raw, each),
                    (lse, each),
                    (gains, whole),
                    (tables, whole),
                    (first, whole),
                ],
            ],
            [
                (wide(F32), each),
                (wide(BF16), each),
                (shaped((images, span, patches), BF16), each),
                (half, each),
                (half, each),
                (shaped((images, 8, quarter), F32), each),
                (shaped((images, 8, head_size), F32), each),
                (shaped((images, 8, head_size), F32), each),
            ],
            [tall, tall],
            images,
        )
        first_terms = call(
            lambda p, a, outs, x: attention_grads(p[0], *a, outs, x),
            [
                [(place, scalars)],
                [(h_one, whole), (draw, whole), (dattn, whole), (ob, whole)],
            ],
            [(shaped(block_shape + (full,), BF16), whole)] * count,
            [pltpu.VMEM((width, full), F32)],
            1,
        )
        ffn_own = mp_quarter(ffn_part)
        first_beside = dp_cross(first_terms)
        dh_one_sums = mp_total(mine, theirs, tuple(first_terms))
        block_out, latent_grad, dmods = call(
            lambda p, w, k, s, a, _, outs, x: last_steps(p[0], w[0], k[0], s, *a, outs, x),
            [
                [(place, scalars)],
                [(image_weight, scalars)],
                [(keep, scalars)],
                [(a, each) for a in dh_one_sums],
                [
                    (lat, each),
                    (dmid, each),
                    (mid, each),
                    (cot, each),
                    (mods, each),
                    (ffn_own, each),
                    (dmods_part, each),
                ],
                [(a, token) for a in first_beside[3:]],
            ],
            [
                (shaped((images, quarter, patches), BF16), each),
                (shaped((images, quarter, patches), BF16), each),
                (shaped((images, 8, quarter), F32), each),
            ],
            [tall, tall],
            images,
        )

        gain_terms = jnp.concatenate([jnp.sum(qgain[:, 0], axis=0), jnp.sum(kgain[:, 0], axis=0)])
        high = gain_terms.astype(BF16)
        low = (gain_terms - high.astype(F32)).astype(BF16)
        beside = jnp.concatenate([high, low])[None]
        beside = jnp.concatenate([beside, jnp.zeros((images - 1, beside.shape[1]), BF16)], axis=0)
        rounded = dmods[:, :6].astype(BF16).reshape(images, 6 * quarter)
        rounded = after(jnp.concatenate([rounded, beside], axis=1), *first_beside[2:3])
        told_back = gather_rows(rounded, "dp")
        halves = dp_pair_sums(first_terms, first_beside) if count > 1 else []
        return block_out, latent_grad, told_back, first_terms[0], first_beside[0], halves

    block_out, latent_grad, told_back, first_own, first_beside, halves = region(given, backward)
    first_far = dp_lines(halves)

    def modulation_grads():
        dmods_all = told_back[:, : 6 * quarter].reshape(all_images, 6, quarter)
        gain_sum = jnp.sum(told_back[:, 6 * quarter :].astype(F32), axis=0)
        gain_sum = gain_sum[: 2 * head_size] + gain_sum[2 * head_size :]
        ada_grad = jnp.einsum("nd,nce->cde", cond_act, dmods_all, preferred_element_type=F32)
        bias_grad = jnp.sum(dmods_all.astype(F32), axis=0)
        cond_terms = jnp.einsum("nce,cde->nd", dmods_all, ada, preferred_element_type=F32)
        both = mp_sum_small(jnp.concatenate([cond_terms.reshape(-1), gain_sum]))
        gain_sum = both[cond_terms.size :]
        cond_sum = rows_to_columns(both[: cond_terms.size].reshape(cond_terms.shape), "dp")
        return ada_grad, bias_grad, gain_sum, cond_sum

    ada_grad, bias_grad, gain_sum, cond_sum = region(given, modulation_grads)
    first_sum = first_beside.astype(F32)
    if count > 1:
        first_sum = first_sum + first_own.astype(F32)
    for line in first_far:
        first_sum = first_sum + line.astype(F32)
    cond_own = condition.astype(F32)
    sig = jax.nn.sigmoid(cond_own)
    condition_grad = (cond_sum * sig * (1.0 + cond_own * (1.0 - sig))).astype(BF16)
    second_sum = second_sum.astype(F32)
    gateup_grad = jnp.stack([second_sum[:, :units], second_sum[:, units : 2 * units]], axis=1)
    down_grad = second_sum[:, 2 * units :].T
    qkv_grad = first_sum[:, : 3 * quarter].reshape(rows, 3, quarter)
    out_grad = first_sum[:, 3 * quarter :].T
    return (
        jnp.transpose(block_out, (0, 2, 1)),
        jnp.transpose(latent_grad, (0, 2, 1)),
        condition_grad,
        jnp.transpose(ada_grad, (1, 0, 2)),
        bias_grad,
        qkv_grad,
        gain_sum[:head_size],
        gain_sum[head_size:],
        out_grad,
        gateup_grad,
        down_grad,
    )


def solution(mesh):
    placed = (
        P("dp", None, "mp"),
        P("dp", None),
        P("dp"),
        P("dp"),
        P("dp", None, "mp"),
        P(None, "mp"),
        P("dp", None, "mp"),
        P(),
        P(),
        P("mp", "dp"),
        P("dp", None, "mp"),
        P("mp", "dp"),
        P("dp", None, "mp"),
    )
    return jax.shard_map(
        body,
        mesh=mesh,
        in_specs=placed,
        out_specs=(
            P("dp", None, "mp"),
            P("dp", None, "mp"),
            P("dp", None),
            P("dp", None, "mp"),
            P(None, "mp"),
            P("dp", None, "mp"),
            P(),
            P(),
            P("mp", "dp"),
            P("dp", None, "mp"),
            P("mp", "dp"),
        ),
        check_vma=False,
    )
```

```python
import functools
import math

import jax
import jax.numpy as jnp
import numpy as np
from jax import lax
from jax.experimental import pallas as pl
from jax.experimental.pallas import tpu as pltpu
from jax.sharding import PartitionSpec as P

GRID = 16
BINS = 8
EPS = 1e-06
F32 = jnp.float32
BF16 = jnp.bfloat16
VMEM_BYTES = 56 * 1024 * 1024
LANES = 128
NT = (((1,), (1,)), ((), ()))
NN = (((1,), (0,)), ((), ()))
TN = (((0,), (0,)), ((), ()))


def dot(left, right, dims):
    return lax.dot_general(left, right, dims, preferred_element_type=F32)


def swap(value, axis, bit):
    size = lax.axis_size(axis)
    return lax.ppermute(value, axis, [(i, i ^ bit) for i in range(size)])


def round_up(value, unit):
    return -(-value // unit) * unit


def region(given, work):
    shapes = jax.eval_shape(work)
    return lax.cond(given, work, lambda: jax.tree.map(lambda a: jnp.zeros(a.shape, a.dtype), shapes))


def ordered(bit, mine, other, axis):
    first = jnp.where(bit == 0, mine, other)
    second = jnp.where(bit == 0, other, mine)
    return jnp.concatenate([first, second], axis=axis)


def gather_rows(value, axis):
    size, me = lax.axis_size(axis), lax.axis_index(axis)
    steps = [1 << k for k in range(size.bit_length() - 1)]
    shape = value.shape
    steps = steps[1:] + steps[:1]
    for step in steps:
        value = ordered((me // step) % 2, value[None], swap(value, axis, step)[None], 0)
    count = len(steps)
    order = sorted(range(count), key=lambda k: -steps[count - 1 - k])
    value = jnp.transpose(value, order + [count, count + 1])
    return value.reshape((size * shape[0],) + shape[1:])


def scatter_rows(value, axis):
    size, me = lax.axis_size(axis), lax.axis_index(axis)
    step = size // 2
    while step >= 1:
        half = value.shape[0] // 2
        bit = (me // step) % 2
        keep = jnp.where(bit == 0, value[:half], value[half:])
        send = jnp.where(bit == 0, value[half:], value[:half])
        value = keep + swap(send, axis, step)
        step //= 2
    return value


def rows_to_columns(value, axis):
    size, me = lax.axis_size(axis), lax.axis_index(axis)
    step = 1
    while step < size:
        rows, cols = value.shape
        bit = (me // step) % 2
        per = rows // (size // step)
        split = value.reshape(size // step // 2, 2, per, cols)
        keep = jnp.where(bit == 0, split[:, 0], split[:, 1]).reshape(rows // 2, cols)
        send = jnp.where(bit == 0, split[:, 1], split[:, 0]).reshape(rows // 2, cols)
        value = ordered(bit, keep, swap(send, axis, step), 1)
        step *= 2
    return value


def mp_sum_small(value):
    step = lax.axis_size("mp") // 2
    while step >= 1:
        value = value + swap(value, "mp", step)
        step //= 2
    return value


def mp_pieces(value):
    far = swap(value, "mp", 2)
    near = swap(value, "mp", 1)
    both = swap(far, "mp", 1)
    return [value, far, near, both]


def mp_chip(mine, theirs, *tokens):
    return add_blocks(mine, swap(theirs, "mp", 1), *tokens)


def mp_join(chip, far, *tokens):
    half = add_blocks(chip, far, *tokens)
    return half, swap(half, "mp", 1)


def mp_total(mine, theirs, tokens=()):
    chip = mp_chip(mine, theirs)
    return mp_join(chip, swap(chip, "mp", 2), *tokens)


def mp_quarter(partial):
    images, width, patches = partial.shape
    quarter = width // 4
    me = lax.axis_index("mp")
    core, side = me % 2, me // 2
    split = partial.reshape(images, 2, 2, quarter, patches)
    send = jnp.where(core == 0, split[:, :, 1], split[:, :, 0])
    keep = jnp.where(core == 0, split[:, :, 0], split[:, :, 1])
    chip = keep.astype(F32) + swap(send, "mp", 1).astype(F32)
    send = jnp.where(side == 0, chip[:, 1], chip[:, 0]).astype(BF16)
    keep = jnp.where(side == 0, chip[:, 0], chip[:, 1])
    return keep + swap(send, "mp", 2).astype(F32)


def direct():
    return lax.axis_size("dp") in (2, 4, 8)


def along(value, pairs):
    return lax.ppermute(value, "dp", [(2 * a + y, 2 * b + y) for a, b in pairs for y in (0, 1)])


def line_first(block):
    up = along(block, [(0, 1), (1, 2), (2, 3)])
    return up, along(block, [(1, 0), (2, 1), (3, 2)])


def line_near(first, token):
    return pick(lax.axis_index("dp") // 2 % 2 == 1, first[0], first[1], token)


def line_second(first):
    return along(first[0], [(1, 2), (2, 3)]), along(first[1], [(1, 0), (2, 1)])


def line_two(first, token):
    second = line_second(first)
    return pick(lax.axis_index("dp") // 2 >= 2, second[0], second[1], token)


def line_rest(block, beside, first, one, two):
    me = lax.axis_index("dp")
    at = me // 2
    end = along(two, [(1, 0), (2, 3)])
    three = jnp.where(at == 0, end, jnp.where(at == 1, first[1], jnp.where(at == 2, first[0], end)))
    found = [block, one, two, three]
    places = [at, at ^ 1, jnp.where(at >= 2, at - 2, at + 2), 3 - at]
    blocks = found + beside + [swap(b, "dp", 1) for b in found[2:]]
    return blocks, [2 * p + me % 2 for p in places] + [2 * p + 1 - me % 2 for p in places]


def pick(flag, left, right, token):
    def kernel(flag_ref, left_ref, right_ref, _, out_ref):
        @pl.when(flag_ref[0] == 1)
        def _():
            out_ref[...] = left_ref[...]

        @pl.when(flag_ref[0] == 0)
        def _():
            out_ref[...] = right_ref[...]

    return pl.pallas_call(
        kernel,
        in_specs=[pl.BlockSpec(memory_space=pltpu.SMEM)]
        + [pl.BlockSpec(memory_space=pltpu.VMEM)] * 2
        + [pl.BlockSpec(memory_space=pl.ANY)],
        out_specs=pl.BlockSpec(memory_space=pltpu.VMEM),
        out_shape=shaped(left.shape, left.dtype),
        cost_estimate=pl.CostEstimate(flops=1, bytes_accessed=1, transcendentals=0),
    )(jnp.reshape(flag.astype(jnp.int32), (1,)), left, right, token)


def unpacked(terms, quarter):
    rows = terms[0].shape[0]

    def kernel(*refs):
        qkv_ref, out_ref = refs[-2:]
        total = refs[0][...].astype(F32)
        for ref in refs[1:-2]:
            total = total + ref[...].astype(F32)
        for part in range(3):
            qkv_ref[part] = total[:, part * quarter : (part + 1) * quarter]
        out_ref[...] = total[:, 3 * quarter :]

    return pl.pallas_call(
        kernel,
        out_shape=[shaped((3, rows, quarter), F32), shaped((rows, quarter), F32)],
        compiler_params=pltpu.CompilerParams(vmem_limit_bytes=VMEM_BYTES),
        cost_estimate=pl.CostEstimate(flops=1, bytes_accessed=1, transcendentals=0),
    )(*terms)


def packed(gate_up, down, token):
    rows, units = down.shape

    def kernel(gate_up_ref, down_ref, _, out_ref):
        out_ref[:, :units] = gate_up_ref[0]
        out_ref[:, units : 2 * units] = gate_up_ref[1]
        out_ref[:, 2 * units :] = down_ref[...]

    return pl.pallas_call(
        kernel,
        in_specs=[pl.BlockSpec(memory_space=pltpu.VMEM)] * 2 + [pl.BlockSpec(memory_space=pl.ANY)],
        out_specs=pl.BlockSpec(memory_space=pltpu.VMEM),
        out_shape=shaped((rows, 3 * units), down.dtype),
        cost_estimate=pl.CostEstimate(flops=1, bytes_accessed=1, transcendentals=0),
    )(gate_up, down, token)


def dp_cross(parts):
    if len(parts) == 1:
        return [lax.psum_scatter(parts[0], "dp", scatter_dimension=0, tiled=True)]
    return [None] + [swap(parts[k + 1], "dp", 1) for k in range(2, len(parts), 2)]


def dp_pair_sums(parts, cross, *tokens):
    return [add_blocks(parts[2 * k], cross[k], *tokens) for k in range(1, len(cross))]


def dp_lines(halves):
    return [swap(half, "dp", 2 * k + 2) for k, half in enumerate(halves)]


def add_blocks(left, right, *tokens):
    def kernel(*refs):
        refs[-1][...] = (refs[0][...].astype(F32) + refs[1][...].astype(F32)).astype(BF16)

    return pl.pallas_call(
        kernel,
        in_specs=[pl.BlockSpec(memory_space=pltpu.VMEM)] * 2
        + [pl.BlockSpec(memory_space=pl.ANY)] * len(tokens),
        out_specs=pl.BlockSpec(memory_space=pltpu.VMEM),
        out_shape=shaped(left.shape, BF16),
        compiler_params=pltpu.CompilerParams(vmem_limit_bytes=VMEM_BYTES),
        cost_estimate=pl.CostEstimate(flops=1, bytes_accessed=1, transcendentals=0),
    )(left, right, *tokens)


def after(value, *others):
    if not others:
        return value

    def kernel(*refs):
        refs[-1][...] = refs[0][...]

    return pl.pallas_call(
        kernel,
        in_specs=[pl.BlockSpec(memory_space=pltpu.VMEM)]
        + [pl.BlockSpec(memory_space=pl.ANY)] * len(others),
        out_specs=pl.BlockSpec(memory_space=pltpu.VMEM),
        out_shape=shaped(value.shape, value.dtype),
        cost_estimate=pl.CostEstimate(flops=1, bytes_accessed=1, transcendentals=0),
    )(value, *others)


def copy_blocks(place, first, blocks, whole_ref):
    for k, ref in enumerate(blocks):
        if len(blocks) == 1:
            whole_ref[...] = ref[...]
        else:
            whole_ref[rows_at(place[first + k], ref.shape[0]), :] = ref[...]


def split_blocks(place, first, sum_ref, outs):
    for k, ref in enumerate(outs):
        if len(outs) == 1:
            ref[...] = sum_ref[...].astype(BF16)
        else:
            ref[...] = sum_ref[rows_at(place[first + k], ref.shape[0]), :].astype(BF16)


def rotary_tables(patches, head_size):
    pairs = head_size // 4
    freqs = 10000.0 ** (-np.arange(pairs, dtype=np.float64) / pairs)
    spots = np.arange(patches)
    row = (spots // GRID)[None, :] * freqs[:, None]
    col = (spots % GRID)[None, :] * freqs[:, None]
    angles = np.concatenate([row, row, col, col], axis=0)
    cosine, sine = np.cos(angles), np.sin(angles)
    first = (np.arange(head_size) // pairs % 2 == 0)[:, None]
    up = np.where(first, -sine, 0.0)
    down = np.where(first, 0.0, sine)
    return np.stack([cosine, up, down]).astype(np.float32)


def turned(value, up, down):
    height = value.shape[0]
    pairs = height // 4
    return pltpu.roll(value, height - pairs, 0) * up + pltpu.roll(value, pairs, 0) * down


def normed(value):
    centred = value - jnp.mean(value, axis=0, keepdims=True)
    scale = lax.rsqrt(jnp.mean(centred * centred, axis=0, keepdims=True) + EPS)
    return centred * scale, scale


def norm_back(grad, unit, scale):
    return scale * (
        grad
        - jnp.mean(grad, axis=0, keepdims=True)
        - unit * jnp.mean(grad * unit, axis=0, keepdims=True)
    )


def row_sums(value):
    ones = jnp.ones((8, value.shape[1]), F32)
    return lax.dot_general(
        ones, value, NT, precision=lax.Precision.HIGHEST, preferred_element_type=F32
    )[0:1]


def rows_at(index, size):
    return pl.ds(pl.multiple_of(index * size, 16), size)


def heads_of(raw, gains, tables, head):
    size = gains.shape[0]
    width = raw.shape[0] // 3
    cosine, up, down = tables[0], tables[1], tables[2]
    found = []
    for part in range(2):
        rows = raw[part * width + head * size : part * width + (head + 1) * size]
        scale = lax.rsqrt(jnp.mean(rows * rows, axis=0, keepdims=True) + EPS)
        hat = rows * scale
        gained = hat * gains[:, part : part + 1]
        rotated = gained * cosine + turned(gained, up, down)
        found.append((hat, scale, rotated.astype(BF16)))
    value = raw[2 * width + head * size : 2 * width + (head + 1) * size].astype(BF16)
    return found[0], found[1], value


def attention_forward(
    heads, place, lat_refs, mods_ref, weight_ref, gains_ref, tables_ref, outs, scratch
):
    lat_ref, h_ref, raw_ref, lse_ref, ob_ref, mine_ref, theirs_ref = outs
    (x_ref,) = scratch
    quarter = lat_refs[0].shape[1]
    width = quarter
    size = gains_ref.shape[0]
    inverse = 1.0 / math.sqrt(size)

    for k, ref in enumerate(lat_refs):
        piece = ref[0]
        lat_ref[0, rows_at(place[k], quarter), :] = piece
        x_ref[rows_at(place[k], quarter), :] = piece.astype(F32)
    mods = mods_ref[0].T
    unit, _ = normed(x_ref[...])
    h = (unit * (1.0 + mods[:, 1:2]) + mods[:, 0:1]).astype(BF16)
    h_ref[0] = h
    span = round_up(3 * width, LANES)
    raw = dot(weight_ref[:, :span], h, TN)[: 3 * width]
    raw_ref[0] = raw
    gains, tables = gains_ref[...], tables_ref[...]
    pad = 4 * width - (3 * width) // LANES * LANES - width
    parts, tops = [], []
    for head in range(heads):
        (_, _, query), (_, _, key), value = heads_of(raw, gains, tables, head)
        scores = dot(key, query, TN) * inverse
        top = jnp.max(scores, axis=0, keepdims=True)
        expo = jnp.exp(scores - top)
        total = jnp.sum(expo, axis=0, keepdims=True)
        probs = (expo / total).astype(BF16)
        parts.append(dot(value, probs, NN))
        tops.append(top + jnp.log(total))
    lse_ref[0] = jnp.concatenate(tops, axis=0)
    patches = raw.shape[1]
    ob = jnp.concatenate([jnp.zeros((pad, patches), F32)] + parts, axis=0).astype(BF16)
    ob_ref[0] = ob
    x_ref[...] = dot(weight_ref[:, 4 * width - width - pad :], ob, NN)
    put_halves(place, x_ref, mine_ref, theirs_ref)


def feed_forward(
    place, image_weight, lat_ref, sums, mods_ref, cot_refs, weight_ref, outs, scratch
):
    mid_ref, attn_ref, h_ref, hidden_ref, dffn_ref, dgu_ref, cot_ref, mine_ref, theirs_ref = outs
    (x_ref,) = scratch
    quarter = cot_refs[0].shape[1]
    units = hidden_ref.shape[1]
    mods = mods_ref[0].T
    take_halves(place, x_ref, sums)
    attn_ref[0] = x_ref[rows_at(place[0], quarter), :]
    mid = lat_ref[0].astype(F32) + mods[:, 2:3] * x_ref[...]
    mid_ref[0] = mid
    unit, _ = normed(mid)
    h = (unit * (1.0 + mods[:, 4:5]) + mods[:, 3:4]).astype(BF16)
    h_ref[0] = h
    for k, ref in enumerate(cot_refs):
        piece = ref[0]
        cot_ref[0, rows_at(place[k], quarter), :] = piece
    weight = image_weight[pl.program_id(0)]
    dffn = (mods[:, 5:6] * (cot_ref[0].astype(F32) * weight)).astype(BF16)
    dffn_ref[0] = dffn
    gate = dot(weight_ref[:, :units], h, TN)
    up = dot(weight_ref[:, units : 2 * units], h, TN)
    sig = jax.nn.sigmoid(gate)
    swish = gate * sig
    hidden_ref[0] = (swish * up).astype(BF16)
    dhidden = dot(weight_ref[:, 2 * units :], dffn, TN)
    dgu_ref[0, :units] = (dhidden * up * sig * (1.0 + gate * (1.0 - sig))).astype(BF16)
    dgu_ref[0, units:] = (dhidden * swish).astype(BF16)
    x_ref[...] = dot(weight_ref[:, : 2 * units], dgu_ref[0], NN)
    put_halves(place, x_ref, mine_ref, theirs_ref)


def put_halves(place, x_ref, mine_ref, theirs_ref):
    core, half = place[4], mine_ref.shape[1]
    mine_ref[0] = x_ref[rows_at(core, half), :].astype(BF16)
    theirs_ref[0] = x_ref[rows_at(1 - core, half), :].astype(BF16)


def take_halves(place, x_ref, halves):
    core, half = place[4], halves[0].shape[1]
    x_ref[rows_at(core, half), :] = halves[0][0].astype(F32)
    x_ref[rows_at(1 - core, half), :] = halves[1][0].astype(F32)


def over_images(left_ref, right_ref, rows=slice(None)):
    total = None
    for n in range(left_ref.shape[0]):
        term = dot(left_ref[n], right_ref[n, rows], NT)
        total = term if total is None else total + term
    return total


def feed_forward_grads(h_ref, hidden_ref, dffn_ref, dgu_ref, outs):
    units = hidden_ref.shape[1]
    (grad_ref,) = outs
    grad_ref[:, :units] = over_images(h_ref, dgu_ref, slice(0, units)).astype(BF16)
    grad_ref[:, units : 2 * units] = over_images(h_ref, dgu_ref, slice(units, 2 * units)).astype(BF16)
    grad_ref[:, 2 * units :] = over_images(dffn_ref, hidden_ref).astype(BF16)


def feed_forward_end(hidden_ref, weight_ref, ffn_ref):
    for n in range(hidden_ref.shape[0]):
        ffn_ref[n] = dot(weight_ref[...], hidden_ref[n], NN).astype(BF16)


def attention_backward(
    heads,
    place,
    image_weight,
    sums,
    mid_ref,
    attn_ref,
    cot_ref,
    mods_ref,
    raw_ref,
    lse_ref,
    gains_ref,
    tables_ref,
    weight_ref,
    outs,
    scratch,
):
    dmid_ref, dattn_ref, draw_ref, mine_ref, theirs_ref, dmods_ref, qgain_ref, kgain_ref = outs
    x_ref, y_ref = scratch
    quarter = attn_ref.shape[1]
    width = quarter
    size = gains_ref.shape[0]
    inverse = 1.0 / math.sqrt(size)
    mods = mods_ref[0].T
    take_halves(place, x_ref, sums)
    unit, scale = normed(mid_ref[0])
    y_ref[...] = unit
    own = rows_at(place[0], quarter)
    dh_own = x_ref[own, :]
    dmods_ref[0] = jnp.zeros(dmods_ref.shape[1:], F32)
    dmods_ref[0, 3:4, :] = row_sums(dh_own)
    dmods_ref[0, 4:5, :] = row_sums(dh_own * y_ref[own, :])
    weight = image_weight[pl.program_id(0)]
    dy = cot_ref[0].astype(F32) * weight
    dmid = dy + norm_back(x_ref[...] * (1.0 + mods[:, 4:5]), unit, scale)
    dmid_ref[0] = dmid
    x_ref[...] = dmid
    dmods_ref[0, 2:3, :] = row_sums(x_ref[own, :] * attn_ref[0])
    dattn = (mods[:, 2:3] * dmid).astype(BF16)
    dattn_ref[0] = dattn
    start = (3 * width) // LANES * LANES
    pad = 3 * width - start
    dob = dot(weight_ref[:, start:], dattn, TN)
    raw = raw_ref[0]
    gains, tables = gains_ref[...], tables_ref[...]
    cosine, up, down = tables[0], tables[1], tables[2]
    parts = [[], [], []]
    sums_of = [None, None]
    for head in range(heads):
        query, key, value = heads_of(raw, gains, tables, head)
        grad = dob[pad + head * size : pad + (head + 1) * size].astype(BF16)
        scores = dot(key[2], query[2], TN) * inverse
        probs = jnp.exp(scores - lse_ref[0, head : head + 1, :])
        dprobs = dot(value, grad, TN)
        parts[2].append(dot(grad, probs.astype(BF16), NT))
        dscores = probs * (dprobs - jnp.sum(probs * dprobs, axis=0, keepdims=True))
        dscores = dscores.astype(BF16)
        turned_grads = (
            dot(key[2], dscores, NN) * inverse,
            dot(query[2], dscores, NT) * inverse,
        )
        for part, (rot, (hat, rms, _)) in enumerate(zip(turned_grads, (query, key))):
            back = rot * cosine - turned(rot, up, down)
            term = back * hat
            sums_of[part] = term if sums_of[part] is None else sums_of[part] + term
            g = back * gains[:, part : part + 1]
            parts[part].append(rms * (g - hat * jnp.mean(g * hat, axis=0, keepdims=True)))
    qgain_ref[0] = jnp.broadcast_to(row_sums(sums_of[0]), qgain_ref.shape[1:])
    kgain_ref[0] = jnp.broadcast_to(row_sums(sums_of[1]), kgain_ref.shape[1:])
    span = round_up(3 * width, LANES)
    patches = raw.shape[1]
    tail = [jnp.zeros((span - 3 * width, patches), F32)] if span > 3 * width else []
    draw = jnp.concatenate(parts[0] + parts[1] + parts[2] + tail, axis=0).astype(BF16)
    draw_ref[0] = draw
    x_ref[...] = dot(weight_ref[:, :span], draw, NN)
    put_halves(place, x_ref, mine_ref, theirs_ref)


def attention_grads(place, h_ref, draw_ref, dattn_ref, ob_ref, outs, scratch):
    span = draw_ref.shape[1]
    (sum_ref,) = scratch
    start = sum_ref.shape[1] - ob_ref.shape[1]
    total = over_images(h_ref, draw_ref)
    out = over_images(dattn_ref, ob_ref)
    sum_ref[:, :start] = total[:, :start]
    sum_ref[:, start:span] = total[:, start:] + out[:, : span - start]
    sum_ref[:, span:] = out[:, span - start :]
    split_blocks(place, 5, sum_ref, outs)


def last_steps(
    place, image_weight, keep, sums, lat_ref, dmid_ref, mid_ref, cot_ref, mods_ref, ffn_ref,
    dmods_ref, outs, scratch
):
    out_ref, dlat_ref, dm_ref = outs
    x_ref, y_ref = scratch
    quarter = ffn_ref.shape[1]
    own = rows_at(place[0], quarter)
    mods = mods_ref[0].T
    take_halves(place, x_ref, sums)
    unit, scale = normed(lat_ref[0].astype(F32))
    y_ref[...] = unit
    dh_own = x_ref[own, :]
    dm_ref[0] = dmods_ref[0]
    dm_ref[0, 0:1, :] = row_sums(dh_own)
    dm_ref[0, 1:2, :] = row_sums(dh_own * y_ref[own, :])
    back = norm_back(x_ref[...] * (1.0 + mods[:, 1:2]), unit, scale)
    x_ref[...] = back
    dlat_ref[0] = (dmid_ref[0, own, :] + x_ref[own, :]).astype(BF16)
    n = pl.program_id(0)
    ffn = ffn_ref[0]
    dy = cot_ref[0, own, :].astype(F32) * image_weight[n]
    dm_ref[0, 5:6, :] = row_sums(dy * ffn)
    y_ref[...] = jnp.broadcast_to(mods[:, 5:6], y_ref.shape)
    out_ref[0] = ((mid_ref[0, own, :] + y_ref[own, :] * ffn) * keep[n]).astype(BF16)


def whole(array):
    return pl.BlockSpec(array.shape, lambda n: (0,) * array.ndim)


def last(array):
    width = array.shape[1] // 3
    return pl.BlockSpec((array.shape[0], width), lambda n: (0, 2))


def each(array):
    return pl.BlockSpec((1,) + array.shape[1:], lambda n: (n,) + (0,) * (array.ndim - 1))


def token(_):
    return pl.BlockSpec(memory_space=pl.ANY)


def scalars(_):
    return pl.BlockSpec(memory_space=pltpu.SMEM)


def call(body, groups, outs, scratch, images, flops=1):
    flat, specs, counts = [], [], []
    for group in groups:
        counts.append(len(group))
        for array, kind in group:
            flat.append(array)
            specs.append(kind(array))

    def kernel(*refs):
        at, lists = 0, []
        for count in counts:
            lists.append(list(refs[at : at + count]))
            at += count
        body(*lists, list(refs[at : at + len(outs)]), list(refs[at + len(outs) :]))

    moved = sum(a.size * a.dtype.itemsize for a in flat) if flops > 1 else 1
    return pl.pallas_call(
        kernel,
        grid=(images,),
        in_specs=specs,
        out_specs=[kind(o) for o, kind in outs],
        out_shape=[o for o, _ in outs],
        scratch_shapes=scratch,
        compiler_params=pltpu.CompilerParams(
            dimension_semantics=("arbitrary",), vmem_limit_bytes=VMEM_BYTES
        ),
        cost_estimate=pl.CostEstimate(flops=flops, bytes_accessed=moved, transcendentals=0),
    )(*flat)


def shaped(shape, dtype):
    return jax.ShapeDtypeStruct(shape, dtype)


def body(
    latents,
    condition,
    noise_bins,
    slot_valid,
    ada_weight,
    ada_bias,
    qkv_weight,
    query_gain,
    key_gain,
    out_weight,
    gate_up,
    down_weight,
    cotangent,
):
    images, patches, quarter = latents.shape
    width = condition.shape[1]
    rows = qkv_weight.shape[0]
    units = gate_up.shape[2]
    head_size = query_gain.shape[0]
    heads = quarter // head_size
    dp, mp = lax.axis_index("dp"), lax.axis_index("mp")
    core = mp % 2
    dp_size = lax.axis_size("dp")
    all_images = dp_size * images
    tokens = images * patches

    by_part = jnp.transpose(qkv_weight, (1, 0, 2))
    first_pack = jnp.concatenate([by_part[0], by_part[1], by_part[2], out_weight.T], axis=1)
    first = lax.all_gather(first_pack, "dp", axis=0, tiled=True)
    lat_pieces = mp_pieces(jnp.transpose(latents, (0, 2, 1)))
    cot_pieces = mp_pieces(jnp.transpose(cotangent, (0, 2, 1)))
    ada = jnp.transpose(ada_weight, (1, 0, 2))
    keep = slot_valid.astype(F32)
    given = noise_bins[0] >= 0
    on_line = dp_size == 8

    def over_dp():
        extra = jnp.stack([noise_bins, slot_valid], axis=1).astype(BF16)
        told = jnp.concatenate([condition, extra, jnp.zeros((images, LANES - 2), BF16)], axis=1)
        told = gather_rows(told, "dp")
        all_bins, all_valid = told[:, width].astype(F32), told[:, width + 1].astype(F32)
        cond_rows = lax.dynamic_slice_in_dim(told[:, :width], dp * rows, rows, 1).astype(F32)

        bin_ids = jnp.arange(BINS, dtype=F32)
        member = (all_bins[:, None] == bin_ids[None, :]).astype(F32) * all_valid[:, None]
        per_bin = jnp.sum(member, axis=0)
        own_bins = noise_bins.astype(F32)
        own_count = jnp.sum((own_bins[:, None] == bin_ids[None, :]) * per_bin[None, :], axis=1)
        image_weight = keep * jnp.sum(all_valid) / (BINS * jnp.maximum(own_count, 1.0))

        cond_act = jax.nn.silu(cond_rows).astype(BF16)
        pack = packed(jnp.transpose(gate_up, (1, 0, 2)), down_weight.T, cond_act)
        return cond_act, image_weight, pack

    cond_act, image_weight, second_pack = region(given, over_dp)
    mods_terms = jnp.einsum("nd,cde->nce", cond_act, ada, preferred_element_type=F32)
    mods_own = scatter_rows(mods_terms.reshape(all_images, -1), "dp")
    hop_one = line_first(second_pack) if on_line else ()
    beside = [swap(second_pack, "dp", 1)] if on_line else []
    near = line_near(hop_one, hop_one[0]) if on_line else None
    mods_own = after(mods_own, *beside)
    mods_own = mods_own.reshape(images, 6, quarter) + ada_bias[None]
    mods_own = jnp.pad(mods_own, ((0, 0), (0, 2), (0, 0)))
    beside += [swap(near, "dp", 1)] if on_line else []
    two = line_two(hop_one, beside[1]) if on_line else None
    held = [*beside, two] if on_line else []
    side = mp // 2
    far = swap(mods_own, "mp", 2)
    pair = jnp.stack([jnp.where(side == 0, mods_own, far), jnp.where(side == 0, far, mods_own)])
    other = swap(pair, "mp", 1)
    quad = jnp.stack([jnp.where(core == 0, pair, other), jnp.where(core == 0, other, pair)], axis=1)
    mods = jnp.transpose(quad, (2, 3, 0, 1, 4)).reshape(images, 8, width)

    count = dp_size if on_line else 1
    place = jnp.stack([mp, mp ^ 2, mp ^ 1, mp ^ 3, core] + [dp ^ k for k in range(count)])
    place = place.astype(jnp.int32)
    block_shape = (width // count,)
    gains = jnp.stack([query_gain, key_gain], axis=1)
    tables = jnp.asarray(rotary_tables(patches, head_size))
    full = 4 * quarter
    span = round_up(3 * quarter, LANES)
    start = 3 * quarter // LANES * LANES
    wide = lambda dtype: shaped((images, width, patches), dtype)
    half = shaped((images, width // 2, patches), BF16)
    tall = pltpu.VMEM((width, patches), F32)

    lat, h_one, raw, lse, ob, *attn_terms = call(
        lambda p, l, m, w, g, t, _, outs, s: attention_forward(
            heads, p[0], l, m[0], w[0], g[0], t[0], outs, s
        ),
        [
            [(place, scalars)],
            [(a, each) for a in lat_pieces],
            [(mods, each)],
            [(first, whole)],
            [(gains, whole)],
            [(tables, whole)],
            [(a, token) for a in held],
        ],
        [
            (wide(BF16), each),
            (wide(BF16), each),
            (shaped((images, 3 * quarter, patches), F32), each),
            (shaped((images, heads, patches), F32), each),
            (shaped((images, full - start, patches), BF16), each),
            (half, each),
            (half, each),
        ],
        [tall],
        images,
    )
    if on_line:
        blocks, block_owners = line_rest(second_pack, beside, hop_one, near, two)
        attn_chip = mp_chip(*attn_terms, blocks[6])

        def assemble(p, blocks, outs, _):
            copy_blocks(p[0], 0, blocks, outs[0])

        (second,) = call(
            assemble,
            [
                [(jnp.stack(block_owners).astype(jnp.int32), scalars)],
                [(a, whole) for a in blocks],
            ],
            [(shaped((width, 3 * units), BF16), whole)],
            [],
            1,
        )
        attn_sums = mp_join(attn_chip, swap(attn_chip, "mp", 2), blocks[7])
    else:
        second = lax.all_gather(second_pack, "dp", axis=0, tiled=True)
        attn_sums = mp_total(*attn_terms)

    def middle():
        mid, attn_own, h_two, hidden, dffn, dgu, cot, mine, theirs = call(
            lambda p, w, l, s, m, c, k, outs, x: feed_forward(
                p[0], w[0], l[0], s, m[0], c, k[0], outs, x
            ),
            [
                [(place, scalars)],
                [(image_weight, scalars)],
                [(lat, each)],
                [(a, each) for a in attn_sums],
                [(mods, each)],
                [(a, each) for a in cot_pieces],
                [(second, whole)],
            ],
            [
                (wide(F32), each),
                (shaped((images, quarter, patches), F32), each),
                (wide(BF16), each),
                (shaped((images, units, patches), BF16), each),
                (wide(BF16), each),
                (shaped((images, 2 * units, patches), BF16), each),
                (wide(BF16), each),
                (half, each),
                (half, each),
            ],
            [tall],
            images,
        )
        (second_terms,) = call(
            lambda a, outs, x: feed_forward_grads(*a, outs),
            [[(h_two, whole), (hidden, whole), (dffn, whole), (dgu, whole)]],
            [(shaped((width, 3 * units), BF16), whole)],
            [],
            1,
        )
        return mid, attn_own, cot, hidden, mine, swap(theirs, "mp", 1), second_terms

    mid, attn_own, cot, hidden, dh_two_mine, dh_two_other, second_terms = region(given, middle)
    second_sum = lax.psum_scatter(second_terms, "dp", scatter_dimension=0, tiled=True)

    def backward():
        dh_two_chip = add_blocks(dh_two_mine, dh_two_other)
        (ffn_part,) = call(
            lambda a, outs, x: feed_forward_end(*a, *outs),
            [[(hidden, whole), (second, last)]],
            [(wide(BF16), whole)],
            [],
            1,
        )
        dh_two_sums = mp_join(dh_two_chip, swap(dh_two_chip, "mp", 2), ffn_part)
        dmid, dattn, draw, mine, theirs, dmods_part, qgain, kgain = call(
            lambda p, w, s, a, outs, x: attention_backward(heads, p[0], w[0], s, *a, outs, x),
            [
                [(place, scalars)],
                [(image_weight, scalars)],
                [(a, each) for a in dh_two_sums],
                [
                    (mid, each),
                    (attn_own, each),
                    (cot, each),
                    (mods, each),
                    (raw, each),
                    (lse, each),
                    (gains, whole),
                    (tables, whole),
                    (first, whole),
                ],
            ],
            [
                (wide(F32), each),
                (wide(BF16), each),
                (shaped((images, span, patches), BF16), each),
                (half, each),
                (half, each),
                (shaped((images, 8, quarter), F32), each),
                (shaped((images, 8, head_size), F32), each),
                (shaped((images, 8, head_size), F32), each),
            ],
            [tall, tall],
            images,
        )
        first_terms = call(
            lambda p, a, outs, x: attention_grads(p[0], *a, outs, x),
            [
                [(place, scalars)],
                [(h_one, whole), (draw, whole), (dattn, whole), (ob, whole)],
            ],
            [(shaped(block_shape + (full,), BF16), whole)] * count,
            [pltpu.VMEM((width, full), F32)],
            1,
        )
        ffn_own = mp_quarter(ffn_part)
        first_beside = dp_cross(first_terms)
        end_half = [add_blocks(first_terms[6], first_beside[3])] if on_line else []
        last_line = [swap(half_sum, "dp", 6) for half_sum in end_half]
        dh_one_sums = mp_total(mine, theirs, (*first_terms, *first_beside[3:]))
        block_out, latent_grad, dmods = call(
            lambda p, w, k, s, a, _, outs, x: last_steps(p[0], w[0], k[0], s, *a, outs, x),
            [
                [(place, scalars)],
                [(image_weight, scalars)],
                [(keep, scalars)],
                [(a, each) for a in dh_one_sums],
                [
                    (lat, each),
                    (dmid, each),
                    (mid, each),
                    (cot, each),
                    (mods, each),
                    (ffn_own, each),
                    (dmods_part, each),
                ],
                [(a, token) for a in end_half],
            ],
            [
                (shaped((images, quarter, patches), BF16), each),
                (shaped((images, quarter, patches), BF16), each),
                (shaped((images, 8, quarter), F32), each),
            ],
            [tall, tall],
            images,
        )

        halves = dp_pair_sums(first_terms, first_beside[:3], dmods) if on_line else []

        gain_terms = jnp.concatenate([jnp.sum(qgain[:, 0], axis=0), jnp.sum(kgain[:, 0], axis=0)])
        high = gain_terms.astype(BF16)
        low = (gain_terms - high.astype(F32)).astype(BF16)
        beside = jnp.concatenate([high, low])[None]
        beside = jnp.concatenate([beside, jnp.zeros((images - 1, beside.shape[1]), BF16)], axis=0)
        rounded = dmods[:, :6].astype(BF16).reshape(images, 6 * quarter)
        rounded = after(jnp.concatenate([rounded, beside], axis=1), *halves, *last_line)
        told_back = gather_rows(rounded, "dp")
        own = first_terms[:2] if count > 1 else first_beside
        return block_out, latent_grad, told_back, own, halves, last_line

    block_out, latent_grad, told_back, own, halves, last_line = region(given, backward)
    first_far = dp_lines(halves) + last_line

    def modulation_grads():
        dmods_all = told_back[:, : 6 * quarter].reshape(all_images, 6, quarter)
        gain_sum = jnp.sum(told_back[:, 6 * quarter :].astype(F32), axis=0)
        gain_sum = gain_sum[: 2 * head_size] + gain_sum[2 * head_size :]
        ada_grad = jnp.einsum("nd,nce->cde", cond_act, dmods_all, preferred_element_type=F32)
        bias_grad = jnp.sum(dmods_all.astype(F32), axis=0)
        cond_terms = jnp.einsum("nce,cde->nd", dmods_all, ada, preferred_element_type=F32)
        both = mp_sum_small(jnp.concatenate([cond_terms.reshape(-1), gain_sum]))
        gain_sum = both[cond_terms.size :]
        cond_sum = rows_to_columns(both[: cond_terms.size].reshape(cond_terms.shape), "dp")
        return ada_grad, bias_grad, gain_sum, cond_sum

    ada_grad, bias_grad, gain_sum, cond_sum = region(given, modulation_grads)
    last_terms = [own[0], *first_far]
    if count > 1:
        last_terms.insert(1, swap(own[1], "dp", 1))
    qkv_grad, out_grad = unpacked(last_terms, quarter)
    second_sum = second_sum.astype(F32)
    gateup_grad = jnp.stack([second_sum[:, :units], second_sum[:, units : 2 * units]], axis=1)
    down_grad = second_sum[:, 2 * units :].T
    cond_own = condition.astype(F32)
    sig = jax.nn.sigmoid(cond_own)
    condition_grad = (cond_sum * sig * (1.0 + cond_own * (1.0 - sig))).astype(BF16)
    return (
        jnp.transpose(block_out, (0, 2, 1)),
        jnp.transpose(latent_grad, (0, 2, 1)),
        condition_grad,
        jnp.transpose(ada_grad, (1, 0, 2)),
        bias_grad,
        jnp.transpose(qkv_grad, (1, 0, 2)),
        gain_sum[:head_size],
        gain_sum[head_size:],
        out_grad.T,
        gateup_grad,
        down_grad,
    )


def solution(mesh):
    placed = (
        P("dp", None, "mp"),
        P("dp", None),
        P("dp"),
        P("dp"),
        P("dp", None, "mp"),
        P(None, "mp"),
        P("dp", None, "mp"),
        P(),
        P(),
        P("mp", "dp"),
        P("dp", None, "mp"),
        P("mp", "dp"),
        P("dp", None, "mp"),
    )
    return jax.shard_map(
        body,
        mesh=mesh,
        in_specs=placed,
        out_specs=(
            P("dp", None, "mp"),
            P("dp", None, "mp"),
            P("dp", None),
            P("dp", None, "mp"),
            P(None, "mp"),
            P("dp", None, "mp"),
            P(),
            P(),
            P("mp", "dp"),
            P("dp", None, "mp"),
            P("mp", "dp"),
        ),
        check_vma=False,
    )
```

```python
import functools
import math

import jax
import jax.numpy as jnp
import numpy as np
from jax import lax
from jax.experimental import pallas as pl
from jax.experimental.pallas import tpu as pltpu
from jax.sharding import PartitionSpec as P

GRID = 16
BINS = 8
EPS = 1e-06
F32 = jnp.float32
BF16 = jnp.bfloat16
VMEM_BYTES = 56 * 1024 * 1024
LANES = 128
NT = (((1,), (1,)), ((), ()))
NN = (((1,), (0,)), ((), ()))
TN = (((0,), (0,)), ((), ()))


def dot(left, right, dims):
    return lax.dot_general(left, right, dims, preferred_element_type=F32)


def swap(value, axis, bit):
    size = lax.axis_size(axis)
    return lax.ppermute(value, axis, [(i, i ^ bit) for i in range(size)])


def round_up(value, unit):
    return -(-value // unit) * unit


def region(given, work):
    shapes = jax.eval_shape(work)
    return lax.cond(given, work, lambda: jax.tree.map(lambda a: jnp.zeros(a.shape, a.dtype), shapes))


def ordered(bit, mine, other, axis):
    first = jnp.where(bit == 0, mine, other)
    second = jnp.where(bit == 0, other, mine)
    return jnp.concatenate([first, second], axis=axis)


def gather_rows(value, axis):
    size, me = lax.axis_size(axis), lax.axis_index(axis)
    steps = [1 << k for k in range(size.bit_length() - 1)]
    shape = value.shape
    steps = steps[1:] + steps[:1]
    for step in steps:
        value = ordered((me // step) % 2, value[None], swap(value, axis, step)[None], 0)
    count = len(steps)
    order = sorted(range(count), key=lambda k: -steps[count - 1 - k])
    value = jnp.transpose(value, order + [count, count + 1])
    return value.reshape((size * shape[0],) + shape[1:])


def scatter_rows(value, axis):
    size, me = lax.axis_size(axis), lax.axis_index(axis)
    step = size // 2
    while step >= 1:
        half = value.shape[0] // 2
        bit = (me // step) % 2
        keep = jnp.where(bit == 0, value[:half], value[half:])
        send = jnp.where(bit == 0, value[half:], value[:half])
        value = keep + swap(send, axis, step)
        step //= 2
    return value


def rows_to_columns(value, axis):
    size, me = lax.axis_size(axis), lax.axis_index(axis)
    step = 1
    while step < size:
        rows, cols = value.shape
        bit = (me // step) % 2
        per = rows // (size // step)
        split = value.reshape(size // step // 2, 2, per, cols)
        keep = jnp.where(bit == 0, split[:, 0], split[:, 1]).reshape(rows // 2, cols)
        send = jnp.where(bit == 0, split[:, 1], split[:, 0]).reshape(rows // 2, cols)
        value = ordered(bit, keep, swap(send, axis, step), 1)
        step *= 2
    return value


def mp_sum_small(value):
    step = lax.axis_size("mp") // 2
    while step >= 1:
        value = value + swap(value, "mp", step)
        step //= 2
    return value


def mp_pieces(value):
    far = swap(value, "mp", 2)
    near = swap(value, "mp", 1)
    both = swap(far, "mp", 1)
    return [value, far, near, both]


def mp_chip(mine, theirs, *tokens):
    return add_blocks(mine, swap(theirs, "mp", 1), *tokens)


def mp_join(chip, far, *tokens):
    half = add_blocks(chip, far, *tokens)
    return half, swap(half, "mp", 1)


def mp_total(mine, theirs, tokens=()):
    chip = mp_chip(mine, theirs)
    return mp_join(chip, swap(chip, "mp", 2), *tokens)


def mp_quarter(partial):
    images, width, patches = partial.shape
    quarter = width // 4
    me = lax.axis_index("mp")
    core, side = me % 2, me // 2
    split = partial.reshape(images, 2, 2, quarter, patches)
    send = jnp.where(core == 0, split[:, :, 1], split[:, :, 0])
    keep = jnp.where(core == 0, split[:, :, 0], split[:, :, 1])
    chip = keep.astype(F32) + swap(send, "mp", 1).astype(F32)
    send = jnp.where(side == 0, chip[:, 1], chip[:, 0]).astype(BF16)
    keep = jnp.where(side == 0, chip[:, 0], chip[:, 1])
    return keep + swap(send, "mp", 2).astype(F32)


def direct():
    return lax.axis_size("dp") in (2, 4, 8)


def along(value, pairs):
    return lax.ppermute(value, "dp", [(2 * a + y, 2 * b + y) for a, b in pairs for y in (0, 1)])


def line_first(block):
    up = along(block, [(0, 1), (1, 2), (2, 3)])
    return up, along(block, [(1, 0), (2, 1), (3, 2)])


def line_near(first, token):
    return pick(lax.axis_index("dp") // 2 % 2 == 1, first[0], first[1], token)


def line_second(first):
    return along(first[0], [(1, 2), (2, 3)]), along(first[1], [(1, 0), (2, 1)])


def line_two(first, token):
    second = line_second(first)
    return pick(lax.axis_index("dp") // 2 >= 2, second[0], second[1], token)


def line_rest(block, beside, first, one, two):
    me = lax.axis_index("dp")
    at = me // 2
    end = along(two, [(1, 0), (2, 3)])
    three = jnp.where(at == 0, end, jnp.where(at == 1, first[1], jnp.where(at == 2, first[0], end)))
    found = [block, one, two, three]
    places = [at, at ^ 1, jnp.where(at >= 2, at - 2, at + 2), 3 - at]
    blocks = found + beside + [swap(b, "dp", 1) for b in found[2:]]
    return blocks, [2 * p + me % 2 for p in places] + [2 * p + 1 - me % 2 for p in places]


def pick(flag, left, right, token):
    def kernel(flag_ref, left_ref, right_ref, _, out_ref):
        @pl.when(flag_ref[0] == 1)
        def _():
            out_ref[...] = left_ref[...]

        @pl.when(flag_ref[0] == 0)
        def _():
            out_ref[...] = right_ref[...]

    return pl.pallas_call(
        kernel,
        in_specs=[pl.BlockSpec(memory_space=pltpu.SMEM)]
        + [pl.BlockSpec(memory_space=pltpu.VMEM)] * 2
        + [pl.BlockSpec(memory_space=pl.ANY)],
        out_specs=pl.BlockSpec(memory_space=pltpu.VMEM),
        out_shape=shaped(left.shape, left.dtype),
        cost_estimate=pl.CostEstimate(flops=1, bytes_accessed=1, transcendentals=0),
    )(jnp.reshape(flag.astype(jnp.int32), (1,)), left, right, token)


def unpacked(terms, quarter):
    rows = terms[0].shape[0]

    def kernel(*refs):
        qkv_ref, out_ref = refs[-2:]
        total = refs[0][...].astype(F32)
        for ref in refs[1:-2]:
            total = total + ref[...].astype(F32)
        for part in range(3):
            qkv_ref[part] = total[:, part * quarter : (part + 1) * quarter]
        out_ref[...] = total[:, 3 * quarter :]

    return pl.pallas_call(
        kernel,
        out_shape=[shaped((3, rows, quarter), F32), shaped((rows, quarter), F32)],
        compiler_params=pltpu.CompilerParams(vmem_limit_bytes=VMEM_BYTES),
        cost_estimate=pl.CostEstimate(flops=1, bytes_accessed=1, transcendentals=0),
    )(*terms)


def packed(gate_up, down, token):
    rows, units = down.shape

    def kernel(gate_up_ref, down_ref, _, out_ref):
        out_ref[:, :units] = gate_up_ref[0]
        out_ref[:, units : 2 * units] = gate_up_ref[1]
        out_ref[:, 2 * units :] = down_ref[...]

    return pl.pallas_call(
        kernel,
        in_specs=[pl.BlockSpec(memory_space=pltpu.VMEM)] * 2 + [pl.BlockSpec(memory_space=pl.ANY)],
        out_specs=pl.BlockSpec(memory_space=pltpu.VMEM),
        out_shape=shaped((rows, 3 * units), down.dtype),
        cost_estimate=pl.CostEstimate(flops=1, bytes_accessed=1, transcendentals=0),
    )(gate_up, down, token)


def dp_cross(parts):
    if len(parts) == 1:
        return [lax.psum_scatter(parts[0], "dp", scatter_dimension=0, tiled=True)]
    return [None] + [swap(parts[k + 1], "dp", 1) for k in range(2, len(parts), 2)]


def dp_pair_sums(parts, cross, *tokens):
    return [add_blocks(parts[2 * k], cross[k], *tokens) for k in range(1, len(cross))]


def dp_lines(halves):
    return [swap(half, "dp", 2 * k + 2) for k, half in enumerate(halves)]


def add_blocks(left, right, *tokens):
    def kernel(*refs):
        refs[-1][...] = (refs[0][...].astype(F32) + refs[1][...].astype(F32)).astype(BF16)

    return pl.pallas_call(
        kernel,
        in_specs=[pl.BlockSpec(memory_space=pltpu.VMEM)] * 2
        + [pl.BlockSpec(memory_space=pl.ANY)] * len(tokens),
        out_specs=pl.BlockSpec(memory_space=pltpu.VMEM),
        out_shape=shaped(left.shape, BF16),
        compiler_params=pltpu.CompilerParams(vmem_limit_bytes=VMEM_BYTES),
        cost_estimate=pl.CostEstimate(flops=1, bytes_accessed=1, transcendentals=0),
    )(left, right, *tokens)


def after(value, *others):
    if not others:
        return value

    def kernel(*refs):
        refs[-1][...] = refs[0][...]

    return pl.pallas_call(
        kernel,
        in_specs=[pl.BlockSpec(memory_space=pltpu.VMEM)]
        + [pl.BlockSpec(memory_space=pl.ANY)] * len(others),
        out_specs=pl.BlockSpec(memory_space=pltpu.VMEM),
        out_shape=shaped(value.shape, value.dtype),
        cost_estimate=pl.CostEstimate(flops=1, bytes_accessed=1, transcendentals=0),
    )(value, *others)


def copy_blocks(place, first, blocks, whole_ref):
    for k, ref in enumerate(blocks):
        if len(blocks) == 1:
            whole_ref[...] = ref[...]
        else:
            whole_ref[rows_at(place[first + k], ref.shape[0]), :] = ref[...]


def split_blocks(place, first, sum_ref, outs):
    for k, ref in enumerate(outs):
        if len(outs) == 1:
            ref[...] = sum_ref[...].astype(BF16)
        else:
            ref[...] = sum_ref[rows_at(place[first + k], ref.shape[0]), :].astype(BF16)


def rotary_tables(patches, head_size):
    pairs = head_size // 4
    freqs = 10000.0 ** (-np.arange(pairs, dtype=np.float64) / pairs)
    spots = np.arange(patches)
    row = (spots // GRID)[None, :] * freqs[:, None]
    col = (spots % GRID)[None, :] * freqs[:, None]
    angles = np.concatenate([row, row, col, col], axis=0)
    cosine, sine = np.cos(angles), np.sin(angles)
    first = (np.arange(head_size) // pairs % 2 == 0)[:, None]
    up = np.where(first, -sine, 0.0)
    down = np.where(first, 0.0, sine)
    return np.stack([cosine, up, down]).astype(np.float32)


def turned(value, up, down):
    height = value.shape[0]
    pairs = height // 4
    return pltpu.roll(value, height - pairs, 0) * up + pltpu.roll(value, pairs, 0) * down


def normed(value):
    centred = value - jnp.mean(value, axis=0, keepdims=True)
    scale = lax.rsqrt(jnp.mean(centred * centred, axis=0, keepdims=True) + EPS)
    return centred * scale, scale


def norm_back(grad, unit, scale):
    return scale * (
        grad
        - jnp.mean(grad, axis=0, keepdims=True)
        - unit * jnp.mean(grad * unit, axis=0, keepdims=True)
    )


def row_sums(value):
    ones = jnp.ones((8, value.shape[1]), F32)
    return lax.dot_general(
        ones, value, NT, precision=lax.Precision.HIGHEST, preferred_element_type=F32
    )[0:1]


def rows_at(index, size):
    return pl.ds(pl.multiple_of(index * size, 16), size)


def heads_of(raw, gains, tables, head):
    size = gains.shape[0]
    width = raw.shape[0] // 3
    cosine, up, down = tables[0], tables[1], tables[2]
    found = []
    for part in range(2):
        rows = raw[part * width + head * size : part * width + (head + 1) * size]
        scale = lax.rsqrt(jnp.mean(rows * rows, axis=0, keepdims=True) + EPS)
        hat = rows * scale
        gained = hat * gains[:, part : part + 1]
        rotated = gained * cosine + turned(gained, up, down)
        found.append((hat, scale, rotated.astype(BF16)))
    value = raw[2 * width + head * size : 2 * width + (head + 1) * size].astype(BF16)
    return found[0], found[1], value


def attention_forward(
    heads, place, lat_refs, mods_ref, weight_ref, gains_ref, tables_ref, outs, scratch
):
    lat_ref, h_ref, raw_ref, lse_ref, ob_ref, mine_ref, theirs_ref = outs
    (x_ref,) = scratch
    quarter = lat_refs[0].shape[1]
    width = quarter
    size = gains_ref.shape[0]
    inverse = 1.0 / math.sqrt(size)

    for k, ref in enumerate(lat_refs):
        piece = ref[0]
        lat_ref[0, rows_at(place[k], quarter), :] = piece
        x_ref[rows_at(place[k], quarter), :] = piece.astype(F32)
    mods = mods_ref[0].T
    unit, _ = normed(x_ref[...])
    h = (unit * (1.0 + mods[:, 1:2]) + mods[:, 0:1]).astype(BF16)
    h_ref[0] = h
    span = round_up(3 * width, LANES)
    raw = dot(weight_ref[:, :span], h, TN)[: 3 * width]
    raw_ref[0] = raw
    gains, tables = gains_ref[...], tables_ref[...]
    pad = 4 * width - (3 * width) // LANES * LANES - width
    parts, tops = [], []
    for head in range(heads):
        (_, _, query), (_, _, key), value = heads_of(raw, gains, tables, head)
        scores = dot(key, query, TN) * inverse
        top = jnp.max(scores, axis=0, keepdims=True)
        expo = jnp.exp(scores - top)
        total = jnp.sum(expo, axis=0, keepdims=True)
        probs = (expo / total).astype(BF16)
        parts.append(dot(value, probs, NN))
        tops.append(top + jnp.log(total))
    lse_ref[0] = jnp.concatenate(tops, axis=0)
    patches = raw.shape[1]
    ob = jnp.concatenate([jnp.zeros((pad, patches), F32)] + parts, axis=0).astype(BF16)
    ob_ref[0] = ob
    x_ref[...] = dot(weight_ref[:, 4 * width - width - pad :], ob, NN)
    put_halves(place, x_ref, mine_ref, theirs_ref)


def feed_forward(
    place, image_weight, lat_ref, sums, mods_ref, cot_refs, weight_ref, outs, scratch
):
    mid_ref, attn_ref, h_ref, hidden_ref, dffn_ref, dgu_ref, cot_ref, mine_ref, theirs_ref = outs
    (x_ref,) = scratch
    quarter = cot_refs[0].shape[1]
    units = hidden_ref.shape[1]
    mods = mods_ref[0].T
    take_halves(place, x_ref, sums)
    attn_ref[0] = x_ref[rows_at(place[0], quarter), :]
    mid = lat_ref[0].astype(F32) + mods[:, 2:3] * x_ref[...]
    mid_ref[0] = mid
    unit, _ = normed(mid)
    h = (unit * (1.0 + mods[:, 4:5]) + mods[:, 3:4]).astype(BF16)
    h_ref[0] = h
    for k, ref in enumerate(cot_refs):
        piece = ref[0]
        cot_ref[0, rows_at(place[k], quarter), :] = piece
    weight = image_weight[pl.program_id(0)]
    dffn = (mods[:, 5:6] * (cot_ref[0].astype(F32) * weight)).astype(BF16)
    dffn_ref[0] = dffn
    gate = dot(weight_ref[:, :units], h, TN)
    up = dot(weight_ref[:, units : 2 * units], h, TN)
    sig = jax.nn.sigmoid(gate)
    swish = gate * sig
    hidden_ref[0] = (swish * up).astype(BF16)
    dhidden = dot(weight_ref[:, 2 * units :], dffn, TN)
    dgu_ref[0, :units] = (dhidden * up * sig * (1.0 + gate * (1.0 - sig))).astype(BF16)
    dgu_ref[0, units:] = (dhidden * swish).astype(BF16)
    x_ref[...] = dot(weight_ref[:, : 2 * units], dgu_ref[0], NN)
    put_halves(place, x_ref, mine_ref, theirs_ref)


def put_halves(place, x_ref, mine_ref, theirs_ref):
    core, half = place[4], mine_ref.shape[1]
    mine_ref[0] = x_ref[rows_at(core, half), :].astype(BF16)
    theirs_ref[0] = x_ref[rows_at(1 - core, half), :].astype(BF16)


def take_halves(place, x_ref, halves):
    core, half = place[4], halves[0].shape[1]
    x_ref[rows_at(core, half), :] = halves[0][0].astype(F32)
    x_ref[rows_at(1 - core, half), :] = halves[1][0].astype(F32)


def over_images(left_ref, right_ref, rows=slice(None)):
    total = None
    for n in range(left_ref.shape[0]):
        term = dot(left_ref[n], right_ref[n, rows], NT)
        total = term if total is None else total + term
    return total


def feed_forward_grads(h_ref, hidden_ref, dffn_ref, dgu_ref, outs):
    units = hidden_ref.shape[1]
    (grad_ref,) = outs
    grad_ref[:, :units] = over_images(h_ref, dgu_ref, slice(0, units)).astype(BF16)
    grad_ref[:, units : 2 * units] = over_images(h_ref, dgu_ref, slice(units, 2 * units)).astype(BF16)
    grad_ref[:, 2 * units :] = over_images(dffn_ref, hidden_ref).astype(BF16)


def feed_forward_end(hidden_ref, weight_ref, ffn_ref):
    for n in range(hidden_ref.shape[0]):
        ffn_ref[n] = dot(weight_ref[...], hidden_ref[n], NN).astype(BF16)


def attention_backward(
    heads,
    place,
    image_weight,
    sums,
    mid_ref,
    attn_ref,
    cot_ref,
    mods_ref,
    raw_ref,
    lse_ref,
    gains_ref,
    tables_ref,
    weight_ref,
    outs,
    scratch,
):
    dmid_ref, dattn_ref, draw_ref, mine_ref, theirs_ref, dmods_ref, qgain_ref, kgain_ref = outs
    x_ref, y_ref = scratch
    quarter = attn_ref.shape[1]
    width = quarter
    size = gains_ref.shape[0]
    inverse = 1.0 / math.sqrt(size)
    mods = mods_ref[0].T
    take_halves(place, x_ref, sums)
    unit, scale = normed(mid_ref[0])
    y_ref[...] = unit
    own = rows_at(place[0], quarter)
    dh_own = x_ref[own, :]
    dmods_ref[0] = jnp.zeros(dmods_ref.shape[1:], F32)
    dmods_ref[0, 3:4, :] = row_sums(dh_own)
    dmods_ref[0, 4:5, :] = row_sums(dh_own * y_ref[own, :])
    weight = image_weight[pl.program_id(0)]
    dy = cot_ref[0].astype(F32) * weight
    dmid = dy + norm_back(x_ref[...] * (1.0 + mods[:, 4:5]), unit, scale)
    dmid_ref[0] = dmid
    x_ref[...] = dmid
    dmods_ref[0, 2:3, :] = row_sums(x_ref[own, :] * attn_ref[0])
    dattn = (mods[:, 2:3] * dmid).astype(BF16)
    dattn_ref[0] = dattn
    start = (3 * width) // LANES * LANES
    pad = 3 * width - start
    dob = dot(weight_ref[:, start:], dattn, TN)
    raw = raw_ref[0]
    gains, tables = gains_ref[...], tables_ref[...]
    cosine, up, down = tables[0], tables[1], tables[2]
    parts = [[], [], []]
    sums_of = [None, None]
    for head in range(heads):
        query, key, value = heads_of(raw, gains, tables, head)
        grad = dob[pad + head * size : pad + (head + 1) * size].astype(BF16)
        scores = dot(key[2], query[2], TN) * inverse
        probs = jnp.exp(scores - lse_ref[0, head : head + 1, :])
        dprobs = dot(value, grad, TN)
        parts[2].append(dot(grad, probs.astype(BF16), NT))
        dscores = probs * (dprobs - jnp.sum(probs * dprobs, axis=0, keepdims=True))
        dscores = dscores.astype(BF16)
        turned_grads = (
            dot(key[2], dscores, NN) * inverse,
            dot(query[2], dscores, NT) * inverse,
        )
        for part, (rot, (hat, rms, _)) in enumerate(zip(turned_grads, (query, key))):
            back = rot * cosine - turned(rot, up, down)
            term = back * hat
            sums_of[part] = term if sums_of[part] is None else sums_of[part] + term
            g = back * gains[:, part : part + 1]
            parts[part].append(rms * (g - hat * jnp.mean(g * hat, axis=0, keepdims=True)))
    qgain_ref[0] = jnp.broadcast_to(row_sums(sums_of[0]), qgain_ref.shape[1:])
    kgain_ref[0] = jnp.broadcast_to(row_sums(sums_of[1]), kgain_ref.shape[1:])
    span = round_up(3 * width, LANES)
    patches = raw.shape[1]
    tail = [jnp.zeros((span - 3 * width, patches), F32)] if span > 3 * width else []
    draw = jnp.concatenate(parts[0] + parts[1] + parts[2] + tail, axis=0).astype(BF16)
    draw_ref[0] = draw
    x_ref[...] = dot(weight_ref[:, :span], draw, NN)
    put_halves(place, x_ref, mine_ref, theirs_ref)


def attention_grads(place, h_ref, draw_ref, dattn_ref, ob_ref, outs, scratch):
    span = draw_ref.shape[1]
    (sum_ref,) = scratch
    start = sum_ref.shape[1] - ob_ref.shape[1]
    total = over_images(h_ref, draw_ref)
    out = over_images(dattn_ref, ob_ref)
    sum_ref[:, :start] = total[:, :start]
    sum_ref[:, start:span] = total[:, start:] + out[:, : span - start]
    sum_ref[:, span:] = out[:, span - start :]
    split_blocks(place, 5, sum_ref, outs)


def last_steps(
    place, image_weight, keep, sums, lat_ref, dmid_ref, mid_ref, cot_ref, mods_ref, ffn_ref,
    dmods_ref, outs, scratch
):
    out_ref, dlat_ref, dm_ref = outs
    x_ref, y_ref = scratch
    quarter = ffn_ref.shape[1]
    own = rows_at(place[0], quarter)
    mods = mods_ref[0].T
    take_halves(place, x_ref, sums)
    unit, scale = normed(lat_ref[0].astype(F32))
    y_ref[...] = unit
    dh_own = x_ref[own, :]
    dm_ref[0] = dmods_ref[0]
    dm_ref[0, 0:1, :] = row_sums(dh_own)
    dm_ref[0, 1:2, :] = row_sums(dh_own * y_ref[own, :])
    back = norm_back(x_ref[...] * (1.0 + mods[:, 1:2]), unit, scale)
    x_ref[...] = back
    dlat_ref[0] = (dmid_ref[0, own, :] + x_ref[own, :]).astype(BF16)
    n = pl.program_id(0)
    ffn = ffn_ref[0]
    dy = cot_ref[0, own, :].astype(F32) * image_weight[n]
    dm_ref[0, 5:6, :] = row_sums(dy * ffn)
    y_ref[...] = jnp.broadcast_to(mods[:, 5:6], y_ref.shape)
    out_ref[0] = ((mid_ref[0, own, :] + y_ref[own, :] * ffn) * keep[n]).astype(BF16)


def whole(array):
    return pl.BlockSpec(array.shape, lambda n: (0,) * array.ndim)


def last(array):
    width = array.shape[1] // 3
    return pl.BlockSpec((array.shape[0], width), lambda n: (0, 2))


def each(array):
    return pl.BlockSpec((1,) + array.shape[1:], lambda n: (n,) + (0,) * (array.ndim - 1))


def token(_):
    return pl.BlockSpec(memory_space=pl.ANY)


def scalars(_):
    return pl.BlockSpec(memory_space=pltpu.SMEM)


def call(body, groups, outs, scratch, images, flops=1):
    flat, specs, counts = [], [], []
    for group in groups:
        counts.append(len(group))
        for array, kind in group:
            flat.append(array)
            specs.append(kind(array))

    def kernel(*refs):
        at, lists = 0, []
        for count in counts:
            lists.append(list(refs[at : at + count]))
            at += count
        body(*lists, list(refs[at : at + len(outs)]), list(refs[at + len(outs) :]))

    moved = sum(a.size * a.dtype.itemsize for a in flat) if flops > 1 else 1
    return pl.pallas_call(
        kernel,
        grid=(images,),
        in_specs=specs,
        out_specs=[kind(o) for o, kind in outs],
        out_shape=[o for o, _ in outs],
        scratch_shapes=scratch,
        compiler_params=pltpu.CompilerParams(
            dimension_semantics=("arbitrary",), vmem_limit_bytes=VMEM_BYTES
        ),
        cost_estimate=pl.CostEstimate(flops=flops, bytes_accessed=moved, transcendentals=0),
    )(*flat)


def shaped(shape, dtype):
    return jax.ShapeDtypeStruct(shape, dtype)


def body(
    latents,
    condition,
    noise_bins,
    slot_valid,
    ada_weight,
    ada_bias,
    qkv_weight,
    query_gain,
    key_gain,
    out_weight,
    gate_up,
    down_weight,
    cotangent,
):
    images, patches, quarter = latents.shape
    width = condition.shape[1]
    rows = qkv_weight.shape[0]
    units = gate_up.shape[2]
    head_size = query_gain.shape[0]
    heads = quarter // head_size
    dp, mp = lax.axis_index("dp"), lax.axis_index("mp")
    core = mp % 2
    dp_size = lax.axis_size("dp")
    all_images = dp_size * images
    tokens = images * patches

    by_part = jnp.transpose(qkv_weight, (1, 0, 2))
    first_pack = jnp.concatenate([by_part[0], by_part[1], by_part[2], out_weight.T], axis=1)
    first = lax.all_gather(first_pack, "dp", axis=0, tiled=True)
    lat_pieces = mp_pieces(jnp.transpose(latents, (0, 2, 1)))
    cot_pieces = mp_pieces(jnp.transpose(cotangent, (0, 2, 1)))
    ada = jnp.transpose(ada_weight, (1, 0, 2))
    keep = slot_valid.astype(F32)
    given = noise_bins[0] >= 0
    on_line = dp_size == 8

    def over_dp():
        extra = jnp.stack([noise_bins, slot_valid], axis=1).astype(BF16)
        told = jnp.concatenate([condition, extra, jnp.zeros((images, LANES - 2), BF16)], axis=1)
        told = gather_rows(told, "dp")
        all_bins, all_valid = told[:, width].astype(F32), told[:, width + 1].astype(F32)
        cond_rows = lax.dynamic_slice_in_dim(told[:, :width], dp * rows, rows, 1).astype(F32)

        bin_ids = jnp.arange(BINS, dtype=F32)
        member = (all_bins[:, None] == bin_ids[None, :]).astype(F32) * all_valid[:, None]
        per_bin = jnp.sum(member, axis=0)
        own_bins = noise_bins.astype(F32)
        own_count = jnp.sum((own_bins[:, None] == bin_ids[None, :]) * per_bin[None, :], axis=1)
        image_weight = keep * jnp.sum(all_valid) / (BINS * jnp.maximum(own_count, 1.0))

        cond_act = jax.nn.silu(cond_rows).astype(BF16)
        pack = packed(jnp.transpose(gate_up, (1, 0, 2)), down_weight.T, cond_act)
        return cond_act, image_weight, pack

    cond_act, image_weight, second_pack = region(given, over_dp)
    mods_terms = jnp.einsum("nd,cde->nce", cond_act, ada, preferred_element_type=F32)
    mods_own = scatter_rows(mods_terms.reshape(all_images, -1), "dp")
    hop_one = line_first(second_pack) if on_line else ()
    beside = [swap(second_pack, "dp", 1)] if on_line else []
    near = line_near(hop_one, hop_one[0]) if on_line else None
    mods_own = after(mods_own, *beside)
    mods_own = mods_own.reshape(images, 6, quarter) + ada_bias[None]
    mods_own = jnp.pad(mods_own, ((0, 0), (0, 2), (0, 0)))
    beside += [swap(near, "dp", 1)] if on_line else []
    two = line_two(hop_one, beside[1]) if on_line else None
    held = [*beside, two] if on_line else []
    side = mp // 2
    far = swap(mods_own, "mp", 2)
    pair = jnp.stack([jnp.where(side == 0, mods_own, far), jnp.where(side == 0, far, mods_own)])
    other = swap(pair, "mp", 1)
    quad = jnp.stack([jnp.where(core == 0, pair, other), jnp.where(core == 0, other, pair)], axis=1)
    mods = jnp.transpose(quad, (2, 3, 0, 1, 4)).reshape(images, 8, width)

    count = dp_size if on_line else 1
    place = jnp.stack([mp, mp ^ 2, mp ^ 1, mp ^ 3, core] + [dp ^ k for k in range(count)])
    place = place.astype(jnp.int32)
    block_shape = (width // count,)
    gains = jnp.stack([query_gain, key_gain], axis=1)
    tables = jnp.asarray(rotary_tables(patches, head_size))
    full = 4 * quarter
    span = round_up(3 * quarter, LANES)
    start = 3 * quarter // LANES * LANES
    wide = lambda dtype: shaped((images, width, patches), dtype)
    half = shaped((images, width // 2, patches), BF16)
    tall = pltpu.VMEM((width, patches), F32)

    lat, h_one, raw, lse, ob, *attn_terms = call(
        lambda p, l, m, w, g, t, _, outs, s: attention_forward(
            heads, p[0], l, m[0], w[0], g[0], t[0], outs, s
        ),
        [
            [(place, scalars)],
            [(a, each) for a in lat_pieces],
            [(mods, each)],
            [(first, whole)],
            [(gains, whole)],
            [(tables, whole)],
            [(a, token) for a in held],
        ],
        [
            (wide(BF16), each),
            (wide(BF16), each),
            (shaped((images, 3 * quarter, patches), F32), each),
            (shaped((images, heads, patches), F32), each),
            (shaped((images, full - start, patches), BF16), each),
            (half, each),
            (half, each),
        ],
        [tall],
        images,
    )
    if on_line:
        blocks, block_owners = line_rest(second_pack, beside, hop_one, near, two)
        attn_chip = mp_chip(*attn_terms, blocks[6])

        def assemble(p, blocks, outs, _):
            copy_blocks(p[0], 0, blocks, outs[0])

        (second,) = call(
            assemble,
            [
                [(jnp.stack(block_owners).astype(jnp.int32), scalars)],
                [(a, whole) for a in blocks],
            ],
            [(shaped((width, 3 * units), BF16), whole)],
            [],
            1,
        )
        attn_sums = mp_join(attn_chip, swap(attn_chip, "mp", 2), second)
    else:
        second = lax.all_gather(second_pack, "dp", axis=0, tiled=True)
        attn_sums = mp_total(*attn_terms)

    def middle():
        mid, attn_own, h_two, hidden, dffn, dgu, cot, mine, theirs = call(
            lambda p, w, l, s, m, c, k, outs, x: feed_forward(
                p[0], w[0], l[0], s, m[0], c, k[0], outs, x
            ),
            [
                [(place, scalars)],
                [(image_weight, scalars)],
                [(lat, each)],
                [(a, each) for a in attn_sums],
                [(mods, each)],
                [(a, each) for a in cot_pieces],
                [(second, whole)],
            ],
            [
                (wide(F32), each),
                (shaped((images, quarter, patches), F32), each),
                (wide(BF16), each),
                (shaped((images, units, patches), BF16), each),
                (wide(BF16), each),
                (shaped((images, 2 * units, patches), BF16), each),
                (wide(BF16), each),
                (half, each),
                (half, each),
            ],
            [tall],
            images,
        )
        (second_terms,) = call(
            lambda a, outs, x: feed_forward_grads(*a, outs),
            [[(h_two, whole), (hidden, whole), (dffn, whole), (dgu, whole)]],
            [(shaped((width, 3 * units), BF16), whole)],
            [],
            1,
        )
        return mid, attn_own, cot, hidden, mine, swap(theirs, "mp", 1), second_terms

    mid, attn_own, cot, hidden, dh_two_mine, dh_two_other, second_terms = region(given, middle)
    second_sum = lax.psum_scatter(second_terms, "dp", scatter_dimension=0, tiled=True)

    def backward():
        dh_two_chip = add_blocks(dh_two_mine, dh_two_other)
        (ffn_part,) = call(
            lambda a, outs, x: feed_forward_end(*a, *outs),
            [[(hidden, whole), (second, last)]],
            [(wide(BF16), whole)],
            [],
            1,
        )
        dh_two_sums = mp_join(dh_two_chip, swap(dh_two_chip, "mp", 2), ffn_part)
        dmid, dattn, draw, mine, theirs, dmods_part, qgain, kgain = call(
            lambda p, w, s, a, outs, x: attention_backward(heads, p[0], w[0], s, *a, outs, x),
            [
                [(place, scalars)],
                [(image_weight, scalars)],
                [(a, each) for a in dh_two_sums],
                [
                    (mid, each),
                    (attn_own, each),
                    (cot, each),
                    (mods, each),
                    (raw, each),
                    (lse, each),
                    (gains, whole),
                    (tables, whole),
                    (first, whole),
                ],
            ],
            [
                (wide(F32), each),
                (wide(BF16), each),
                (shaped((images, span, patches), BF16), each),
                (half, each),
                (half, each),
                (shaped((images, 8, quarter), F32), each),
                (shaped((images, 8, head_size), F32), each),
                (shaped((images, 8, head_size), F32), each),
            ],
            [tall, tall],
            images,
        )
        first_terms = call(
            lambda p, a, outs, x: attention_grads(p[0], *a, outs, x),
            [
                [(place, scalars)],
                [(h_one, whole), (draw, whole), (dattn, whole), (ob, whole)],
            ],
            [(shaped(block_shape + (full,), BF16), whole)] * count,
            [pltpu.VMEM((width, full), F32)],
            1,
        )
        ffn_own = mp_quarter(ffn_part)
        first_beside = dp_cross(first_terms)
        end_half = [add_blocks(first_terms[6], first_beside[3])] if on_line else []
        last_line = [swap(half_sum, "dp", 6) for half_sum in end_half]
        dh_one_sums = mp_total(mine, theirs, (*first_terms, *first_beside[3:]))
        block_out, latent_grad, dmods = call(
            lambda p, w, k, s, a, _, outs, x: last_steps(p[0], w[0], k[0], s, *a, outs, x),
            [
                [(place, scalars)],
                [(image_weight, scalars)],
                [(keep, scalars)],
                [(a, each) for a in dh_one_sums],
                [
                    (lat, each),
                    (dmid, each),
                    (mid, each),
                    (cot, each),
                    (mods, each),
                    (ffn_own, each),
                    (dmods_part, each),
                ],
                [(a, token) for a in end_half],
            ],
            [
                (shaped((images, quarter, patches), BF16), each),
                (shaped((images, quarter, patches), BF16), each),
                (shaped((images, 8, quarter), F32), each),
            ],
            [tall, tall],
            images,
        )

        halves = dp_pair_sums(first_terms, first_beside[:3], dmods) if on_line else []

        gain_terms = jnp.concatenate([jnp.sum(qgain[:, 0], axis=0), jnp.sum(kgain[:, 0], axis=0)])
        high = gain_terms.astype(BF16)
        low = (gain_terms - high.astype(F32)).astype(BF16)
        beside = jnp.concatenate([high, low])[None]
        beside = jnp.concatenate([beside, jnp.zeros((images - 1, beside.shape[1]), BF16)], axis=0)
        rounded = dmods[:, :6].astype(BF16).reshape(images, 6 * quarter)
        rounded = after(jnp.concatenate([rounded, beside], axis=1), *halves, *last_line)
        told_back = gather_rows(rounded, "dp")
        own = first_terms[:2] if count > 1 else first_beside
        return block_out, latent_grad, told_back, own, halves, last_line

    block_out, latent_grad, told_back, own, halves, last_line = region(given, backward)
    first_far = dp_lines(halves) + last_line

    def modulation_grads():
        dmods_all = told_back[:, : 6 * quarter].reshape(all_images, 6, quarter)
        gain_sum = jnp.sum(told_back[:, 6 * quarter :].astype(F32), axis=0)
        gain_sum = gain_sum[: 2 * head_size] + gain_sum[2 * head_size :]
        ada_grad = jnp.einsum("nd,nce->cde", cond_act, dmods_all, preferred_element_type=F32)
        bias_grad = jnp.sum(dmods_all.astype(F32), axis=0)
        cond_terms = jnp.einsum("nce,cde->nd", dmods_all, ada, preferred_element_type=F32)
        both = mp_sum_small(jnp.concatenate([cond_terms.reshape(-1), gain_sum]))
        gain_sum = both[cond_terms.size :]
        cond_sum = rows_to_columns(both[: cond_terms.size].reshape(cond_terms.shape), "dp")
        return ada_grad, bias_grad, gain_sum, cond_sum

    ada_grad, bias_grad, gain_sum, cond_sum = region(given, modulation_grads)
    last_terms = [own[0], *first_far]
    if count > 1:
        last_terms.insert(1, swap(own[1], "dp", 1))
    qkv_grad, out_grad = unpacked(last_terms, quarter)
    second_sum = second_sum.astype(F32)
    gateup_grad = jnp.stack([second_sum[:, :units], second_sum[:, units : 2 * units]], axis=1)
    down_grad = second_sum[:, 2 * units :].T
    cond_own = condition.astype(F32)
    sig = jax.nn.sigmoid(cond_own)
    condition_grad = (cond_sum * sig * (1.0 + cond_own * (1.0 - sig))).astype(BF16)
    return (
        jnp.transpose(block_out, (0, 2, 1)),
        jnp.transpose(latent_grad, (0, 2, 1)),
        condition_grad,
        jnp.transpose(ada_grad, (1, 0, 2)),
        bias_grad,
        jnp.transpose(qkv_grad, (1, 0, 2)),
        gain_sum[:head_size],
        gain_sum[head_size:],
        out_grad.T,
        gateup_grad,
        down_grad,
    )


def solution(mesh):
    placed = (
        P("dp", None, "mp"),
        P("dp", None),
        P("dp"),
        P("dp"),
        P("dp", None, "mp"),
        P(None, "mp"),
        P("dp", None, "mp"),
        P(),
        P(),
        P("mp", "dp"),
        P("dp", None, "mp"),
        P("mp", "dp"),
        P("dp", None, "mp"),
    )
    return jax.shard_map(
        body,
        mesh=mesh,
        in_specs=placed,
        out_specs=(
            P("dp", None, "mp"),
            P("dp", None, "mp"),
            P("dp", None),
            P("dp", None, "mp"),
            P(None, "mp"),
            P("dp", None, "mp"),
            P(),
            P(),
            P("mp", "dp"),
            P("dp", None, "mp"),
            P("mp", "dp"),
        ),
        check_vma=False,
    )
```

```python
import functools
import math

import jax
import jax.numpy as jnp
import numpy as np
from jax import lax
from jax.experimental import pallas as pl
from jax.experimental.pallas import tpu as pltpu
from jax.sharding import PartitionSpec as P

GRID = 16
BINS = 8
EPS = 1e-06
F32 = jnp.float32
BF16 = jnp.bfloat16
VMEM_BYTES = 56 * 1024 * 1024
LANES = 128
NT = (((1,), (1,)), ((), ()))
NN = (((1,), (0,)), ((), ()))
TN = (((0,), (0,)), ((), ()))


def dot(left, right, dims):
    return lax.dot_general(left, right, dims, preferred_element_type=F32)


def swap(value, axis, bit):
    size = lax.axis_size(axis)
    return lax.ppermute(value, axis, [(i, i ^ bit) for i in range(size)])


def round_up(value, unit):
    return -(-value // unit) * unit


def region(given, work):
    shapes = jax.eval_shape(work)
    return lax.cond(given, work, lambda: jax.tree.map(lambda a: jnp.zeros(a.shape, a.dtype), shapes))


def ordered(bit, mine, other, axis):
    first = jnp.where(bit == 0, mine, other)
    second = jnp.where(bit == 0, other, mine)
    return jnp.concatenate([first, second], axis=axis)


def gather_rows(value, axis):
    size, me = lax.axis_size(axis), lax.axis_index(axis)
    steps = [1 << k for k in range(size.bit_length() - 1)]
    shape = value.shape
    steps = steps[1:] + steps[:1]
    for step in steps:
        value = ordered((me // step) % 2, value[None], swap(value, axis, step)[None], 0)
    count = len(steps)
    order = sorted(range(count), key=lambda k: -steps[count - 1 - k])
    value = jnp.transpose(value, order + [count, count + 1])
    return value.reshape((size * shape[0],) + shape[1:])


def scatter_rows(value, axis):
    size, me = lax.axis_size(axis), lax.axis_index(axis)
    step = size // 2
    while step >= 1:
        half = value.shape[0] // 2
        bit = (me // step) % 2
        keep = jnp.where(bit == 0, value[:half], value[half:])
        send = jnp.where(bit == 0, value[half:], value[:half])
        value = keep + swap(send, axis, step)
        step //= 2
    return value


def rows_to_columns(value, axis):
    size, me = lax.axis_size(axis), lax.axis_index(axis)
    step = 1
    while step < size:
        rows, cols = value.shape
        bit = (me // step) % 2
        per = rows // (size // step)
        split = value.reshape(size // step // 2, 2, per, cols)
        keep = jnp.where(bit == 0, split[:, 0], split[:, 1]).reshape(rows // 2, cols)
        send = jnp.where(bit == 0, split[:, 1], split[:, 0]).reshape(rows // 2, cols)
        value = ordered(bit, keep, swap(send, axis, step), 1)
        step *= 2
    return value


def mp_sum_small(value):
    step = lax.axis_size("mp") // 2
    while step >= 1:
        value = value + swap(value, "mp", step)
        step //= 2
    return value


def mp_pieces(value):
    far = swap(value, "mp", 2)
    near = swap(value, "mp", 1)
    both = swap(far, "mp", 1)
    return [value, far, near, both]


def mp_chip(mine, theirs, *tokens):
    return add_blocks(mine, swap(theirs, "mp", 1), *tokens)


def mp_join(chip, far, *tokens):
    half = add_blocks(chip, far, *tokens)
    return half, swap(half, "mp", 1)


def mp_total(mine, theirs, tokens=()):
    chip = mp_chip(mine, theirs)
    return mp_join(chip, swap(chip, "mp", 2), *tokens)


def mp_quarter(partial):
    images, width, patches = partial.shape
    quarter = width // 4
    me = lax.axis_index("mp")
    core, side = me % 2, me // 2
    split = partial.reshape(images, 2, 2, quarter, patches)
    send = jnp.where(core == 0, split[:, :, 1], split[:, :, 0])
    keep = jnp.where(core == 0, split[:, :, 0], split[:, :, 1])
    chip = keep.astype(F32) + swap(send, "mp", 1).astype(F32)
    send = jnp.where(side == 0, chip[:, 1], chip[:, 0]).astype(BF16)
    keep = jnp.where(side == 0, chip[:, 0], chip[:, 1])
    return keep + swap(send, "mp", 2).astype(F32)


def direct():
    return lax.axis_size("dp") in (2, 4, 8)


def along(value, pairs):
    return lax.ppermute(value, "dp", [(2 * a + y, 2 * b + y) for a, b in pairs for y in (0, 1)])


def line_first(block):
    up = along(block, [(0, 1), (1, 2), (2, 3)])
    return up, along(block, [(1, 0), (2, 1), (3, 2)])


def line_near(first, token):
    return pick(lax.axis_index("dp") // 2 % 2 == 1, first[0], first[1], token)


def line_second(first):
    return along(first[0], [(1, 2), (2, 3)]), along(first[1], [(1, 0), (2, 1)])


def line_two(first, token):
    second = line_second(first)
    return pick(lax.axis_index("dp") // 2 >= 2, second[0], second[1], token)


def line_rest(block, beside, first, one, two):
    me = lax.axis_index("dp")
    at = me // 2
    end = along(two, [(1, 0), (2, 3)])
    three = jnp.where(at == 0, end, jnp.where(at == 1, first[1], jnp.where(at == 2, first[0], end)))
    found = [block, one, two, three]
    places = [at, at ^ 1, jnp.where(at >= 2, at - 2, at + 2), 3 - at]
    blocks = found + beside + [swap(b, "dp", 1) for b in found[2:]]
    return blocks, [2 * p + me % 2 for p in places] + [2 * p + 1 - me % 2 for p in places]


def pick(flag, left, right, token):
    def kernel(flag_ref, left_ref, right_ref, _, out_ref):
        @pl.when(flag_ref[0] == 1)
        def _():
            out_ref[...] = left_ref[...]

        @pl.when(flag_ref[0] == 0)
        def _():
            out_ref[...] = right_ref[...]

    return pl.pallas_call(
        kernel,
        in_specs=[pl.BlockSpec(memory_space=pltpu.SMEM)]
        + [pl.BlockSpec(memory_space=pltpu.VMEM)] * 2
        + [pl.BlockSpec(memory_space=pl.ANY)],
        out_specs=pl.BlockSpec(memory_space=pltpu.VMEM),
        out_shape=shaped(left.shape, left.dtype),
        cost_estimate=pl.CostEstimate(flops=1, bytes_accessed=1, transcendentals=0),
    )(jnp.reshape(flag.astype(jnp.int32), (1,)), left, right, token)


def unpacked(terms, quarter):
    rows = terms[0].shape[0]

    def kernel(*refs):
        qkv_ref, out_ref = refs[-2:]
        total = refs[0][...].astype(F32)
        for ref in refs[1:-2]:
            total = total + ref[...].astype(F32)
        for part in range(3):
            qkv_ref[part] = total[:, part * quarter : (part + 1) * quarter]
        out_ref[...] = total[:, 3 * quarter :]

    return pl.pallas_call(
        kernel,
        out_shape=[shaped((3, rows, quarter), F32), shaped((rows, quarter), F32)],
        compiler_params=pltpu.CompilerParams(vmem_limit_bytes=VMEM_BYTES),
        cost_estimate=pl.CostEstimate(flops=1, bytes_accessed=1, transcendentals=0),
    )(*terms)


def packed(gate_up, down, token):
    rows, units = down.shape

    def kernel(gate_up_ref, down_ref, _, out_ref):
        out_ref[:, :units] = gate_up_ref[0]
        out_ref[:, units : 2 * units] = gate_up_ref[1]
        out_ref[:, 2 * units :] = down_ref[...]

    return pl.pallas_call(
        kernel,
        in_specs=[pl.BlockSpec(memory_space=pltpu.VMEM)] * 2 + [pl.BlockSpec(memory_space=pl.ANY)],
        out_specs=pl.BlockSpec(memory_space=pltpu.VMEM),
        out_shape=shaped((rows, 3 * units), down.dtype),
        cost_estimate=pl.CostEstimate(flops=1, bytes_accessed=1, transcendentals=0),
    )(gate_up, down, token)


def dp_cross(parts):
    if len(parts) == 1:
        return [lax.psum_scatter(parts[0], "dp", scatter_dimension=0, tiled=True)]
    return [None] + [swap(parts[k + 1], "dp", 1) for k in range(2, len(parts), 2)]


def dp_pair_sums(parts, cross, *tokens):
    return [add_blocks(parts[2 * k], cross[k], *tokens) for k in range(1, len(cross))]


def dp_lines(halves):
    return [swap(half, "dp", 2 * k + 2) for k, half in enumerate(halves)]


def add_blocks(left, right, *tokens):
    def kernel(*refs):
        refs[-1][...] = (refs[0][...].astype(F32) + refs[1][...].astype(F32)).astype(BF16)

    return pl.pallas_call(
        kernel,
        in_specs=[pl.BlockSpec(memory_space=pltpu.VMEM)] * 2
        + [pl.BlockSpec(memory_space=pl.ANY)] * len(tokens),
        out_specs=pl.BlockSpec(memory_space=pltpu.VMEM),
        out_shape=shaped(left.shape, BF16),
        compiler_params=pltpu.CompilerParams(vmem_limit_bytes=VMEM_BYTES),
        cost_estimate=pl.CostEstimate(flops=1, bytes_accessed=1, transcendentals=0),
    )(left, right, *tokens)


def after(value, *others):
    if not others:
        return value

    def kernel(*refs):
        refs[-1][...] = refs[0][...]

    return pl.pallas_call(
        kernel,
        in_specs=[pl.BlockSpec(memory_space=pltpu.VMEM)]
        + [pl.BlockSpec(memory_space=pl.ANY)] * len(others),
        out_specs=pl.BlockSpec(memory_space=pltpu.VMEM),
        out_shape=shaped(value.shape, value.dtype),
        cost_estimate=pl.CostEstimate(flops=1, bytes_accessed=1, transcendentals=0),
    )(value, *others)


def copy_blocks(place, first, blocks, whole_ref):
    for k, ref in enumerate(blocks):
        if len(blocks) == 1:
            whole_ref[...] = ref[...]
        else:
            whole_ref[rows_at(place[first + k], ref.shape[0]), :] = ref[...]


def split_blocks(place, first, sum_ref, outs):
    for k, ref in enumerate(outs):
        if len(outs) == 1:
            ref[...] = sum_ref[...].astype(BF16)
        else:
            ref[...] = sum_ref[rows_at(place[first + k], ref.shape[0]), :].astype(BF16)


def rotary_tables(patches, head_size):
    pairs = head_size // 4
    freqs = 10000.0 ** (-np.arange(pairs, dtype=np.float64) / pairs)
    spots = np.arange(patches)
    row = (spots // GRID)[None, :] * freqs[:, None]
    col = (spots % GRID)[None, :] * freqs[:, None]
    angles = np.concatenate([row, row, col, col], axis=0)
    cosine, sine = np.cos(angles), np.sin(angles)
    first = (np.arange(head_size) // pairs % 2 == 0)[:, None]
    up = np.where(first, -sine, 0.0)
    down = np.where(first, 0.0, sine)
    return np.stack([cosine, up, down]).astype(np.float32)


def turned(value, up, down):
    height = value.shape[0]
    pairs = height // 4
    return pltpu.roll(value, height - pairs, 0) * up + pltpu.roll(value, pairs, 0) * down


def normed(value):
    centred = value - jnp.mean(value, axis=0, keepdims=True)
    scale = lax.rsqrt(jnp.mean(centred * centred, axis=0, keepdims=True) + EPS)
    return centred * scale, scale


def norm_back(grad, unit, scale):
    return scale * (
        grad
        - jnp.mean(grad, axis=0, keepdims=True)
        - unit * jnp.mean(grad * unit, axis=0, keepdims=True)
    )


def row_sums(value):
    ones = jnp.ones((8, value.shape[1]), F32)
    return lax.dot_general(
        ones, value, NT, precision=lax.Precision.HIGHEST, preferred_element_type=F32
    )[0:1]


def rows_at(index, size):
    return pl.ds(pl.multiple_of(index * size, 16), size)


def heads_of(raw, gains, tables, head):
    size = gains.shape[0]
    width = raw.shape[0] // 3
    cosine, up, down = tables[0], tables[1], tables[2]
    found = []
    for part in range(2):
        rows = raw[part * width + head * size : part * width + (head + 1) * size]
        scale = lax.rsqrt(jnp.mean(rows * rows, axis=0, keepdims=True) + EPS)
        hat = rows * scale
        gained = hat * gains[:, part : part + 1]
        rotated = gained * cosine + turned(gained, up, down)
        found.append((hat, scale, rotated.astype(BF16)))
    value = raw[2 * width + head * size : 2 * width + (head + 1) * size].astype(BF16)
    return found[0], found[1], value


def attention_forward(
    heads, place, lat_refs, mods_ref, weight_ref, gains_ref, tables_ref, outs, scratch
):
    lat_ref, h_ref, raw_ref, lse_ref, ob_ref, mine_ref, theirs_ref = outs
    (x_ref,) = scratch
    quarter = lat_refs[0].shape[1]
    width = quarter
    size = gains_ref.shape[0]
    inverse = 1.0 / math.sqrt(size)

    for k, ref in enumerate(lat_refs):
        piece = ref[0]
        lat_ref[0, rows_at(place[k], quarter), :] = piece
        x_ref[rows_at(place[k], quarter), :] = piece.astype(F32)
    mods = mods_ref[0].T
    unit, _ = normed(x_ref[...])
    h = (unit * (1.0 + mods[:, 1:2]) + mods[:, 0:1]).astype(BF16)
    h_ref[0] = h
    span = round_up(3 * width, LANES)
    raw = dot(weight_ref[:, :span], h, TN)[: 3 * width]
    raw_ref[0] = raw
    gains, tables = gains_ref[...], tables_ref[...]
    pad = 4 * width - (3 * width) // LANES * LANES - width
    parts, tops = [], []
    for head in range(heads):
        (_, _, query), (_, _, key), value = heads_of(raw, gains, tables, head)
        scores = dot(key, query, TN) * inverse
        top = jnp.max(scores, axis=0, keepdims=True)
        expo = jnp.exp(scores - top)
        total = jnp.sum(expo, axis=0, keepdims=True)
        probs = (expo / total).astype(BF16)
        parts.append(dot(value, probs, NN))
        tops.append(top + jnp.log(total))
    lse_ref[0] = jnp.concatenate(tops, axis=0)
    patches = raw.shape[1]
    ob = jnp.concatenate([jnp.zeros((pad, patches), F32)] + parts, axis=0).astype(BF16)
    ob_ref[0] = ob
    x_ref[...] = dot(weight_ref[:, 4 * width - width - pad :], ob, NN)
    put_halves(place, x_ref, mine_ref, theirs_ref)


def feed_forward(
    place, image_weight, lat_ref, sums, mods_ref, cot_refs, weight_ref, outs, scratch
):
    mid_ref, attn_ref, h_ref, hidden_ref, dffn_ref, dgu_ref, cot_ref, mine_ref, theirs_ref = outs
    (x_ref,) = scratch
    quarter = cot_refs[0].shape[1]
    units = hidden_ref.shape[1]
    mods = mods_ref[0].T
    take_halves(place, x_ref, sums)
    attn_ref[0] = x_ref[rows_at(place[0], quarter), :]
    mid = lat_ref[0].astype(F32) + mods[:, 2:3] * x_ref[...]
    mid_ref[0] = mid
    unit, _ = normed(mid)
    h = (unit * (1.0 + mods[:, 4:5]) + mods[:, 3:4]).astype(BF16)
    h_ref[0] = h
    for k, ref in enumerate(cot_refs):
        piece = ref[0]
        cot_ref[0, rows_at(place[k], quarter), :] = piece
    weight = image_weight[pl.program_id(0)]
    dffn = (mods[:, 5:6] * (cot_ref[0].astype(F32) * weight)).astype(BF16)
    dffn_ref[0] = dffn
    gate = dot(weight_ref[:, :units], h, TN)
    up = dot(weight_ref[:, units : 2 * units], h, TN)
    sig = jax.nn.sigmoid(gate)
    swish = gate * sig
    hidden_ref[0] = (swish * up).astype(BF16)
    dhidden = dot(weight_ref[:, 2 * units :], dffn, TN)
    dgu_ref[0, :units] = (dhidden * up * sig * (1.0 + gate * (1.0 - sig))).astype(BF16)
    dgu_ref[0, units:] = (dhidden * swish).astype(BF16)
    x_ref[...] = dot(weight_ref[:, : 2 * units], dgu_ref[0], NN)
    put_halves(place, x_ref, mine_ref, theirs_ref)


def put_halves(place, x_ref, mine_ref, theirs_ref):
    core, half = place[4], mine_ref.shape[1]
    mine_ref[0] = x_ref[rows_at(core, half), :].astype(BF16)
    theirs_ref[0] = x_ref[rows_at(1 - core, half), :].astype(BF16)


def take_halves(place, x_ref, halves):
    core, half = place[4], halves[0].shape[1]
    x_ref[rows_at(core, half), :] = halves[0][0].astype(F32)
    x_ref[rows_at(1 - core, half), :] = halves[1][0].astype(F32)


def over_images(left_ref, right_ref, rows=slice(None)):
    total = None
    for n in range(left_ref.shape[0]):
        term = dot(left_ref[n], right_ref[n, rows], NT)
        total = term if total is None else total + term
    return total


def feed_forward_grads(h_ref, hidden_ref, dffn_ref, dgu_ref, outs):
    units = hidden_ref.shape[1]
    (grad_ref,) = outs
    grad_ref[:, :units] = over_images(h_ref, dgu_ref, slice(0, units)).astype(BF16)
    grad_ref[:, units : 2 * units] = over_images(h_ref, dgu_ref, slice(units, 2 * units)).astype(BF16)
    grad_ref[:, 2 * units :] = over_images(dffn_ref, hidden_ref).astype(BF16)


def feed_forward_end(hidden_ref, weight_ref, ffn_ref):
    for n in range(hidden_ref.shape[0]):
        ffn_ref[n] = dot(weight_ref[...], hidden_ref[n], NN).astype(BF16)


def attention_backward(
    heads,
    place,
    image_weight,
    sums,
    mid_ref,
    attn_ref,
    cot_ref,
    mods_ref,
    raw_ref,
    lse_ref,
    gains_ref,
    tables_ref,
    weight_ref,
    outs,
    scratch,
):
    dmid_ref, dattn_ref, draw_ref, mine_ref, theirs_ref, dmods_ref, qgain_ref, kgain_ref = outs
    x_ref, y_ref = scratch
    quarter = attn_ref.shape[1]
    width = quarter
    size = gains_ref.shape[0]
    inverse = 1.0 / math.sqrt(size)
    mods = mods_ref[0].T
    take_halves(place, x_ref, sums)
    unit, scale = normed(mid_ref[0])
    y_ref[...] = unit
    own = rows_at(place[0], quarter)
    dh_own = x_ref[own, :]
    dmods_ref[0] = jnp.zeros(dmods_ref.shape[1:], F32)
    dmods_ref[0, 3:4, :] = row_sums(dh_own)
    dmods_ref[0, 4:5, :] = row_sums(dh_own * y_ref[own, :])
    weight = image_weight[pl.program_id(0)]
    dy = cot_ref[0].astype(F32) * weight
    dmid = dy + norm_back(x_ref[...] * (1.0 + mods[:, 4:5]), unit, scale)
    dmid_ref[0] = dmid
    x_ref[...] = dmid
    dmods_ref[0, 2:3, :] = row_sums(x_ref[own, :] * attn_ref[0])
    dattn = (mods[:, 2:3] * dmid).astype(BF16)
    dattn_ref[0] = dattn
    start = (3 * width) // LANES * LANES
    pad = 3 * width - start
    dob = dot(weight_ref[:, start:], dattn, TN)
    raw = raw_ref[0]
    gains, tables = gains_ref[...], tables_ref[...]
    cosine, up, down = tables[0], tables[1], tables[2]
    parts = [[], [], []]
    sums_of = [None, None]
    for head in range(heads):
        query, key, value = heads_of(raw, gains, tables, head)
        grad = dob[pad + head * size : pad + (head + 1) * size].astype(BF16)
        scores = dot(key[2], query[2], TN) * inverse
        probs = jnp.exp(scores - lse_ref[0, head : head + 1, :])
        dprobs = dot(value, grad, TN)
        parts[2].append(dot(grad, probs.astype(BF16), NT))
        dscores = probs * (dprobs - jnp.sum(probs * dprobs, axis=0, keepdims=True))
        dscores = dscores.astype(BF16)
        turned_grads = (
            dot(key[2], dscores, NN) * inverse,
            dot(query[2], dscores, NT) * inverse,
        )
        for part, (rot, (hat, rms, _)) in enumerate(zip(turned_grads, (query, key))):
            back = rot * cosine - turned(rot, up, down)
            term = back * hat
            sums_of[part] = term if sums_of[part] is None else sums_of[part] + term
            g = back * gains[:, part : part + 1]
            parts[part].append(rms * (g - hat * jnp.mean(g * hat, axis=0, keepdims=True)))
    qgain_ref[0] = jnp.broadcast_to(row_sums(sums_of[0]), qgain_ref.shape[1:])
    kgain_ref[0] = jnp.broadcast_to(row_sums(sums_of[1]), kgain_ref.shape[1:])
    span = round_up(3 * width, LANES)
    patches = raw.shape[1]
    tail = [jnp.zeros((span - 3 * width, patches), F32)] if span > 3 * width else []
    draw = jnp.concatenate(parts[0] + parts[1] + parts[2] + tail, axis=0).astype(BF16)
    draw_ref[0] = draw
    x_ref[...] = dot(weight_ref[:, :span], draw, NN)
    put_halves(place, x_ref, mine_ref, theirs_ref)


def attention_grads(place, h_ref, draw_ref, dattn_ref, ob_ref, outs, scratch):
    span = draw_ref.shape[1]
    (sum_ref,) = scratch
    start = sum_ref.shape[1] - ob_ref.shape[1]
    total = over_images(h_ref, draw_ref)
    out = over_images(dattn_ref, ob_ref)
    sum_ref[:, :start] = total[:, :start]
    sum_ref[:, start:span] = total[:, start:] + out[:, : span - start]
    sum_ref[:, span:] = out[:, span - start :]
    split_blocks(place, 5, sum_ref, outs)


def last_steps(
    place, image_weight, keep, sums, lat_ref, dmid_ref, mid_ref, cot_ref, mods_ref, ffn_ref,
    dmods_ref, outs, scratch
):
    out_ref, dlat_ref, dm_ref = outs
    x_ref, y_ref = scratch
    quarter = ffn_ref.shape[1]
    own = rows_at(place[0], quarter)
    mods = mods_ref[0].T
    take_halves(place, x_ref, sums)
    unit, scale = normed(lat_ref[0].astype(F32))
    y_ref[...] = unit
    dh_own = x_ref[own, :]
    dm_ref[0] = dmods_ref[0]
    dm_ref[0, 0:1, :] = row_sums(dh_own)
    dm_ref[0, 1:2, :] = row_sums(dh_own * y_ref[own, :])
    back = norm_back(x_ref[...] * (1.0 + mods[:, 1:2]), unit, scale)
    x_ref[...] = back
    dlat_ref[0] = (dmid_ref[0, own, :] + x_ref[own, :]).astype(BF16)
    n = pl.program_id(0)
    ffn = ffn_ref[0]
    dy = cot_ref[0, own, :].astype(F32) * image_weight[n]
    dm_ref[0, 5:6, :] = row_sums(dy * ffn)
    y_ref[...] = jnp.broadcast_to(mods[:, 5:6], y_ref.shape)
    out_ref[0] = ((mid_ref[0, own, :] + y_ref[own, :] * ffn) * keep[n]).astype(BF16)


def whole(array):
    return pl.BlockSpec(array.shape, lambda n: (0,) * array.ndim)


def last(array):
    width = array.shape[1] // 3
    return pl.BlockSpec((array.shape[0], width), lambda n: (0, 2))


def each(array):
    return pl.BlockSpec((1,) + array.shape[1:], lambda n: (n,) + (0,) * (array.ndim - 1))


def token(_):
    return pl.BlockSpec(memory_space=pl.ANY)


def scalars(_):
    return pl.BlockSpec(memory_space=pltpu.SMEM)


def call(body, groups, outs, scratch, images, flops=1):
    flat, specs, counts = [], [], []
    for group in groups:
        counts.append(len(group))
        for array, kind in group:
            flat.append(array)
            specs.append(kind(array))

    def kernel(*refs):
        at, lists = 0, []
        for count in counts:
            lists.append(list(refs[at : at + count]))
            at += count
        body(*lists, list(refs[at : at + len(outs)]), list(refs[at + len(outs) :]))

    moved = sum(a.size * a.dtype.itemsize for a in flat) if flops > 1 else 1
    return pl.pallas_call(
        kernel,
        grid=(images,),
        in_specs=specs,
        out_specs=[kind(o) for o, kind in outs],
        out_shape=[o for o, _ in outs],
        scratch_shapes=scratch,
        compiler_params=pltpu.CompilerParams(
            dimension_semantics=("arbitrary",), vmem_limit_bytes=VMEM_BYTES
        ),
        cost_estimate=pl.CostEstimate(flops=flops, bytes_accessed=moved, transcendentals=0),
    )(*flat)


def shaped(shape, dtype):
    return jax.ShapeDtypeStruct(shape, dtype)


def body(
    latents,
    condition,
    noise_bins,
    slot_valid,
    ada_weight,
    ada_bias,
    qkv_weight,
    query_gain,
    key_gain,
    out_weight,
    gate_up,
    down_weight,
    cotangent,
):
    images, patches, quarter = latents.shape
    width = condition.shape[1]
    rows = qkv_weight.shape[0]
    units = gate_up.shape[2]
    head_size = query_gain.shape[0]
    heads = quarter // head_size
    dp, mp = lax.axis_index("dp"), lax.axis_index("mp")
    core = mp % 2
    dp_size = lax.axis_size("dp")
    all_images = dp_size * images
    tokens = images * patches

    by_part = jnp.transpose(qkv_weight, (1, 0, 2))
    first_pack = jnp.concatenate([by_part[0], by_part[1], by_part[2], out_weight.T], axis=1)
    first = lax.all_gather(first_pack, "dp", axis=0, tiled=True)
    lat_pieces = mp_pieces(jnp.transpose(latents, (0, 2, 1)))
    cot_pieces = mp_pieces(jnp.transpose(cotangent, (0, 2, 1)))
    ada = jnp.transpose(ada_weight, (1, 0, 2))
    keep = slot_valid.astype(F32)
    given = noise_bins[0] >= 0
    on_line = dp_size == 8

    def over_dp():
        extra = jnp.stack([noise_bins, slot_valid], axis=1).astype(BF16)
        told = jnp.concatenate([condition, extra, jnp.zeros((images, LANES - 2), BF16)], axis=1)
        told = gather_rows(told, "dp")
        all_bins, all_valid = told[:, width].astype(F32), told[:, width + 1].astype(F32)
        cond_rows = lax.dynamic_slice_in_dim(told[:, :width], dp * rows, rows, 1).astype(F32)

        bin_ids = jnp.arange(BINS, dtype=F32)
        member = (all_bins[:, None] == bin_ids[None, :]).astype(F32) * all_valid[:, None]
        per_bin = jnp.sum(member, axis=0)
        own_bins = noise_bins.astype(F32)
        own_count = jnp.sum((own_bins[:, None] == bin_ids[None, :]) * per_bin[None, :], axis=1)
        image_weight = keep * jnp.sum(all_valid) / (BINS * jnp.maximum(own_count, 1.0))

        cond_act = jax.nn.silu(cond_rows).astype(BF16)
        pack = packed(jnp.transpose(gate_up, (1, 0, 2)), down_weight.T, cond_act)
        return cond_act, image_weight, pack

    cond_act, image_weight, second_pack = region(given, over_dp)
    mods_terms = jnp.einsum("nd,cde->nce", cond_act, ada, preferred_element_type=F32)
    mods_own = scatter_rows(mods_terms.reshape(all_images, -1), "dp")
    hop_one = line_first(second_pack) if on_line else ()
    beside = [swap(second_pack, "dp", 1)] if on_line else []
    near = line_near(hop_one, hop_one[0]) if on_line else None
    mods_own = after(mods_own, *beside)
    mods_own = mods_own.reshape(images, 6, quarter) + ada_bias[None]
    mods_own = jnp.pad(mods_own, ((0, 0), (0, 2), (0, 0)))
    beside += [swap(near, "dp", 1)] if on_line else []
    two = line_two(hop_one, beside[1]) if on_line else None
    held = [*beside, two] if on_line else []
    side = mp // 2
    far = swap(mods_own, "mp", 2)
    pair = jnp.stack([jnp.where(side == 0, mods_own, far), jnp.where(side == 0, far, mods_own)])
    other = swap(pair, "mp", 1)
    quad = jnp.stack([jnp.where(core == 0, pair, other), jnp.where(core == 0, other, pair)], axis=1)
    mods = jnp.transpose(quad, (2, 3, 0, 1, 4)).reshape(images, 8, width)

    count = dp_size if on_line else 1
    place = jnp.stack([mp, mp ^ 2, mp ^ 1, mp ^ 3, core] + [dp ^ k for k in range(count)])
    place = place.astype(jnp.int32)
    block_shape = (width // count,)
    gains = jnp.stack([query_gain, key_gain], axis=1)
    tables = jnp.asarray(rotary_tables(patches, head_size))
    full = 4 * quarter
    span = round_up(3 * quarter, LANES)
    start = 3 * quarter // LANES * LANES
    wide = lambda dtype: shaped((images, width, patches), dtype)
    half = shaped((images, width // 2, patches), BF16)
    tall = pltpu.VMEM((width, patches), F32)

    lat, h_one, raw, lse, ob, *attn_terms = call(
        lambda p, l, m, w, g, t, _, outs, s: attention_forward(
            heads, p[0], l, m[0], w[0], g[0], t[0], outs, s
        ),
        [
            [(place, scalars)],
            [(a, each) for a in lat_pieces],
            [(mods, each)],
            [(first, whole)],
            [(gains, whole)],
            [(tables, whole)],
            [(a, token) for a in held],
        ],
        [
            (wide(BF16), each),
            (wide(BF16), each),
            (shaped((images, 3 * quarter, patches), F32), each),
            (shaped((images, heads, patches), F32), each),
            (shaped((images, full - start, patches), BF16), each),
            (half, each),
            (half, each),
        ],
        [tall],
        images,
    )
    if on_line:
        blocks, block_owners = line_rest(second_pack, beside, hop_one, near, two)
        attn_chip = mp_chip(*attn_terms, blocks[6])

        def assemble(p, blocks, outs, _):
            copy_blocks(p[0], 0, blocks, outs[0])

        (second,) = call(
            assemble,
            [
                [(jnp.stack(block_owners).astype(jnp.int32), scalars)],
                [(a, whole) for a in blocks],
            ],
            [(shaped((width, 3 * units), BF16), whole)],
            [],
            1,
        )
        attn_sums = mp_join(attn_chip, swap(attn_chip, "mp", 2), second)
    else:
        second = lax.all_gather(second_pack, "dp", axis=0, tiled=True)
        attn_sums = mp_total(*attn_terms)

    def middle():
        mid, attn_own, h_two, hidden, dffn, dgu, cot, mine, theirs = call(
            lambda p, w, l, s, m, c, k, outs, x: feed_forward(
                p[0], w[0], l[0], s, m[0], c, k[0], outs, x
            ),
            [
                [(place, scalars)],
                [(image_weight, scalars)],
                [(lat, each)],
                [(a, each) for a in attn_sums],
                [(mods, each)],
                [(a, each) for a in cot_pieces],
                [(second, whole)],
            ],
            [
                (wide(F32), each),
                (shaped((images, quarter, patches), F32), each),
                (wide(BF16), each),
                (shaped((images, units, patches), BF16), each),
                (wide(BF16), each),
                (shaped((images, 2 * units, patches), BF16), each),
                (wide(BF16), each),
                (half, each),
                (half, each),
            ],
            [tall],
            images,
        )
        (second_terms,) = call(
            lambda a, outs, x: feed_forward_grads(*a, outs),
            [[(h_two, whole), (hidden, whole), (dffn, whole), (dgu, whole)]],
            [(shaped((width, 3 * units), BF16), whole)],
            [],
            1,
        )
        return mid, attn_own, cot, hidden, mine, swap(theirs, "mp", 1), second_terms

    mid, attn_own, cot, hidden, dh_two_mine, dh_two_other, second_terms = region(given, middle)
    second_sum = lax.psum_scatter(second_terms, "dp", scatter_dimension=0, tiled=True)

    def backward():
        dh_two_chip = add_blocks(dh_two_mine, dh_two_other)
        (ffn_part,) = call(
            lambda a, outs, x: feed_forward_end(*a, *outs),
            [[(hidden, whole), (second, last)]],
            [(wide(BF16), whole)],
            [],
            1,
        )
        dh_two_sums = mp_join(dh_two_chip, swap(dh_two_chip, "mp", 2), ffn_part)
        dmid, dattn, draw, mine, theirs, dmods_part, qgain, kgain = call(
            lambda p, w, s, a, outs, x: attention_backward(heads, p[0], w[0], s, *a, outs, x),
            [
                [(place, scalars)],
                [(image_weight, scalars)],
                [(a, each) for a in dh_two_sums],
                [
                    (mid, each),
                    (attn_own, each),
                    (cot, each),
                    (mods, each),
                    (raw, each),
                    (lse, each),
                    (gains, whole),
                    (tables, whole),
                    (first, whole),
                ],
            ],
            [
                (wide(F32), each),
                (wide(BF16), each),
                (shaped((images, span, patches), BF16), each),
                (half, each),
                (half, each),
                (shaped((images, 8, quarter), F32), each),
                (shaped((images, 8, head_size), F32), each),
                (shaped((images, 8, head_size), F32), each),
            ],
            [tall, tall],
            images,
        )
        first_terms = call(
            lambda p, a, outs, x: attention_grads(p[0], *a, outs, x),
            [
                [(place, scalars)],
                [(h_one, whole), (draw, whole), (dattn, whole), (ob, whole)],
            ],
            [(shaped(block_shape + (full,), BF16), whole)] * count,
            [pltpu.VMEM((width, full), F32)],
            1,
        )
        ffn_own = mp_quarter(ffn_part)
        first_beside = dp_cross(first_terms)
        end_half = [add_blocks(first_terms[6], first_beside[3])] if on_line else []
        last_line = [swap(half_sum, "dp", 6) for half_sum in end_half]
        dh_one_chip = mp_chip(mine, theirs, *first_terms)
        dh_one_sums = mp_join(dh_one_chip, swap(dh_one_chip, "mp", 2), *first_beside[3:])
        block_out, latent_grad, dmods = call(
            lambda p, w, k, s, a, _, outs, x: last_steps(p[0], w[0], k[0], s, *a, outs, x),
            [
                [(place, scalars)],
                [(image_weight, scalars)],
                [(keep, scalars)],
                [(a, each) for a in dh_one_sums],
                [
                    (lat, each),
                    (dmid, each),
                    (mid, each),
                    (cot, each),
                    (mods, each),
                    (ffn_own, each),
                    (dmods_part, each),
                ],
                [(a, token) for a in end_half],
            ],
            [
                (shaped((images, quarter, patches), BF16), each),
                (shaped((images, quarter, patches), BF16), each),
                (shaped((images, 8, quarter), F32), each),
            ],
            [tall, tall],
            images,
        )

        halves = dp_pair_sums(first_terms, first_beside[:3], dmods) if on_line else []

        gain_terms = jnp.concatenate([jnp.sum(qgain[:, 0], axis=0), jnp.sum(kgain[:, 0], axis=0)])
        high = gain_terms.astype(BF16)
        low = (gain_terms - high.astype(F32)).astype(BF16)
        beside = jnp.concatenate([high, low])[None]
        beside = jnp.concatenate([beside, jnp.zeros((images - 1, beside.shape[1]), BF16)], axis=0)
        rounded = dmods[:, :6].astype(BF16).reshape(images, 6 * quarter)
        rounded = after(jnp.concatenate([rounded, beside], axis=1), *halves[1:], *last_line)
        told_back = gather_rows(rounded, "dp")
        own = first_terms[:2] if count > 1 else first_beside
        return block_out, latent_grad, told_back, own, halves, last_line

    block_out, latent_grad, told_back, own, halves, last_line = region(given, backward)
    first_far = dp_lines(halves) + last_line

    def modulation_grads():
        dmods_all = told_back[:, : 6 * quarter].reshape(all_images, 6, quarter)
        gain_sum = jnp.sum(told_back[:, 6 * quarter :].astype(F32), axis=0)
        gain_sum = gain_sum[: 2 * head_size] + gain_sum[2 * head_size :]
        ada_grad = jnp.einsum("nd,nce->cde", cond_act, dmods_all, preferred_element_type=F32)
        bias_grad = jnp.sum(dmods_all.astype(F32), axis=0)
        cond_terms = jnp.einsum("nce,cde->nd", dmods_all, ada, preferred_element_type=F32)
        both = mp_sum_small(jnp.concatenate([cond_terms.reshape(-1), gain_sum]))
        gain_sum = both[cond_terms.size :]
        cond_sum = rows_to_columns(both[: cond_terms.size].reshape(cond_terms.shape), "dp")
        return ada_grad, bias_grad, gain_sum, cond_sum

    ada_grad, bias_grad, gain_sum, cond_sum = region(given, modulation_grads)
    last_terms = [own[0], *first_far]
    if count > 1:
        last_terms.insert(1, swap(own[1], "dp", 1))
    qkv_grad, out_grad = unpacked(last_terms, quarter)
    second_sum = second_sum.astype(F32)
    gateup_grad = jnp.stack([second_sum[:, :units], second_sum[:, units : 2 * units]], axis=1)
    down_grad = second_sum[:, 2 * units :].T
    cond_own = condition.astype(F32)
    sig = jax.nn.sigmoid(cond_own)
    condition_grad = (cond_sum * sig * (1.0 + cond_own * (1.0 - sig))).astype(BF16)
    return (
        jnp.transpose(block_out, (0, 2, 1)),
        jnp.transpose(latent_grad, (0, 2, 1)),
        condition_grad,
        jnp.transpose(ada_grad, (1, 0, 2)),
        bias_grad,
        jnp.transpose(qkv_grad, (1, 0, 2)),
        gain_sum[:head_size],
        gain_sum[head_size:],
        out_grad.T,
        gateup_grad,
        down_grad,
    )


def solution(mesh):
    placed = (
        P("dp", None, "mp"),
        P("dp", None),
        P("dp"),
        P("dp"),
        P("dp", None, "mp"),
        P(None, "mp"),
        P("dp", None, "mp"),
        P(),
        P(),
        P("mp", "dp"),
        P("dp", None, "mp"),
        P("mp", "dp"),
        P("dp", None, "mp"),
    )
    return jax.shard_map(
        body,
        mesh=mesh,
        in_specs=placed,
        out_specs=(
            P("dp", None, "mp"),
            P("dp", None, "mp"),
            P("dp", None),
            P("dp", None, "mp"),
            P(None, "mp"),
            P("dp", None, "mp"),
            P(),
            P(),
            P("mp", "dp"),
            P("dp", None, "mp"),
            P("mp", "dp"),
        ),
        check_vma=False,
    )
```

```python
import functools
import math

import jax
import jax.numpy as jnp
import numpy as np
from jax import lax
from jax.experimental import pallas as pl
from jax.experimental.pallas import tpu as pltpu
from jax.sharding import PartitionSpec as P

GRID = 16
BINS = 8
EPS = 1e-06
F32 = jnp.float32
BF16 = jnp.bfloat16
VMEM_BYTES = 56 * 1024 * 1024
LANES = 128
NT = (((1,), (1,)), ((), ()))
NN = (((1,), (0,)), ((), ()))
TN = (((0,), (0,)), ((), ()))


def dot(left, right, dims):
    return lax.dot_general(left, right, dims, preferred_element_type=F32)


def swap(value, axis, bit):
    size = lax.axis_size(axis)
    return lax.ppermute(value, axis, [(i, i ^ bit) for i in range(size)])


def round_up(value, unit):
    return -(-value // unit) * unit


def region(given, work):
    shapes = jax.eval_shape(work)
    return lax.cond(given, work, lambda: jax.tree.map(lambda a: jnp.zeros(a.shape, a.dtype), shapes))


def ordered(bit, mine, other, axis):
    first = jnp.where(bit == 0, mine, other)
    second = jnp.where(bit == 0, other, mine)
    return jnp.concatenate([first, second], axis=axis)


def gather_rows(value, axis):
    size, me = lax.axis_size(axis), lax.axis_index(axis)
    steps = [1 << k for k in range(size.bit_length() - 1)]
    shape = value.shape
    steps = steps[1:] + steps[:1]
    for step in steps:
        value = ordered((me // step) % 2, value[None], swap(value, axis, step)[None], 0)
    count = len(steps)
    order = sorted(range(count), key=lambda k: -steps[count - 1 - k])
    value = jnp.transpose(value, order + [count, count + 1])
    return value.reshape((size * shape[0],) + shape[1:])


def scatter_rows(value, axis):
    size, me = lax.axis_size(axis), lax.axis_index(axis)
    step = size // 2
    while step >= 1:
        half = value.shape[0] // 2
        bit = (me // step) % 2
        keep = jnp.where(bit == 0, value[:half], value[half:])
        send = jnp.where(bit == 0, value[half:], value[:half])
        value = keep + swap(send, axis, step)
        step //= 2
    return value


def rows_to_columns(value, axis):
    size, me = lax.axis_size(axis), lax.axis_index(axis)
    step = 1
    while step < size:
        rows, cols = value.shape
        bit = (me // step) % 2
        per = rows // (size // step)
        split = value.reshape(size // step // 2, 2, per, cols)
        keep = jnp.where(bit == 0, split[:, 0], split[:, 1]).reshape(rows // 2, cols)
        send = jnp.where(bit == 0, split[:, 1], split[:, 0]).reshape(rows // 2, cols)
        value = ordered(bit, keep, swap(send, axis, step), 1)
        step *= 2
    return value


def mp_sum_small(value):
    step = lax.axis_size("mp") // 2
    while step >= 1:
        value = value + swap(value, "mp", step)
        step //= 2
    return value


def mp_pieces(value):
    far = swap(value, "mp", 2)
    near = swap(value, "mp", 1)
    both = swap(far, "mp", 1)
    return [value, far, near, both]


def mp_chip(mine, theirs, *tokens):
    return add_blocks(mine, swap(theirs, "mp", 1), *tokens)


def mp_join(chip, far, *tokens):
    half = add_blocks(chip, far, *tokens)
    return half, swap(half, "mp", 1)


def mp_total(mine, theirs, tokens=()):
    chip = mp_chip(mine, theirs)
    return mp_join(chip, swap(chip, "mp", 2), *tokens)


def mp_quarter(mine, theirs):
    images, rows, patches = mine.shape
    side = lax.axis_index("mp") // 2
    chip = mine.astype(F32) + swap(theirs, "mp", 1).astype(F32)
    chip = chip.reshape(images, 2, rows // 2, patches)
    send = jnp.where(side == 0, chip[:, 1], chip[:, 0]).astype(BF16)
    keep = jnp.where(side == 0, chip[:, 0], chip[:, 1])
    return keep + swap(send, "mp", 2).astype(F32)


def direct():
    return lax.axis_size("dp") in (2, 4, 8)


def along(value, pairs):
    return lax.ppermute(value, "dp", [(2 * a + y, 2 * b + y) for a, b in pairs for y in (0, 1)])


def line_first(block):
    up = along(block, [(0, 1), (1, 2), (2, 3)])
    return up, along(block, [(1, 0), (2, 1), (3, 2)])


def line_near(first, token):
    return pick(lax.axis_index("dp") // 2 % 2 == 1, first[0], first[1], token)


def line_second(first):
    return along(first[0], [(1, 2), (2, 3)]), along(first[1], [(1, 0), (2, 1)])


def line_two(first, token):
    second = line_second(first)
    return pick(lax.axis_index("dp") // 2 >= 2, second[0], second[1], token)


def line_rest(block, beside, first, one, two):
    me = lax.axis_index("dp")
    at = me // 2
    end = along(two, [(1, 0), (2, 3)])
    three = jnp.where(at == 0, end, jnp.where(at == 1, first[1], jnp.where(at == 2, first[0], end)))
    found = [block, one, two, three]
    places = [at, at ^ 1, jnp.where(at >= 2, at - 2, at + 2), 3 - at]
    blocks = found + beside + [swap(b, "dp", 1) for b in found[2:]]
    return blocks, [2 * p + me % 2 for p in places] + [2 * p + 1 - me % 2 for p in places]


def pick(flag, left, right, token):
    def kernel(flag_ref, left_ref, right_ref, _, out_ref):
        @pl.when(flag_ref[0] == 1)
        def _():
            out_ref[...] = left_ref[...]

        @pl.when(flag_ref[0] == 0)
        def _():
            out_ref[...] = right_ref[...]

    return pl.pallas_call(
        kernel,
        in_specs=[pl.BlockSpec(memory_space=pltpu.SMEM)]
        + [pl.BlockSpec(memory_space=pltpu.VMEM)] * 2
        + [pl.BlockSpec(memory_space=pl.ANY)],
        out_specs=pl.BlockSpec(memory_space=pltpu.VMEM),
        out_shape=shaped(left.shape, left.dtype),
        cost_estimate=pl.CostEstimate(flops=1, bytes_accessed=1, transcendentals=0),
    )(jnp.reshape(flag.astype(jnp.int32), (1,)), left, right, token)


def unpacked(terms, quarter):
    rows = terms[0].shape[0]

    def kernel(*refs):
        qkv_ref, out_ref = refs[-2:]
        total = refs[0][...].astype(F32)
        for ref in refs[1:-2]:
            total = total + ref[...].astype(F32)
        for part in range(3):
            qkv_ref[part] = total[:, part * quarter : (part + 1) * quarter]
        out_ref[...] = total[:, 3 * quarter :]

    return pl.pallas_call(
        kernel,
        out_shape=[shaped((3, rows, quarter), F32), shaped((rows, quarter), F32)],
        compiler_params=pltpu.CompilerParams(vmem_limit_bytes=VMEM_BYTES),
        cost_estimate=pl.CostEstimate(flops=1, bytes_accessed=1, transcendentals=0),
    )(*terms)


def packed(gate_up, down, token):
    rows, units = down.shape

    def kernel(gate_up_ref, down_ref, _, out_ref):
        out_ref[:, :units] = gate_up_ref[0]
        out_ref[:, units : 2 * units] = gate_up_ref[1]
        out_ref[:, 2 * units :] = down_ref[...]

    return pl.pallas_call(
        kernel,
        in_specs=[pl.BlockSpec(memory_space=pltpu.VMEM)] * 2 + [pl.BlockSpec(memory_space=pl.ANY)],
        out_specs=pl.BlockSpec(memory_space=pltpu.VMEM),
        out_shape=shaped((rows, 3 * units), down.dtype),
        cost_estimate=pl.CostEstimate(flops=1, bytes_accessed=1, transcendentals=0),
    )(gate_up, down, token)


def dp_cross(parts):
    if len(parts) == 1:
        return [lax.psum_scatter(parts[0], "dp", scatter_dimension=0, tiled=True)]
    return [None] + [swap(parts[k + 1], "dp", 1) for k in range(2, len(parts), 2)]


def dp_pair_sums(parts, cross, *tokens):
    return [add_blocks(parts[2 * k], cross[k], *tokens) for k in range(1, len(cross))]


def dp_lines(halves):
    return [swap(half, "dp", 2 * k + 2) for k, half in enumerate(halves)]


def add_blocks(left, right, *tokens):
    def kernel(*refs):
        refs[-1][...] = (refs[0][...].astype(F32) + refs[1][...].astype(F32)).astype(BF16)

    return pl.pallas_call(
        kernel,
        in_specs=[pl.BlockSpec(memory_space=pltpu.VMEM)] * 2
        + [pl.BlockSpec(memory_space=pl.ANY)] * len(tokens),
        out_specs=pl.BlockSpec(memory_space=pltpu.VMEM),
        out_shape=shaped(left.shape, BF16),
        compiler_params=pltpu.CompilerParams(vmem_limit_bytes=VMEM_BYTES),
        cost_estimate=pl.CostEstimate(flops=1, bytes_accessed=1, transcendentals=0),
    )(left, right, *tokens)


def after(value, *others):
    if not others:
        return value

    def kernel(*refs):
        refs[-1][...] = refs[0][...]

    return pl.pallas_call(
        kernel,
        in_specs=[pl.BlockSpec(memory_space=pltpu.VMEM)]
        + [pl.BlockSpec(memory_space=pl.ANY)] * len(others),
        out_specs=pl.BlockSpec(memory_space=pltpu.VMEM),
        out_shape=shaped(value.shape, value.dtype),
        cost_estimate=pl.CostEstimate(flops=1, bytes_accessed=1, transcendentals=0),
    )(value, *others)


def copy_blocks(place, first, blocks, whole_ref):
    for k, ref in enumerate(blocks):
        if len(blocks) == 1:
            whole_ref[...] = ref[...]
        else:
            whole_ref[rows_at(place[first + k], ref.shape[0]), :] = ref[...]


def split_blocks(place, first, sum_ref, outs):
    for k, ref in enumerate(outs):
        if len(outs) == 1:
            ref[...] = sum_ref[...].astype(BF16)
        else:
            ref[...] = sum_ref[rows_at(place[first + k], ref.shape[0]), :].astype(BF16)


def rotary_tables(patches, head_size):
    pairs = head_size // 4
    freqs = 10000.0 ** (-np.arange(pairs, dtype=np.float64) / pairs)
    spots = np.arange(patches)
    row = (spots // GRID)[None, :] * freqs[:, None]
    col = (spots % GRID)[None, :] * freqs[:, None]
    angles = np.concatenate([row, row, col, col], axis=0)
    cosine, sine = np.cos(angles), np.sin(angles)
    first = (np.arange(head_size) // pairs % 2 == 0)[:, None]
    up = np.where(first, -sine, 0.0)
    down = np.where(first, 0.0, sine)
    return np.stack([cosine, up, down]).astype(np.float32)


def turned(value, up, down):
    height = value.shape[0]
    pairs = height // 4
    return pltpu.roll(value, height - pairs, 0) * up + pltpu.roll(value, pairs, 0) * down


def normed(value):
    centred = value - jnp.mean(value, axis=0, keepdims=True)
    scale = lax.rsqrt(jnp.mean(centred * centred, axis=0, keepdims=True) + EPS)
    return centred * scale, scale


def norm_back(grad, unit, scale):
    return scale * (
        grad
        - jnp.mean(grad, axis=0, keepdims=True)
        - unit * jnp.mean(grad * unit, axis=0, keepdims=True)
    )


def row_sums(value):
    ones = jnp.ones((8, value.shape[1]), F32)
    return lax.dot_general(
        ones, value, NT, precision=lax.Precision.HIGHEST, preferred_element_type=F32
    )[0:1]


def rows_at(index, size):
    return pl.ds(pl.multiple_of(index * size, 16), size)


def heads_of(raw, gains, tables, head):
    size = gains.shape[0]
    width = raw.shape[0] // 3
    cosine, up, down = tables[0], tables[1], tables[2]
    found = []
    for part in range(2):
        rows = raw[part * width + head * size : part * width + (head + 1) * size]
        scale = lax.rsqrt(jnp.mean(rows * rows, axis=0, keepdims=True) + EPS)
        hat = rows * scale
        gained = hat * gains[:, part : part + 1]
        rotated = gained * cosine + turned(gained, up, down)
        found.append((hat, scale, rotated.astype(BF16)))
    value = raw[2 * width + head * size : 2 * width + (head + 1) * size].astype(BF16)
    return found[0], found[1], value


def attention_forward(
    heads, place, lat_refs, mods_ref, weight_ref, gains_ref, tables_ref, outs, scratch
):
    lat_ref, h_ref, raw_ref, lse_ref, ob_ref, mine_ref, theirs_ref = outs
    (x_ref,) = scratch
    quarter = lat_refs[0].shape[1]
    width = quarter
    size = gains_ref.shape[0]
    inverse = 1.0 / math.sqrt(size)

    for k, ref in enumerate(lat_refs):
        piece = ref[0]
        lat_ref[0, rows_at(place[k], quarter), :] = piece
        x_ref[rows_at(place[k], quarter), :] = piece.astype(F32)
    mods = mods_ref[0].T
    unit, _ = normed(x_ref[...])
    h = (unit * (1.0 + mods[:, 1:2]) + mods[:, 0:1]).astype(BF16)
    h_ref[0] = h
    span = round_up(3 * width, LANES)
    raw = dot(weight_ref[:, :span], h, TN)[: 3 * width]
    raw_ref[0] = raw
    gains, tables = gains_ref[...], tables_ref[...]
    pad = 4 * width - (3 * width) // LANES * LANES - width
    parts, tops = [], []
    for head in range(heads):
        (_, _, query), (_, _, key), value = heads_of(raw, gains, tables, head)
        scores = dot(key, query, TN) * inverse
        top = jnp.max(scores, axis=0, keepdims=True)
        expo = jnp.exp(scores - top)
        total = jnp.sum(expo, axis=0, keepdims=True)
        probs = (expo / total).astype(BF16)
        parts.append(dot(value, probs, NN))
        tops.append(top + jnp.log(total))
    lse_ref[0] = jnp.concatenate(tops, axis=0)
    patches = raw.shape[1]
    ob = jnp.concatenate([jnp.zeros((pad, patches), F32)] + parts, axis=0).astype(BF16)
    ob_ref[0] = ob
    x_ref[...] = dot(weight_ref[:, 4 * width - width - pad :], ob, NN)
    put_halves(place, x_ref, mine_ref, theirs_ref)


def feed_forward(
    place, image_weight, lat_ref, sums, mods_ref, cot_refs, weight_ref, outs, scratch
):
    mid_ref, attn_ref, h_ref, hidden_ref, dffn_ref, dgu_ref, cot_ref, mine_ref, theirs_ref = outs
    (x_ref,) = scratch
    quarter = cot_refs[0].shape[1]
    units = hidden_ref.shape[1]
    mods = mods_ref[0].T
    take_halves(place, x_ref, sums)
    attn_ref[0] = x_ref[rows_at(place[0], quarter), :]
    mid = lat_ref[0].astype(F32) + mods[:, 2:3] * x_ref[...]
    mid_ref[0] = mid
    unit, _ = normed(mid)
    h = (unit * (1.0 + mods[:, 4:5]) + mods[:, 3:4]).astype(BF16)
    h_ref[0] = h
    for k, ref in enumerate(cot_refs):
        piece = ref[0]
        cot_ref[0, rows_at(place[k], quarter), :] = piece
    weight = image_weight[pl.program_id(0)]
    dffn = (mods[:, 5:6] * (cot_ref[0].astype(F32) * weight)).astype(BF16)
    dffn_ref[0] = dffn
    gate = dot(weight_ref[:, :units], h, TN)
    up = dot(weight_ref[:, units : 2 * units], h, TN)
    sig = jax.nn.sigmoid(gate)
    swish = gate * sig
    hidden_ref[0] = (swish * up).astype(BF16)
    dhidden = dot(weight_ref[:, 2 * units :], dffn, TN)
    dgu_ref[0, :units] = (dhidden * up * sig * (1.0 + gate * (1.0 - sig))).astype(BF16)
    dgu_ref[0, units:] = (dhidden * swish).astype(BF16)
    x_ref[...] = dot(weight_ref[:, : 2 * units], dgu_ref[0], NN)
    put_halves(place, x_ref, mine_ref, theirs_ref)


def put_halves(place, x_ref, mine_ref, theirs_ref):
    core, half = place[4], mine_ref.shape[1]
    mine_ref[0] = x_ref[rows_at(core, half), :].astype(BF16)
    theirs_ref[0] = x_ref[rows_at(1 - core, half), :].astype(BF16)


def take_halves(place, x_ref, halves):
    core, half = place[4], halves[0].shape[1]
    x_ref[rows_at(core, half), :] = halves[0][0].astype(F32)
    x_ref[rows_at(1 - core, half), :] = halves[1][0].astype(F32)


def over_images(left_ref, right_ref, rows=slice(None)):
    total = None
    for n in range(left_ref.shape[0]):
        term = dot(left_ref[n], right_ref[n, rows], NT)
        total = term if total is None else total + term
    return total


def feed_forward_grads(h_ref, hidden_ref, dffn_ref, dgu_ref, outs):
    units = hidden_ref.shape[1]
    (grad_ref,) = outs
    grad_ref[:, :units] = over_images(h_ref, dgu_ref, slice(0, units)).astype(BF16)
    grad_ref[:, units : 2 * units] = over_images(h_ref, dgu_ref, slice(units, 2 * units)).astype(BF16)
    grad_ref[:, 2 * units :] = over_images(dffn_ref, hidden_ref).astype(BF16)


def feed_forward_end(place, hidden_ref, weight_ref, outs, scratch):
    mine_ref, theirs_ref = outs
    (x_ref,) = scratch
    core, quarter = place[4], mine_ref.shape[1] // 2
    for n in range(hidden_ref.shape[0]):
        x_ref[...] = dot(weight_ref[...], hidden_ref[n], NN)
        for side in range(2):
            rows = slice(side * quarter, (side + 1) * quarter)
            mine_ref[n, rows] = x_ref[rows_at(2 * side + core, quarter), :].astype(BF16)
            theirs_ref[n, rows] = x_ref[rows_at(2 * side + 1 - core, quarter), :].astype(BF16)


def attention_backward(
    heads,
    place,
    image_weight,
    sums,
    mid_ref,
    attn_ref,
    cot_ref,
    mods_ref,
    raw_ref,
    lse_ref,
    gains_ref,
    tables_ref,
    weight_ref,
    outs,
    scratch,
):
    dmid_ref, dattn_ref, draw_ref, mine_ref, theirs_ref, dmods_ref, qgain_ref, kgain_ref = outs
    x_ref, y_ref = scratch
    quarter = attn_ref.shape[1]
    width = quarter
    size = gains_ref.shape[0]
    inverse = 1.0 / math.sqrt(size)
    mods = mods_ref[0].T
    take_halves(place, x_ref, sums)
    unit, scale = normed(mid_ref[0])
    y_ref[...] = unit
    own = rows_at(place[0], quarter)
    dh_own = x_ref[own, :]
    dmods_ref[0] = jnp.zeros(dmods_ref.shape[1:], F32)
    dmods_ref[0, 3:4, :] = row_sums(dh_own)
    dmods_ref[0, 4:5, :] = row_sums(dh_own * y_ref[own, :])
    weight = image_weight[pl.program_id(0)]
    dy = cot_ref[0].astype(F32) * weight
    dmid = dy + norm_back(x_ref[...] * (1.0 + mods[:, 4:5]), unit, scale)
    dmid_ref[0] = dmid
    x_ref[...] = dmid
    dmods_ref[0, 2:3, :] = row_sums(x_ref[own, :] * attn_ref[0])
    dattn = (mods[:, 2:3] * dmid).astype(BF16)
    dattn_ref[0] = dattn
    start = (3 * width) // LANES * LANES
    pad = 3 * width - start
    dob = dot(weight_ref[:, start:], dattn, TN)
    raw = raw_ref[0]
    gains, tables = gains_ref[...], tables_ref[...]
    cosine, up, down = tables[0], tables[1], tables[2]
    parts = [[], [], []]
    sums_of = [None, None]
    for head in range(heads):
        query, key, value = heads_of(raw, gains, tables, head)
        grad = dob[pad + head * size : pad + (head + 1) * size].astype(BF16)
        scores = dot(key[2], query[2], TN) * inverse
        probs = jnp.exp(scores - lse_ref[0, head : head + 1, :])
        dprobs = dot(value, grad, TN)
        parts[2].append(dot(grad, probs.astype(BF16), NT))
        dscores = probs * (dprobs - jnp.sum(probs * dprobs, axis=0, keepdims=True))
        dscores = dscores.astype(BF16)
        turned_grads = (
            dot(key[2], dscores, NN) * inverse,
            dot(query[2], dscores, NT) * inverse,
        )
        for part, (rot, (hat, rms, _)) in enumerate(zip(turned_grads, (query, key))):
            back = rot * cosine - turned(rot, up, down)
            term = back * hat
            sums_of[part] = term if sums_of[part] is None else sums_of[part] + term
            g = back * gains[:, part : part + 1]
            parts[part].append(rms * (g - hat * jnp.mean(g * hat, axis=0, keepdims=True)))
    qgain_ref[0] = jnp.broadcast_to(row_sums(sums_of[0]), qgain_ref.shape[1:])
    kgain_ref[0] = jnp.broadcast_to(row_sums(sums_of[1]), kgain_ref.shape[1:])
    span = round_up(3 * width, LANES)
    patches = raw.shape[1]
    tail = [jnp.zeros((span - 3 * width, patches), F32)] if span > 3 * width else []
    draw = jnp.concatenate(parts[0] + parts[1] + parts[2] + tail, axis=0).astype(BF16)
    draw_ref[0] = draw
    x_ref[...] = dot(weight_ref[:, :span], draw, NN)
    put_halves(place, x_ref, mine_ref, theirs_ref)


def attention_grads(place, h_ref, draw_ref, dattn_ref, ob_ref, outs, scratch):
    span = draw_ref.shape[1]
    (sum_ref,) = scratch
    start = sum_ref.shape[1] - ob_ref.shape[1]
    total = over_images(h_ref, draw_ref)
    out = over_images(dattn_ref, ob_ref)
    sum_ref[:, :start] = total[:, :start]
    sum_ref[:, start:span] = total[:, start:] + out[:, : span - start]
    sum_ref[:, span:] = out[:, span - start :]
    split_blocks(place, 5, sum_ref, outs)


def last_steps(
    place, image_weight, keep, sums, lat_ref, dmid_ref, mid_ref, cot_ref, mods_ref, ffn_ref,
    dmods_ref, outs, scratch
):
    out_ref, dlat_ref, dm_ref = outs
    x_ref, y_ref = scratch
    quarter = ffn_ref.shape[1]
    own = rows_at(place[0], quarter)
    mods = mods_ref[0].T
    take_halves(place, x_ref, sums)
    unit, scale = normed(lat_ref[0].astype(F32))
    y_ref[...] = unit
    dh_own = x_ref[own, :]
    dm_ref[0] = dmods_ref[0]
    dm_ref[0, 0:1, :] = row_sums(dh_own)
    dm_ref[0, 1:2, :] = row_sums(dh_own * y_ref[own, :])
    back = norm_back(x_ref[...] * (1.0 + mods[:, 1:2]), unit, scale)
    x_ref[...] = back
    dlat_ref[0] = (dmid_ref[0, own, :] + x_ref[own, :]).astype(BF16)
    n = pl.program_id(0)
    ffn = ffn_ref[0]
    dy = cot_ref[0, own, :].astype(F32) * image_weight[n]
    dm_ref[0, 5:6, :] = row_sums(dy * ffn)
    y_ref[...] = jnp.broadcast_to(mods[:, 5:6], y_ref.shape)
    out_ref[0] = ((mid_ref[0, own, :] + y_ref[own, :] * ffn) * keep[n]).astype(BF16)


def whole(array):
    return pl.BlockSpec(array.shape, lambda n: (0,) * array.ndim)


def last(array):
    width = array.shape[1] // 3
    return pl.BlockSpec((array.shape[0], width), lambda n: (0, 2))


def each(array):
    return pl.BlockSpec((1,) + array.shape[1:], lambda n: (n,) + (0,) * (array.ndim - 1))


def token(_):
    return pl.BlockSpec(memory_space=pl.ANY)


def scalars(_):
    return pl.BlockSpec(memory_space=pltpu.SMEM)


def call(body, groups, outs, scratch, images, flops=1):
    flat, specs, counts = [], [], []
    for group in groups:
        counts.append(len(group))
        for array, kind in group:
            flat.append(array)
            specs.append(kind(array))

    def kernel(*refs):
        at, lists = 0, []
        for count in counts:
            lists.append(list(refs[at : at + count]))
            at += count
        body(*lists, list(refs[at : at + len(outs)]), list(refs[at + len(outs) :]))

    moved = sum(a.size * a.dtype.itemsize for a in flat) if flops > 1 else 1
    return pl.pallas_call(
        kernel,
        grid=(images,),
        in_specs=specs,
        out_specs=[kind(o) for o, kind in outs],
        out_shape=[o for o, _ in outs],
        scratch_shapes=scratch,
        compiler_params=pltpu.CompilerParams(
            dimension_semantics=("arbitrary",), vmem_limit_bytes=VMEM_BYTES
        ),
        cost_estimate=pl.CostEstimate(flops=flops, bytes_accessed=moved, transcendentals=0),
    )(*flat)


def shaped(shape, dtype):
    return jax.ShapeDtypeStruct(shape, dtype)


def body(
    latents,
    condition,
    noise_bins,
    slot_valid,
    ada_weight,
    ada_bias,
    qkv_weight,
    query_gain,
    key_gain,
    out_weight,
    gate_up,
    down_weight,
    cotangent,
):
    images, patches, quarter = latents.shape
    width = condition.shape[1]
    rows = qkv_weight.shape[0]
    units = gate_up.shape[2]
    head_size = query_gain.shape[0]
    heads = quarter // head_size
    dp, mp = lax.axis_index("dp"), lax.axis_index("mp")
    core = mp % 2
    dp_size = lax.axis_size("dp")
    all_images = dp_size * images
    tokens = images * patches

    by_part = jnp.transpose(qkv_weight, (1, 0, 2))
    first_pack = jnp.concatenate([by_part[0], by_part[1], by_part[2], out_weight.T], axis=1)
    first = lax.all_gather(first_pack, "dp", axis=0, tiled=True)
    lat_pieces = mp_pieces(jnp.transpose(latents, (0, 2, 1)))
    cot_pieces = mp_pieces(jnp.transpose(cotangent, (0, 2, 1)))
    ada = jnp.transpose(ada_weight, (1, 0, 2))
    keep = slot_valid.astype(F32)
    given = noise_bins[0] >= 0
    on_line = dp_size == 8

    def over_dp():
        extra = jnp.stack([noise_bins, slot_valid], axis=1).astype(BF16)
        told = jnp.concatenate([condition, extra, jnp.zeros((images, LANES - 2), BF16)], axis=1)
        told = gather_rows(told, "dp")
        all_bins, all_valid = told[:, width].astype(F32), told[:, width + 1].astype(F32)
        cond_rows = lax.dynamic_slice_in_dim(told[:, :width], dp * rows, rows, 1).astype(F32)

        bin_ids = jnp.arange(BINS, dtype=F32)
        member = (all_bins[:, None] == bin_ids[None, :]).astype(F32) * all_valid[:, None]
        per_bin = jnp.sum(member, axis=0)
        own_bins = noise_bins.astype(F32)
        own_count = jnp.sum((own_bins[:, None] == bin_ids[None, :]) * per_bin[None, :], axis=1)
        image_weight = keep * jnp.sum(all_valid) / (BINS * jnp.maximum(own_count, 1.0))

        cond_act = jax.nn.silu(cond_rows).astype(BF16)
        pack = packed(jnp.transpose(gate_up, (1, 0, 2)), down_weight.T, cond_act)
        return cond_act, image_weight, pack

    cond_act, image_weight, second_pack = region(given, over_dp)
    mods_terms = jnp.einsum("nd,cde->nce", cond_act, ada, preferred_element_type=F32)
    mods_own = scatter_rows(mods_terms.reshape(all_images, -1), "dp")
    hop_one = line_first(second_pack) if on_line else ()
    beside = [swap(second_pack, "dp", 1)] if on_line else []
    near = line_near(hop_one, hop_one[0]) if on_line else None
    mods_own = after(mods_own, *beside)
    mods_own = mods_own.reshape(images, 6, quarter) + ada_bias[None]
    mods_own = jnp.pad(mods_own, ((0, 0), (0, 2), (0, 0)))
    beside += [swap(near, "dp", 1)] if on_line else []
    two = line_two(hop_one, beside[1]) if on_line else None
    held = [*beside, two] if on_line else []
    side = mp // 2
    far = swap(mods_own, "mp", 2)
    pair = jnp.stack([jnp.where(side == 0, mods_own, far), jnp.where(side == 0, far, mods_own)])
    other = swap(pair, "mp", 1)
    quad = jnp.stack([jnp.where(core == 0, pair, other), jnp.where(core == 0, other, pair)], axis=1)
    mods = jnp.transpose(quad, (2, 3, 0, 1, 4)).reshape(images, 8, width)

    count = dp_size if on_line else 1
    place = jnp.stack([mp, mp ^ 2, mp ^ 1, mp ^ 3, core] + [dp ^ k for k in range(count)])
    place = place.astype(jnp.int32)
    block_shape = (width // count,)
    gains = jnp.stack([query_gain, key_gain], axis=1)
    tables = jnp.asarray(rotary_tables(patches, head_size))
    full = 4 * quarter
    span = round_up(3 * quarter, LANES)
    start = 3 * quarter // LANES * LANES
    wide = lambda dtype: shaped((images, width, patches), dtype)
    half = shaped((images, width // 2, patches), BF16)
    tall = pltpu.VMEM((width, patches), F32)

    lat, h_one, raw, lse, ob, *attn_terms = call(
        lambda p, l, m, w, g, t, _, outs, s: attention_forward(
            heads, p[0], l, m[0], w[0], g[0], t[0], outs, s
        ),
        [
            [(place, scalars)],
            [(a, each) for a in lat_pieces],
            [(mods, each)],
            [(first, whole)],
            [(gains, whole)],
            [(tables, whole)],
            [(a, token) for a in held],
        ],
        [
            (wide(BF16), each),
            (wide(BF16), each),
            (shaped((images, 3 * quarter, patches), F32), each),
            (shaped((images, heads, patches), F32), each),
            (shaped((images, full - start, patches), BF16), each),
            (half, each),
            (half, each),
        ],
        [tall],
        images,
    )
    if on_line:
        blocks, block_owners = line_rest(second_pack, beside, hop_one, near, two)
        attn_chip = mp_chip(*attn_terms, blocks[6])

        def assemble(p, blocks, outs, _):
            copy_blocks(p[0], 0, blocks, outs[0])

        (second,) = call(
            assemble,
            [
                [(jnp.stack(block_owners).astype(jnp.int32), scalars)],
                [(a, whole) for a in blocks],
            ],
            [(shaped((width, 3 * units), BF16), whole)],
            [],
            1,
        )
        attn_sums = mp_join(attn_chip, swap(attn_chip, "mp", 2), second)
    else:
        second = lax.all_gather(second_pack, "dp", axis=0, tiled=True)
        attn_sums = mp_total(*attn_terms)

    def middle():
        mid, attn_own, h_two, hidden, dffn, dgu, cot, mine, theirs = call(
            lambda p, w, l, s, m, c, k, outs, x: feed_forward(
                p[0], w[0], l[0], s, m[0], c, k[0], outs, x
            ),
            [
                [(place, scalars)],
                [(image_weight, scalars)],
                [(lat, each)],
                [(a, each) for a in attn_sums],
                [(mods, each)],
                [(a, each) for a in cot_pieces],
                [(second, whole)],
            ],
            [
                (wide(F32), each),
                (shaped((images, quarter, patches), F32), each),
                (wide(BF16), each),
                (shaped((images, units, patches), BF16), each),
                (wide(BF16), each),
                (shaped((images, 2 * units, patches), BF16), each),
                (wide(BF16), each),
                (half, each),
                (half, each),
            ],
            [tall],
            images,
        )
        (second_terms,) = call(
            lambda a, outs, x: feed_forward_grads(*a, outs),
            [[(h_two, whole), (hidden, whole), (dffn, whole), (dgu, whole)]],
            [(shaped((width, 3 * units), BF16), whole)],
            [],
            1,
        )
        return mid, attn_own, cot, hidden, mine, swap(theirs, "mp", 1), second_terms

    mid, attn_own, cot, hidden, dh_two_mine, dh_two_other, second_terms = region(given, middle)
    second_sum = lax.psum_scatter(second_terms, "dp", scatter_dimension=0, tiled=True)

    def backward():
        dh_two_chip = add_blocks(dh_two_mine, dh_two_other)
        ffn_terms = call(
            lambda p, a, outs, x: feed_forward_end(p[0], *a, outs, x),
            [[(place, scalars)], [(hidden, whole), (second, last)]],
            [(half, whole), (half, whole)],
            [tall],
            1,
        )
        dh_two_sums = mp_join(dh_two_chip, swap(dh_two_chip, "mp", 2), ffn_terms[0])
        dmid, dattn, draw, mine, theirs, dmods_part, qgain, kgain = call(
            lambda p, w, s, a, outs, x: attention_backward(heads, p[0], w[0], s, *a, outs, x),
            [
                [(place, scalars)],
                [(image_weight, scalars)],
                [(a, each) for a in dh_two_sums],
                [
                    (mid, each),
                    (attn_own, each),
                    (cot, each),
                    (mods, each),
                    (raw, each),
                    (lse, each),
                    (gains, whole),
                    (tables, whole),
                    (first, whole),
                ],
            ],
            [
                (wide(F32), each),
                (wide(BF16), each),
                (shaped((images, span, patches), BF16), each),
                (half, each),
                (half, each),
                (shaped((images, 8, quarter), F32), each),
                (shaped((images, 8, head_size), F32), each),
                (shaped((images, 8, head_size), F32), each),
            ],
            [tall, tall],
            images,
        )
        first_terms = call(
            lambda p, a, outs, x: attention_grads(p[0], *a, outs, x),
            [
                [(place, scalars)],
                [(h_one, whole), (draw, whole), (dattn, whole), (ob, whole)],
            ],
            [(shaped(block_shape + (full,), BF16), whole)] * count,
            [pltpu.VMEM((width, full), F32)],
            1,
        )
        ffn_own = mp_quarter(*ffn_terms)
        first_beside = dp_cross(first_terms)
        end_half = [add_blocks(first_terms[6], first_beside[3])] if on_line else []
        last_line = [swap(half_sum, "dp", 6) for half_sum in end_half]
        dh_one_chip = mp_chip(mine, theirs, *first_terms)
        dh_one_sums = mp_join(dh_one_chip, swap(dh_one_chip, "mp", 2), *first_beside[3:])
        block_out, latent_grad, dmods = call(
            lambda p, w, k, s, a, _, outs, x: last_steps(p[0], w[0], k[0], s, *a, outs, x),
            [
                [(place, scalars)],
                [(image_weight, scalars)],
                [(keep, scalars)],
                [(a, each) for a in dh_one_sums],
                [
                    (lat, each),
                    (dmid, each),
                    (mid, each),
                    (cot, each),
                    (mods, each),
                    (ffn_own, each),
                    (dmods_part, each),
                ],
                [(a, token) for a in end_half],
            ],
            [
                (shaped((images, quarter, patches), BF16), each),
                (shaped((images, quarter, patches), BF16), each),
                (shaped((images, 8, quarter), F32), each),
            ],
            [tall, tall],
            images,
        )

        halves = dp_pair_sums(first_terms, first_beside[:3], dmods) if on_line else []

        gain_terms = jnp.concatenate([jnp.sum(qgain[:, 0], axis=0), jnp.sum(kgain[:, 0], axis=0)])
        high = gain_terms.astype(BF16)
        low = (gain_terms - high.astype(F32)).astype(BF16)
        beside = jnp.concatenate([high, low])[None]
        beside = jnp.concatenate([beside, jnp.zeros((images - 1, beside.shape[1]), BF16)], axis=0)
        rounded = dmods[:, :6].astype(BF16).reshape(images, 6 * quarter)
        rounded = after(jnp.concatenate([rounded, beside], axis=1), *halves[1:], *last_line)
        told_back = gather_rows(rounded, "dp")
        own = first_terms[:2] if count > 1 else first_beside
        return block_out, latent_grad, told_back, own, halves, last_line

    block_out, latent_grad, told_back, own, halves, last_line = region(given, backward)
    first_far = dp_lines(halves) + last_line

    def modulation_grads():
        dmods_all = told_back[:, : 6 * quarter].reshape(all_images, 6, quarter)
        gain_sum = jnp.sum(told_back[:, 6 * quarter :].astype(F32), axis=0)
        gain_sum = gain_sum[: 2 * head_size] + gain_sum[2 * head_size :]
        ada_grad = jnp.einsum("nd,nce->cde", cond_act, dmods_all, preferred_element_type=F32)
        bias_grad = jnp.sum(dmods_all.astype(F32), axis=0)
        cond_terms = jnp.einsum("nce,cde->nd", dmods_all, ada, preferred_element_type=F32)
        both = mp_sum_small(jnp.concatenate([cond_terms.reshape(-1), gain_sum]))
        gain_sum = both[cond_terms.size :]
        cond_sum = rows_to_columns(both[: cond_terms.size].reshape(cond_terms.shape), "dp")
        return ada_grad, bias_grad, gain_sum, cond_sum

    ada_grad, bias_grad, gain_sum, cond_sum = region(given, modulation_grads)
    last_terms = [own[0], *first_far]
    if count > 1:
        last_terms.insert(1, swap(own[1], "dp", 1))
    qkv_grad, out_grad = unpacked(last_terms, quarter)
    second_sum = second_sum.astype(F32)
    gateup_grad = jnp.stack([second_sum[:, :units], second_sum[:, units : 2 * units]], axis=1)
    down_grad = second_sum[:, 2 * units :].T
    cond_own = condition.astype(F32)
    sig = jax.nn.sigmoid(cond_own)
    condition_grad = (cond_sum * sig * (1.0 + cond_own * (1.0 - sig))).astype(BF16)
    return (
        jnp.transpose(block_out, (0, 2, 1)),
        jnp.transpose(latent_grad, (0, 2, 1)),
        condition_grad,
        jnp.transpose(ada_grad, (1, 0, 2)),
        bias_grad,
        jnp.transpose(qkv_grad, (1, 0, 2)),
        gain_sum[:head_size],
        gain_sum[head_size:],
        out_grad.T,
        gateup_grad,
        down_grad,
    )


def solution(mesh):
    placed = (
        P("dp", None, "mp"),
        P("dp", None),
        P("dp"),
        P("dp"),
        P("dp", None, "mp"),
        P(None, "mp"),
        P("dp", None, "mp"),
        P(),
        P(),
        P("mp", "dp"),
        P("dp", None, "mp"),
        P("mp", "dp"),
        P("dp", None, "mp"),
    )
    return jax.shard_map(
        body,
        mesh=mesh,
        in_specs=placed,
        out_specs=(
            P("dp", None, "mp"),
            P("dp", None, "mp"),
            P("dp", None),
            P("dp", None, "mp"),
            P(None, "mp"),
            P("dp", None, "mp"),
            P(),
            P(),
            P("mp", "dp"),
            P("dp", None, "mp"),
            P("mp", "dp"),
        ),
        check_vma=False,
    )
```
